32 devices in a mesh: grp: 2 (over core), seq: 4 (over z), head: 4 (over y, x).
Axes of the slice: x: 2, y: 2, z: 4, core: 2. Of those that a mesh axis runs over, the one named last changes fastest.
Arguments:
- queries: bfloat16 [2048, 8192], P('seq', ('grp', 'head')), may hold values from -140 to 140
- key_rows: bfloat16 [2048, 1024], P('seq', ('grp', 'head')), may hold values from -6 to 6
- values: bfloat16 [2048, 1024], P('seq', ('grp', 'head')), may hold values from -6 to 6
- out_grad: bfloat16 [2048, 8192], P('seq', ('grp', 'head')), may hold values from -6 to 6
- teacher_window: bfloat16 [16, 3, 64, 128, 128], P('seq', None, ('grp', 'head')), may hold values from -16 to 250
- teacher_global: bfloat16 [16, 2, 64, 128, 128], P('seq', None, ('grp', 'head')), may hold values from -16 to 250
- global_picks: int32 [16, 2], P('seq'), may hold values from -1 to 3, as said below
- mix_weight: float32 [2048], P('seq'), may hold values from 0.05 to 0.95
Outputs:
- query_grad: bfloat16 [2048, 8192], P('seq', ('grp', 'head'))
- key_grad: bfloat16 [2048, 1024], P('seq', ('grp', 'head'))
- value_grad: bfloat16 [2048, 1024], P('seq', ('grp', 'head'))
- row_loss: float32 [2048], P('seq')
The draws below stay inside these ranges and needn't reach their ends.
Inputs may be any that keep to these rules, and one draw needn't show every extreme that they name: `global_picks`: in each row the non-negative entries are distinct, and an entry of query block b is below b - 2.
All inputs are finite; a program needn't handle non-finite values.
Results may differ from the reference program's by a relative error of at most 0.005.
Values may be sent and summed in bfloat16 or wider, within the bound.
No kernel may reach another device: no remote copies, remote signals or barrier semaphores. Data moves between devices by JAX's collectives and lax.ppermute only.
A program may use at most 128 MiB of HBM per device.

```python
import math
import jax
import jax.numpy as jnp
from jax import lax

H = 64
KVH = 8
E = 128
BLK = 128
WIN = 3
NGLOB = 4
GSEL = 2
NQB = 16
TOKENS = 2048


def shared_keys(key):
    base = jax.random.normal(jax.random.fold_in(key, 101), (TOKENS, KVH * E), jnp.float32)
    return jnp.clip(base, -6.0, 6.0)


def draw_key_rows(key, part):
    return shared_keys(key).astype(jnp.bfloat16)


def draw_queries(key, part):
    base = jnp.clip(jax.random.normal(jax.random.fold_in(key, 102), (TOKENS, H * E), jnp.float32), -6.0, 6.0)
    return base.astype(jnp.bfloat16)


def draw_teacher_window(key, part):
    shape = (NQB, WIN, H, BLK, BLK)
    base = jnp.clip(2.0 * jax.random.normal(jax.random.fold_in(key, 111), shape, jnp.float32), -16.0, 16.0)
    return base.astype(jnp.bfloat16)


def draw_teacher_global(key, part):
    shape = (NQB, GSEL, H, BLK, BLK)
    base = jnp.clip(2.0 * jax.random.normal(jax.random.fold_in(key, 121), shape, jnp.float32), -16.0, 16.0)
    return base.astype(jnp.bfloat16)


def draw_global_picks(key, part):
    row_keys = jax.random.split(jax.random.fold_in(key, 201), NQB)
    orders = jax.vmap(lambda row_key: jax.random.permutation(row_key, NGLOB))(row_keys).astype(jnp.int32)[:, :GSEL]
    keeping = jax.random.randint(jax.random.fold_in(key, 202), (NQB, GSEL), 0, 4) > 0
    limits = jnp.arange(NQB, dtype=jnp.int32)[:, None] - (WIN - 1)
    return jnp.where(keeping & (orders < limits), orders, -1).astype(jnp.int32)


def block_scale(own_key, dims, shards, smallest, top_value):
    gain = 1.0
    for dim, shards_of in shards:
        steps = jax.random.uniform(jax.random.fold_in(jax.random.fold_in(own_key, 6), dim), (shards_of,), jnp.float32, smallest / len(shards), top_value / len(shards))
        gain = gain * jnp.repeat(jnp.exp(steps), dims[dim] // shards_of).reshape((-1,) + (1,) * (len(dims) - 1 - dim))
    return gain


def noise(stream_key, extent, spread, limit, cuts=(), kind=jnp.bfloat16):
    values = spread * jax.random.normal(stream_key, extent, jnp.float32)
    if cuts:
        values = values * block_scale(stream_key, extent, cuts, -0.22, 0.18)
    return jnp.clip(values, -limit, limit).astype(kind)


def setup_inputs(seed: int = 0) -> dict:
    key_list = jax.random.split(jax.random.key(seed), 9)
    queries = draw_queries(jax.random.fold_in(key_list[8], 71), 0)
    key_rows = draw_key_rows(jax.random.fold_in(key_list[8], 71), 0)
    values = noise(key_list[2], (TOKENS, KVH * E), 1.0, 6.0, ((0, 4), (1, 8)))
    out_grad = noise(key_list[3], (TOKENS, H * E), 1.0, 6.0, ((0, 4), (1, 8)))
    teacher_window = draw_teacher_window(jax.random.fold_in(key_list[8], 71), 0)
    teacher_global = draw_teacher_global(jax.random.fold_in(key_list[8], 71), 0)
    global_picks = draw_global_picks(jax.random.fold_in(key_list[8], 71), 0)
    mix_weight = jnp.clip(0.05 + 0.9 * jax.random.uniform(key_list[7], (TOKENS,), jnp.float32) ** block_scale(key_list[7], (TOKENS,), ((0, 4),), -0.2, 0.2), 0.05, 0.95)
    return dict(queries=queries, key_rows=key_rows, values=values, out_grad=out_grad, teacher_window=teacher_window, teacher_global=teacher_global, global_picks=global_picks, mix_weight=mix_weight)


def block_terms(query_tiles, key_cat, value_cat, teacher_cat, live_slots, grad_tiles, weights, scale):
    hiprec = lax.Precision.HIGHEST
    nblk, rows, kv_heads, group, width = query_tiles.shape
    slots = key_cat.shape[1]
    query_f = query_tiles.astype(jnp.float32)
    key_f = key_cat.astype(jnp.float32)
    value_f = value_cat.astype(jnp.float32)
    grad_f = grad_tiles.astype(jnp.float32)
    scores = jnp.einsum('bqnge,bsjne->bsngqj', query_f, key_f, precision=hiprec) * scale
    causal = lax.broadcasted_iota(jnp.int32, (rows, rows), 1) <= lax.broadcasted_iota(jnp.int32, (rows, rows), 0)
    later_slot = jnp.arange(slots) > 0
    live = live_slots[:, :, None, None, None, None] & (causal[None, None, None, None] | later_slot[None, :, None, None, None, None])
    masked = jnp.where(live, scores, -1000000000.0)
    shifted = masked - lax.optimization_barrier(jnp.max(masked, axis=(1, 5), keepdims=True))
    expo = jnp.where(live, jnp.exp(shifted), 0.0)
    total = lax.optimization_barrier(jnp.sum(expo, axis=(1, 5), keepdims=True))
    student_p = expo / total
    student_logp = shifted - jnp.log(total)
    teacher_grouped = teacher_cat.reshape(nblk, slots, kv_heads, group, rows, rows)
    teacher = jnp.where(live, teacher_grouped.astype(jnp.float32), -1000000000.0)
    teacher_shift = teacher - lax.optimization_barrier(jnp.max(teacher, axis=(1, 5), keepdims=True))
    teacher_exp = jnp.where(live, jnp.exp(teacher_shift), 0.0)
    teacher_total = lax.optimization_barrier(jnp.sum(teacher_exp, axis=(1, 5), keepdims=True))
    teacher_p = teacher_exp / teacher_total
    teacher_logp = teacher_shift - jnp.log(teacher_total)
    forward_kl = lax.optimization_barrier(jnp.sum(jnp.where(live, teacher_p * (teacher_logp - student_logp), 0.0), axis=(1, 5), keepdims=True))
    reverse_kl = lax.optimization_barrier(jnp.sum(jnp.where(live, student_p * (student_logp - teacher_logp), 0.0), axis=(1, 5), keepdims=True))
    mixing = weights[:, None, None, None, :, None]
    row_terms = lax.optimization_barrier(jnp.sum(mixing * forward_kl + (1.0 - mixing) * reverse_kl, axis=(1, 2, 3, 5)))
    probs_low = student_p.astype(jnp.bfloat16)
    prob_grad = jnp.einsum('bqnge,bsjne->bsngqj', grad_f, value_f, precision=hiprec)
    delta = lax.optimization_barrier(jnp.sum(student_p * prob_grad, axis=(1, 5), keepdims=True))
    score_grad = jnp.where(live, mixing * (student_p - teacher_p) + (1.0 - mixing) * student_p * (student_logp - teacher_logp - reverse_kl) + student_p * (prob_grad - delta), 0.0) * scale
    score_low = score_grad.astype(jnp.bfloat16).astype(jnp.float32)
    query_part = jnp.einsum('bsngqj,bsjne->bqnge', score_low, key_f, precision=hiprec)
    key_part = jnp.einsum('bsngqj,bqnge->bsjne', score_low, query_f, precision=hiprec)
    value_part = jnp.einsum('bsngqj,bqnge->bsjne', probs_low.astype(jnp.float32), grad_f, precision=hiprec)
    return (query_part, key_part, value_part, row_terms)

def reference(queries, key_rows, values, out_grad, teacher_window, teacher_global, global_picks, mix_weight):
    scale = 1.0 / math.sqrt(E)
    group = H // KVH
    lead_rows = (WIN - 1) * BLK
    query_tiles = queries.reshape(NQB, BLK, KVH, group, E)
    grad_tiles = out_grad.reshape(NQB, BLK, KVH, group, E)
    weight_rows = mix_weight.reshape(NQB, BLK)
    pad_block = jnp.zeros((lead_rows, KVH * E), jnp.bfloat16)
    key_padded = jnp.concatenate([pad_block, key_rows], axis=0).reshape(-1, KVH, E)
    value_padded = jnp.concatenate([pad_block, values], axis=0).reshape(-1, KVH, E)
    key_global = key_rows[:NGLOB * BLK].reshape(NGLOB, BLK, KVH, E)
    value_global = values[:NGLOB * BLK].reshape(NGLOB, BLK, KVH, E)

    def one_block(carry, block_id):
        key_acc, value_acc, key_sink, value_sink = carry
        start = (block_id * BLK).astype(jnp.int32)
        key_window = lax.dynamic_slice_in_dim(key_padded, start, WIN * BLK, 0).reshape(WIN, BLK, KVH, E)[::-1]
        value_window = lax.dynamic_slice_in_dim(value_padded, start, WIN * BLK, 0).reshape(WIN, BLK, KVH, E)[::-1]
        picks_row = global_picks[block_id]
        safe_picks = jnp.maximum(picks_row, 0).astype(jnp.int32)
        key_cat = jnp.concatenate([key_window, jnp.take(key_global, safe_picks, axis=0)], axis=0)[None]
        value_cat = jnp.concatenate([value_window, jnp.take(value_global, safe_picks, axis=0)], axis=0)[None]
        window_tiles = jnp.stack([teacher_window[jnp.maximum(block_id - offset, 0).astype(jnp.int32), offset] for offset in range(WIN)])
        teacher_cat = jnp.concatenate([window_tiles, teacher_global[block_id]], axis=0)[None]
        live_window = block_id - jnp.arange(WIN, dtype=jnp.int32) >= 0
        live_slots = jnp.concatenate([live_window, picks_row >= 0])[None]
        query_part, key_part, value_part, row_terms = block_terms(query_tiles[block_id][None], key_cat, value_cat, teacher_cat, live_slots, grad_tiles[block_id][None], weight_rows[block_id][None], scale)
        key_win = key_part[0, :WIN][::-1].reshape(WIN * BLK, KVH, E)
        value_win = value_part[0, :WIN][::-1].reshape(WIN * BLK, KVH, E)
        key_acc = lax.dynamic_update_slice_in_dim(key_acc, lax.dynamic_slice_in_dim(key_acc, start, WIN * BLK, 0) + key_win, start, 0)
        value_acc = lax.dynamic_update_slice_in_dim(value_acc, lax.dynamic_slice_in_dim(value_acc, start, WIN * BLK, 0) + value_win, start, 0)
        onehot = (picks_row[:, None] == jnp.arange(NGLOB, dtype=jnp.int32)[None, :]).astype(jnp.float32)
        key_sink = key_sink + jnp.einsum('gn,gkhe->nkhe', onehot, key_part[0, WIN:], precision=lax.Precision.HIGHEST)
        value_sink = value_sink + jnp.einsum('gn,gkhe->nkhe', onehot, value_part[0, WIN:], precision=lax.Precision.HIGHEST)
        return ((key_acc, value_acc, key_sink, value_sink), (query_part[0], row_terms[0]))
    acc_zero = jnp.zeros((lead_rows + TOKENS, KVH, E), jnp.float32)
    sink_zero = jnp.zeros((NGLOB, BLK, KVH, E), jnp.float32)
    carry, outputs = lax.scan(one_block, (acc_zero, acc_zero, sink_zero, sink_zero), jnp.arange(NQB, dtype=jnp.int32))
    key_acc, value_acc, key_sink, value_sink = carry
    query_parts, loss_rows = outputs
    key_full = key_acc[lead_rows:].at[:NGLOB * BLK].add(key_sink.reshape(NGLOB * BLK, KVH, E))
    value_full = value_acc[lead_rows:].at[:NGLOB * BLK].add(value_sink.reshape(NGLOB * BLK, KVH, E))
    query_grad = query_parts.reshape(TOKENS, H * E).astype(jnp.bfloat16)
    key_grad = key_full.reshape(TOKENS, KVH * E).astype(jnp.bfloat16)
    value_grad = value_full.reshape(TOKENS, KVH * E).astype(jnp.bfloat16)
    return (query_grad, key_grad, value_grad, loss_rows.reshape(TOKENS))
```

```python
import functools
import math

import jax
import jax.numpy as jnp
from jax import lax
from jax.experimental import pallas as pl
from jax.experimental.pallas import tpu as pltpu
from jax.sharding import PartitionSpec as P

E = 128
BLK = 128
WIN = 3
NGLOB = 4
LEAD = WIN - 1
LOG2E = math.log2(math.e)
LN2 = math.log(2.0)
NT = (((1,), (1,)), ((), ()))
BF = jnp.bfloat16
F32 = jnp.float32


def shift(block, axis, distance):
    count = lax.axis_size(axis)
    route = [(i, i + distance) for i in range(count) if 0 <= i + distance < count]
    return lax.ppermute(block, axis, route)


def sum_over(block, axis):
    count = lax.axis_size(axis)
    if count & (count - 1):
        return lax.psum(block, axis)
    step = 1
    while step < count:
        block = block + lax.ppermute(block, axis, [(i, i ^ step) for i in range(count)])
        step *= 2
    return block


def block_kernel(
    first, crossing, slots, chained,
    base_ref, picks_ref, q_ref, g_ref, *rest,
):
    teacher_refs = rest[:slots]
    rest = rest[slots:]
    own_k, own_v, sink_k, sink_v, w_ref = rest[:5]
    rest = rest[5:]
    if crossing:
        before_ref, rest = rest[0], rest[1:]
    if chained:
        acc_in, rest = rest[:4], rest[4:]
    dq_ref, loss_ref, dk_ref, dv_ref, dsk_ref, dsv_ref = rest[:6]
    rest = rest[6:]
    if crossing:
        back_ref, rest = rest[0], rest[1:]
    ds_scr, pb_scr = rest
    step = pl.program_id(0)
    block = first + step
    heads = q_ref.shape[1] // E
    scale = 1.0 / math.sqrt(E)
    factor = scale * LOG2E

    @pl.when(step == 0)
    def _():
        if chained:
            for out, given in zip((dk_ref, dv_ref, dsk_ref, dsv_ref), acc_in):
                out[...] = given[...]
        else:
            for out in (dk_ref, dv_ref, dsk_ref, dsv_ref):
                out[...] = jnp.zeros_like(out)

    picks = [picks_ref[block, g] for g in range(slots - WIN)]
    live = [None] + [base_ref[0] + block - d >= 0 for d in range(1, WIN)] + [p >= 0 for p in picks]
    sink_at = [pl.multiple_of(jnp.maximum(p, 0) * BLK, BLK) for p in picks]

    def rows_of(d):
        return pl.ds(pl.multiple_of((block - d) * BLK, BLK), BLK)

    keys, vals = [], []
    for d in range(WIN):
        if d in crossing:
            at = first + LEAD - d
            keys.append(before_ref[0, at])
            vals.append(before_ref[1, at])
        else:
            keys.append(own_k[rows_of(d), :])
            vals.append(own_v[rows_of(d), :])
    for at in sink_at:
        keys.append(sink_k[pl.ds(at, BLK), :])
        vals.append(sink_v[pl.ds(at, BLK), :])
    kcat = jnp.concatenate(keys, axis=0)
    vcat = jnp.concatenate(vals, axis=0)
    kcat_t = kcat.T

    w1 = w_ref[0]
    w2 = jnp.concatenate([w1, w1], axis=1)
    slope = (w2 - 1.0) * LN2
    wide = 2 * BLK
    key_id = lax.broadcasted_iota(jnp.int32, (BLK, wide), 0)
    row_id = lax.broadcasted_iota(jnp.int32, (BLK, wide), 1) & (BLK - 1)
    causal = key_id <= row_id
    low = jnp.float32(-1e9)
    loss = jnp.zeros((1, wide), F32)

    def total(x):
        return jnp.sum(x, axis=0, keepdims=True)

    for pair in range(heads // 2):
        ha, hb = 2 * pair, 2 * pair + 1
        q2 = jnp.concatenate([q_ref[:, ha * E:(ha + 1) * E], q_ref[:, hb * E:(hb + 1) * E]], axis=0)
        g2 = jnp.concatenate([g_ref[:, ha * E:(ha + 1) * E], g_ref[:, hb * E:(hb + 1) * E]], axis=0)
        s_all = lax.dot_general(kcat, q2, NT, preferred_element_type=F32)
        pg_all = lax.dot_general(vcat, g2, NT, preferred_element_type=F32)
        held, stats = [], []
        for j in range(slots):
            s = s_all[j * BLK:(j + 1) * BLK]
            pg = pg_all[j * BLK:(j + 1) * BLK]
            t = jnp.concatenate([teacher_refs[j][0, 0, ha], teacher_refs[j][0, 0, hb]], axis=0)
            t = t.T.astype(F32)
            if j == 0:
                s = jnp.where(causal, s, low)
                t = jnp.where(causal, t, low)
            m = jnp.max(s, axis=0, keepdims=True)
            mt = jnp.max(t, axis=0, keepdims=True)
            x = (s - m) * factor
            y = (t - mt) * LOG2E
            es = jnp.exp2(x)
            et = jnp.exp2(y)
            gap = y - x
            u = pg + slope * gap
            stats.append((m, mt, total(es), total(et), total(et * gap), total(es * gap), total(es * u)))
            held.append((es, et, u))
        m = stats[0][0]
        mt = stats[0][1]
        for j in range(1, slots):
            m = jnp.maximum(m, jnp.where(live[j], stats[j][0], low))
            mt = jnp.maximum(mt, jnp.where(live[j], stats[j][1], low))
        a = [(st[0] - m) * factor for st in stats]
        b = [(st[1] - mt) * LOG2E for st in stats]
        fa = [jnp.exp2(v) for v in a]
        fb = [jnp.exp2(v) for v in b]
        for j in range(1, slots):
            fa[j] = jnp.where(live[j], fa[j], 0.0)
            fb[j] = jnp.where(live[j], fb[j], 0.0)
        z = functools.reduce(jnp.add, [f * st[2] for f, st in zip(fa, stats)])
        zt = functools.reduce(jnp.add, [f * st[3] for f, st in zip(fb, stats)])
        rz, rzt = 1.0 / z, 1.0 / zt
        both = jnp.log2(z) - jnp.log2(zt)
        off = [vb - va + both for va, vb in zip(a, b)]
        fwd = functools.reduce(jnp.add, [f * (st[4] + o * st[3]) for f, o, st in zip(fb, off, stats)])
        rev = functools.reduce(jnp.add, [f * (st[5] + o * st[2]) for f, o, st in zip(fa, off, stats)])
        mean_u = functools.reduce(
            jnp.add, [f * (st[6] + slope * o * st[2]) for f, o, st in zip(fa, off, stats)]
        )
        loss = loss + (w2 * LN2) * (rzt * fwd) + slope * (rz * rev)
        base = w2 - rz * mean_u
        cols = pl.ds(pair * wide, wide)
        for j in range(slots):
            es, et, u = held[j]
            p = es * (fa[j] * rz)
            ds = p * (u + (base + slope * off[j])) - et * (w2 * (fb[j] * rzt))
            ds_scr[j * BLK:(j + 1) * BLK, cols] = ds.astype(BF)
            pb_scr[j * BLK:(j + 1) * BLK, cols] = p.astype(BF)
        dq_t = jnp.dot(kcat_t, ds_scr[:, cols], preferred_element_type=F32) * scale
        dq2 = dq_t.T.astype(BF)
        dq_ref[:, ha * E:(ha + 1) * E] = dq2[:BLK]
        dq_ref[:, hb * E:(hb + 1) * E] = dq2[BLK:]
    loss_ref[0] = loss[:, :BLK] + loss[:, BLK:]

    q_all = jnp.concatenate([q_ref[:, h * E:(h + 1) * E] for h in range(heads)], axis=0)
    g_all = jnp.concatenate([g_ref[:, h * E:(h + 1) * E] for h in range(heads)], axis=0)
    dk = jnp.dot(ds_scr[...], q_all, preferred_element_type=F32) * scale
    dv = jnp.dot(pb_scr[...], g_all, preferred_element_type=F32)
    for d in range(WIN):
        part_k, part_v = dk[d * BLK:(d + 1) * BLK], dv[d * BLK:(d + 1) * BLK]
        if d in crossing:
            at = first + LEAD - d
            back_ref[0, at] = part_k
            back_ref[1, at] = part_v
        else:
            dk_ref[rows_of(d), :] += part_k
            dv_ref[rows_of(d), :] += part_v
    if crossing:
        untouched = [i for i in range(LEAD) if i not in [first + LEAD - d for d in crossing]]
        for i in untouched:
            back_ref[0, i] = jnp.zeros((BLK, E), F32)
            back_ref[1, i] = jnp.zeros((BLK, E), F32)
    for g, at in enumerate(sink_at):
        j = WIN + g
        dsk_ref[pl.ds(at, BLK), :] += dk[j * BLK:(j + 1) * BLK]
        dsv_ref[pl.ds(at, BLK), :] += dv[j * BLK:(j + 1) * BLK]


def run_blocks(first, count, base, picks, queries, out_grad, window, incoming, glob, own, sinks, weights,
               before, acc):
    crossing = [d for d in range(WIN) if d > first]
    assert not crossing or count == 1
    tokens, columns = queries.shape
    heads = window.shape[2]
    slots = WIN + picks.shape[1]
    tile = (1, 1, heads, BLK, BLK)
    whole = lambda i, *_: (0, 0)
    args = [queries, out_grad]
    specs = [pl.BlockSpec((BLK, columns), lambda i, *_: (first + i, 0))] * 2
    for d in range(WIN):
        if d in crossing:
            args.append(incoming[d])
            specs.append(pl.BlockSpec(tile, lambda i, *_: (0, 0, 0, 0, 0)))
        else:
            args.append(window)
            specs.append(pl.BlockSpec(tile, lambda i, *_, d=d: (first + i - d, d, 0, 0, 0)))
    for g in range(slots - WIN):
        args.append(glob)
        specs.append(pl.BlockSpec(tile, lambda i, *_, g=g: (first + i, g, 0, 0, 0)))
    for x in (*own, *sinks):
        args.append(x)
        specs.append(pl.BlockSpec(x.shape, whole))
    args.append(weights)
    specs.append(pl.BlockSpec((1, 1, BLK), lambda i, *_: (first + i, 0, 0)))
    if crossing:
        args.append(before)
        specs.append(pl.BlockSpec(before.shape, lambda i, *_: (0, 0, 0, 0)))
    chained = acc is not None
    acc_shapes = [(tokens, E)] * 2 + [(NGLOB * BLK, E)] * 2
    if chained:
        args.extend(acc)
        specs.extend(pl.BlockSpec(s, whole) for s in acc_shapes)
    outs = [
        jax.ShapeDtypeStruct((count * BLK, columns), BF),
        jax.ShapeDtypeStruct((count, 1, BLK), F32),
    ] + [jax.ShapeDtypeStruct(s, F32) for s in acc_shapes]
    out_specs = [
        pl.BlockSpec((BLK, columns), lambda i, *_: (i, 0)),
        pl.BlockSpec((1, 1, BLK), lambda i, *_: (i, 0, 0)),
    ] + [pl.BlockSpec(s, whole) for s in acc_shapes]
    if crossing:
        back = (2, LEAD, BLK, E)
        outs.append(jax.ShapeDtypeStruct(back, F32))
        out_specs.append(pl.BlockSpec(back, lambda i, *_: (0, 0, 0, 0)))
    elements = count * slots * heads * BLK * BLK
    return pl.pallas_call(
        functools.partial(block_kernel, first, crossing, slots, chained),
        out_shape=outs,
        grid_spec=pltpu.PrefetchScalarGridSpec(
            num_scalar_prefetch=2,
            grid=(count,),
            in_specs=specs,
            out_specs=out_specs,
            scratch_shapes=[pltpu.VMEM((slots * BLK, heads * BLK), BF)] * 2,
        ),
        compiler_params=pltpu.CompilerParams(vmem_limit_bytes=48 * 1024 * 1024),
        cost_estimate=pl.CostEstimate(
            flops=elements * E * 10, bytes_accessed=elements * 3, transcendentals=2 * elements
        ),
        name=f"blocks_from_{first}",
    )(base, picks, *args)


def local(queries, key_rows, values, out_grad, teacher_window, teacher_global, global_picks, mix_weight):
    tokens, columns = queries.shape
    blocks = tokens // BLK
    assert key_rows.shape[1] == E and blocks >= NGLOB
    where = lax.axis_index("seq")
    count = lax.axis_size("seq")
    base = (where * blocks).astype(jnp.int32).reshape(1)
    weights = mix_weight.reshape(blocks, 1, BLK)

    tail = slice(tokens - LEAD * BLK, tokens)
    first_rows = slice(0, NGLOB * BLK)
    sink_pair = jnp.stack([key_rows[first_rows], values[first_rows]])
    tail_pair = jnp.stack([key_rows[tail], values[tail]])
    sent = jnp.concatenate([tail_pair, sink_pair], axis=1)
    got = shift(sent, "seq", 1)
    before = got[:, :LEAD * BLK].reshape(2, LEAD, BLK, E)
    sinks = jnp.where(where == 0, sink_pair, got[:, LEAD * BLK:])
    reach = 2
    while reach < count:
        route = [(i, i + reach) for i in range(reach) if i + reach < count]
        more = lax.ppermute(sinks, "seq", route)
        sinks = jnp.where(where >= reach, more, sinks)
        reach *= 2

    incoming = {}
    for block in range(LEAD - 1, -1, -1):
        offsets = list(range(block + 1, WIN))
        out = jnp.concatenate(
            [teacher_window[blocks + block - d:blocks + block - d + 1, d:d + 1] for d in offsets], axis=0
        )
        came = shift(out, "seq", 1)
        incoming[block] = {d: came[i:i + 1] for i, d in enumerate(offsets)}

    own = (key_rows, values)
    sink_arrays = (sinks[0], sinks[1])
    run = lambda first, n, acc: run_blocks(
        first, n, base, global_picks, queries, out_grad, teacher_window, incoming.get(first),
        teacher_global, own, sink_arrays, weights, before, acc,
    )
    dq, loss = {}, {}
    dq[LEAD], loss[LEAD], *acc = run(LEAD, blocks - LEAD, None)
    back = 0.0
    for block in range(LEAD - 1, -1, -1):
        dq[block], loss[block], *rest = run(block, 1, acc)
        acc, part = rest[:4], rest[4]
        back = back + part
    order = sorted(dq)
    query_grad = jnp.concatenate([dq[i] for i in order], axis=0)
    row_terms = jnp.concatenate([loss[i] for i in order], axis=0).reshape(tokens)

    dk, dv, dsk, dsv = acc
    sums = jnp.stack([dsk, dsv])
    leaving = jnp.concatenate([back.reshape(2, LEAD * BLK, E), sums], axis=1).astype(BF)
    arrived = shift(leaving, "seq", -1)
    returned = arrived[:, :LEAD * BLK].astype(F32)
    sums = sums + arrived[:, LEAD * BLK:].astype(F32)
    reach = 2
    while reach < count:
        route = [(i, i - reach) for i in range(reach, count, 2 * reach)]
        sums = sums + lax.ppermute(sums.astype(BF), "seq", route).astype(F32)
        reach *= 2
    row_loss = sum_over(sum_over(row_terms, "grp"), "head")
    own_sums = jnp.stack([dk, dv])
    own_sums = own_sums.at[:, tail].add(returned)
    own_sums = own_sums.at[:, first_rows].add(jnp.where(where == 0, sums, 0.0))
    grads = own_sums.astype(BF)
    return (query_grad, grads[0], grads[1], row_loss)


def solution(mesh):
    heads = ("grp", "head")
    placed = (
        P("seq", heads),
        P("seq", heads),
        P("seq", heads),
        P("seq", heads),
        P("seq", None, heads, None, None),
        P("seq", None, heads, None, None),
        P("seq", None),
        P("seq"),
    )
    return jax.shard_map(
        local,
        mesh=mesh,
        in_specs=placed,
        out_specs=(P("seq", heads), P("seq", heads), P("seq", heads), P("seq")),
        check_vma=False,
    )
```

```python
import functools
import math

import jax
import jax.numpy as jnp
from jax import lax
from jax.experimental import pallas as pl
from jax.experimental.pallas import tpu as pltpu
from jax.sharding import PartitionSpec as P

E = 128
BLK = 128
WIN = 3
NGLOB = 4
LEAD = WIN - 1
FAN = 4
LOG2E = math.log2(math.e)
LN2 = math.log(2.0)
NT = (((1,), (1,)), ((), ()))
BF = jnp.bfloat16
F32 = jnp.float32


def shift(block, axis, distance):
    count = lax.axis_size(axis)
    route = [(i, i + distance) for i in range(count) if 0 <= i + distance < count]
    return lax.ppermute(block, axis, route)


def sum_over(block, axis):
    count = lax.axis_size(axis)
    if count & (count - 1):
        return lax.psum(block, axis)
    step = 1
    while step < count:
        block = block + lax.ppermute(block, axis, [(i, i ^ step) for i in range(count)])
        step *= 2
    return block


def block_kernel(
    first, crossing, slots, chained,
    base_ref, picks_ref, q_ref, g_ref, *rest,
):
    teacher_refs = rest[:slots]
    rest = rest[slots:]
    own_k, own_v, sink_k, sink_v, w_ref = rest[:5]
    rest = rest[5:]
    if crossing:
        before_ref, rest = rest[0], rest[1:]
    if chained:
        acc_in, rest = rest[:4], rest[4:]
    dq_ref, loss_ref, dk_ref, dv_ref, dsk_ref, dsv_ref = rest[:6]
    rest = rest[6:]
    if crossing:
        back_ref, rest = rest[0], rest[1:]
    ds_scr, pb_scr = rest
    step = pl.program_id(0)
    block = first + step
    heads = q_ref.shape[1] // E
    scale = 1.0 / math.sqrt(E)
    factor = scale * LOG2E

    @pl.when(step == 0)
    def _():
        if chained:
            for out, given in zip((dk_ref, dv_ref, dsk_ref, dsv_ref), acc_in):
                out[...] = given[...]
        else:
            for out in (dk_ref, dv_ref, dsk_ref, dsv_ref):
                out[...] = jnp.zeros_like(out)

    picks = [picks_ref[block, g] for g in range(slots - WIN)]
    live = [None] + [base_ref[0] + block - d >= 0 for d in range(1, WIN)] + [p >= 0 for p in picks]
    sink_at = [pl.multiple_of(jnp.maximum(p, 0) * BLK, BLK) for p in picks]

    def rows_of(d):
        return pl.ds(pl.multiple_of((block - d) * BLK, BLK), BLK)

    keys, vals = [], []
    for d in range(WIN):
        if d in crossing:
            at = first + LEAD - d
            keys.append(before_ref[0, at])
            vals.append(before_ref[1, at])
        else:
            keys.append(own_k[rows_of(d), :])
            vals.append(own_v[rows_of(d), :])
    for at in sink_at:
        keys.append(sink_k[pl.ds(at, BLK), :])
        vals.append(sink_v[pl.ds(at, BLK), :])
    kcat = jnp.concatenate(keys, axis=0)
    vcat = jnp.concatenate(vals, axis=0)
    kcat_t = kcat.T

    w1 = w_ref[0]
    w2 = jnp.concatenate([w1, w1], axis=1)
    slope = (w2 - 1.0) * LN2
    wide = 2 * BLK
    key_id = lax.broadcasted_iota(jnp.int32, (BLK, wide), 0)
    row_id = lax.broadcasted_iota(jnp.int32, (BLK, wide), 1) & (BLK - 1)
    causal = key_id <= row_id
    low = jnp.float32(-1e9)
    loss = jnp.zeros((1, wide), F32)

    def total(x):
        return jnp.sum(x, axis=0, keepdims=True)

    for pair in range(heads // 2):
        ha, hb = 2 * pair, 2 * pair + 1
        q2 = jnp.concatenate([q_ref[:, ha * E:(ha + 1) * E], q_ref[:, hb * E:(hb + 1) * E]], axis=0)
        g2 = jnp.concatenate([g_ref[:, ha * E:(ha + 1) * E], g_ref[:, hb * E:(hb + 1) * E]], axis=0)
        s_all = lax.dot_general(kcat, q2, NT, preferred_element_type=F32)
        pg_all = lax.dot_general(vcat, g2, NT, preferred_element_type=F32)
        held, stats = [], []
        for j in range(slots):
            s = s_all[j * BLK:(j + 1) * BLK]
            pg = pg_all[j * BLK:(j + 1) * BLK]
            t = jnp.concatenate([teacher_refs[j][0, 0, ha], teacher_refs[j][0, 0, hb]], axis=0)
            t = t.T.astype(F32)
            if j == 0:
                s = jnp.where(causal, s, low)
                t = jnp.where(causal, t, low)
            m = jnp.max(s, axis=0, keepdims=True)
            mt = jnp.max(t, axis=0, keepdims=True)
            x = (s - m) * factor
            y = (t - mt) * LOG2E
            es = jnp.exp2(x)
            et = jnp.exp2(y)
            gap = y - x
            u = pg + slope * gap
            stats.append((m, mt, total(es), total(et), total(et * gap), total(es * gap), total(es * u)))
            held.append((es, et, u))
        m = stats[0][0]
        mt = stats[0][1]
        for j in range(1, slots):
            m = jnp.maximum(m, jnp.where(live[j], stats[j][0], low))
            mt = jnp.maximum(mt, jnp.where(live[j], stats[j][1], low))
        a = [(st[0] - m) * factor for st in stats]
        b = [(st[1] - mt) * LOG2E for st in stats]
        fa = [jnp.exp2(v) for v in a]
        fb = [jnp.exp2(v) for v in b]
        for j in range(1, slots):
            fa[j] = jnp.where(live[j], fa[j], 0.0)
            fb[j] = jnp.where(live[j], fb[j], 0.0)
        z = functools.reduce(jnp.add, [f * st[2] for f, st in zip(fa, stats)])
        zt = functools.reduce(jnp.add, [f * st[3] for f, st in zip(fb, stats)])
        rz, rzt = 1.0 / z, 1.0 / zt
        both = jnp.log2(z) - jnp.log2(zt)
        off = [vb - va + both for va, vb in zip(a, b)]
        fwd = functools.reduce(jnp.add, [f * (st[4] + o * st[3]) for f, o, st in zip(fb, off, stats)])
        rev = functools.reduce(jnp.add, [f * (st[5] + o * st[2]) for f, o, st in zip(fa, off, stats)])
        mean_u = functools.reduce(
            jnp.add, [f * (st[6] + slope * o * st[2]) for f, o, st in zip(fa, off, stats)]
        )
        loss = loss + (w2 * LN2) * (rzt * fwd) + slope * (rz * rev)
        base = w2 - rz * mean_u
        cols = pl.ds(pair * wide, wide)
        for j in range(slots):
            es, et, u = held[j]
            p = es * (fa[j] * rz)
            ds = p * (u + (base + slope * off[j])) - et * (w2 * (fb[j] * rzt))
            ds_scr[j * BLK:(j + 1) * BLK, cols] = ds.astype(BF)
            pb_scr[j * BLK:(j + 1) * BLK, cols] = p.astype(BF)
        dq_t = jnp.dot(kcat_t, ds_scr[:, cols], preferred_element_type=F32) * scale
        dq2 = dq_t.T.astype(BF)
        dq_ref[:, ha * E:(ha + 1) * E] = dq2[:BLK]
        dq_ref[:, hb * E:(hb + 1) * E] = dq2[BLK:]
    loss_ref[0] = loss[:, :BLK] + loss[:, BLK:]

    q_all = jnp.concatenate([q_ref[:, h * E:(h + 1) * E] for h in range(heads)], axis=0)
    g_all = jnp.concatenate([g_ref[:, h * E:(h + 1) * E] for h in range(heads)], axis=0)
    dk = jnp.dot(ds_scr[...], q_all, preferred_element_type=F32) * scale
    dv = jnp.dot(pb_scr[...], g_all, preferred_element_type=F32)
    for d in range(WIN):
        part_k, part_v = dk[d * BLK:(d + 1) * BLK], dv[d * BLK:(d + 1) * BLK]
        if d in crossing:
            at = first + LEAD - d
            back_ref[0, at] = part_k
            back_ref[1, at] = part_v
        else:
            dk_ref[rows_of(d), :] += part_k
            dv_ref[rows_of(d), :] += part_v
    if crossing:
        untouched = [i for i in range(LEAD) if i not in [first + LEAD - d for d in crossing]]
        for i in untouched:
            back_ref[0, i] = jnp.zeros((BLK, E), F32)
            back_ref[1, i] = jnp.zeros((BLK, E), F32)
    for g, at in enumerate(sink_at):
        j = WIN + g
        dsk_ref[pl.ds(at, BLK), :] += dk[j * BLK:(j + 1) * BLK]
        dsv_ref[pl.ds(at, BLK), :] += dv[j * BLK:(j + 1) * BLK]


def run_blocks(first, count, base, picks, queries, out_grad, window, incoming, glob, own, sinks, weights,
               before, acc):
    crossing = [d for d in range(WIN) if d > first]
    assert not crossing or count == 1
    tokens, columns = queries.shape
    heads = window.shape[2]
    slots = WIN + picks.shape[1]
    tile = (1, 1, heads, BLK, BLK)
    whole = lambda i, *_: (0, 0)
    args = [queries, out_grad]
    specs = [pl.BlockSpec((BLK, columns), lambda i, *_: (first + i, 0))] * 2
    for d in range(WIN):
        if d in crossing:
            args.append(incoming[d])
            specs.append(pl.BlockSpec(tile, lambda i, *_: (0, 0, 0, 0, 0)))
        else:
            args.append(window)
            specs.append(pl.BlockSpec(tile, lambda i, *_, d=d: (first + i - d, d, 0, 0, 0)))
    for g in range(slots - WIN):
        args.append(glob)
        specs.append(pl.BlockSpec(tile, lambda i, *_, g=g: (first + i, g, 0, 0, 0)))
    for x in (*own, *sinks):
        args.append(x)
        specs.append(pl.BlockSpec(x.shape, whole))
    args.append(weights)
    specs.append(pl.BlockSpec((1, 1, BLK), lambda i, *_: (first + i, 0, 0)))
    if crossing:
        args.append(before)
        specs.append(pl.BlockSpec(before.shape, lambda i, *_: (0, 0, 0, 0)))
    chained = acc is not None
    acc_shapes = [(tokens, E)] * 2 + [(NGLOB * BLK, E)] * 2
    if chained:
        args.extend(acc)
        specs.extend(pl.BlockSpec(s, whole) for s in acc_shapes)
    outs = [
        jax.ShapeDtypeStruct((count * BLK, columns), BF),
        jax.ShapeDtypeStruct((count, 1, BLK), F32),
    ] + [jax.ShapeDtypeStruct(s, F32) for s in acc_shapes]
    out_specs = [
        pl.BlockSpec((BLK, columns), lambda i, *_: (i, 0)),
        pl.BlockSpec((1, 1, BLK), lambda i, *_: (i, 0, 0)),
    ] + [pl.BlockSpec(s, whole) for s in acc_shapes]
    if crossing:
        back = (2, LEAD, BLK, E)
        outs.append(jax.ShapeDtypeStruct(back, F32))
        out_specs.append(pl.BlockSpec(back, lambda i, *_: (0, 0, 0, 0)))
    elements = count * slots * heads * BLK * BLK
    return pl.pallas_call(
        functools.partial(block_kernel, first, crossing, slots, chained),
        out_shape=outs,
        grid_spec=pltpu.PrefetchScalarGridSpec(
            num_scalar_prefetch=2,
            grid=(count,),
            in_specs=specs,
            out_specs=out_specs,
            scratch_shapes=[pltpu.VMEM((slots * BLK, heads * BLK), BF)] * 2,
        ),
        compiler_params=pltpu.CompilerParams(vmem_limit_bytes=48 * 1024 * 1024),
        cost_estimate=pl.CostEstimate(
            flops=elements * E * 10, bytes_accessed=elements * 3, transcendentals=2 * elements
        ),
        name=f"blocks_from_{first}",
    )(base, picks, *args)


def local(queries, key_rows, values, out_grad, teacher_window, teacher_global, global_picks, mix_weight):
    tokens, columns = queries.shape
    blocks = tokens // BLK
    assert key_rows.shape[1] == E and blocks >= NGLOB
    where = lax.axis_index("seq")
    count = lax.axis_size("seq")
    base = (where * blocks).astype(jnp.int32).reshape(1)
    weights = mix_weight.reshape(blocks, 1, BLK)

    tail = slice(tokens - LEAD * BLK, tokens)
    first_rows = slice(0, NGLOB * BLK)
    pair = jnp.stack([key_rows, values])
    got = shift(pair, "seq", 1)
    before = got[:, tail].reshape(2, LEAD, BLK, E)
    sinks = jnp.where(where == 0, pair[:, first_rows], got[:, first_rows])
    span, known = 1, pair[:, first_rows]
    while span < count:
        for times in range(1, FAN):
            if span == 1 and times == 1:
                continue
            route = [(i, i + times * span) for i in range(span) if i + times * span < count]
            if route:
                more = lax.ppermute(known, "seq", route)
                sinks = jnp.where((where >= times * span) & (where < (times + 1) * span), more, sinks)
        span *= FAN
        known = sinks

    incoming = {}
    for block in range(LEAD - 1, -1, -1):
        offsets = list(range(block + 1, WIN))
        out = jnp.concatenate(
            [teacher_window[blocks + block - d:blocks + block - d + 1, d:d + 1] for d in offsets], axis=0
        )
        came = shift(out, "seq", 1)
        incoming[block] = {d: came[i:i + 1] for i, d in enumerate(offsets)}

    own = (key_rows, values)
    sink_arrays = (sinks[0], sinks[1])
    run = lambda first, n, acc: run_blocks(
        first, n, base, global_picks, queries, out_grad, teacher_window, incoming.get(first),
        teacher_global, own, sink_arrays, weights, before, acc,
    )
    dq, loss = {}, {}
    dq[LEAD], loss[LEAD], *acc = run(LEAD, blocks - LEAD, None)
    back = 0.0
    for block in range(LEAD - 1, -1, -1):
        dq[block], loss[block], *rest = run(block, 1, acc)
        acc, part = rest[:4], rest[4]
        back = back + part
    order = sorted(dq)
    query_grad = jnp.concatenate([dq[i] for i in order], axis=0)
    row_terms = jnp.concatenate([loss[i] for i in order], axis=0).reshape(tokens)

    dk, dv, dsk, dsv = acc
    sums = jnp.stack([dsk, dsv])
    leaving = jnp.concatenate([back.reshape(2, LEAD * BLK, E), sums], axis=1).astype(BF)
    arrived = shift(leaving, "seq", -1)
    returned = arrived[:, :LEAD * BLK].astype(F32)
    sums = sums + arrived[:, LEAD * BLK:].astype(F32)
    reach = 2
    while reach < count:
        route = [(i, i - reach) for i in range(reach, count, 2 * reach)]
        sums = sums + lax.ppermute(sums.astype(BF), "seq", route).astype(F32)
        reach *= 2
    row_loss = sum_over(sum_over(row_terms, "grp"), "head")
    own_sums = jnp.stack([dk, dv])
    own_sums = own_sums.at[:, tail].add(returned)
    own_sums = own_sums.at[:, first_rows].add(jnp.where(where == 0, sums, 0.0))
    grads = own_sums.astype(BF)
    return (query_grad, grads[0], grads[1], row_loss)


def solution(mesh):
    heads = ("grp", "head")
    placed = (
        P("seq", heads),
        P("seq", heads),
        P("seq", heads),
        P("seq", heads),
        P("seq", None, heads, None, None),
        P("seq", None, heads, None, None),
        P("seq", None),
        P("seq"),
    )
    return jax.shard_map(
        local,
        mesh=mesh,
        in_specs=placed,
        out_specs=(P("seq", heads), P("seq", heads), P("seq", heads), P("seq")),
        check_vma=False,
    )
```

```python
import functools
import math

import jax
import jax.numpy as jnp
from jax import lax
from jax.experimental import pallas as pl
from jax.experimental.pallas import tpu as pltpu
from jax.sharding import PartitionSpec as P

E = 128
BLK = 128
WIN = 3
NGLOB = 4
LEAD = WIN - 1
FAN = 4
LOG2E = math.log2(math.e)
LN2 = math.log(2.0)
NT = (((1,), (1,)), ((), ()))
BF = jnp.bfloat16
F32 = jnp.float32


def shift(block, axis, distance):
    count = lax.axis_size(axis)
    route = [(i, i + distance) for i in range(count) if 0 <= i + distance < count]
    return lax.ppermute(block, axis, route)


def sum_over(block, axis):
    count = lax.axis_size(axis)
    if count & (count - 1):
        return lax.psum(block, axis)
    step = 1
    while step < count:
        block = block + lax.ppermute(block, axis, [(i, i ^ step) for i in range(count)])
        step *= 2
    return block


def block_kernel(
    first, crossing, slots, chained,
    base_ref, picks_ref, q_ref, g_ref, *rest,
):
    teacher_refs = rest[:slots]
    rest = rest[slots:]
    own_k, own_v, sink_k, sink_v, w_ref = rest[:5]
    rest = rest[5:]
    if crossing:
        before_ref, rest = rest[0], rest[1:]
    if chained:
        acc_in, rest = rest[:4], rest[4:]
    dq_ref, loss_ref, dk_ref, dv_ref, dsk_ref, dsv_ref = rest[:6]
    rest = rest[6:]
    if crossing:
        back_ref, rest = rest[0], rest[1:]
    ds_scr, pb_scr = rest
    step = pl.program_id(0)
    block = first + step
    heads = q_ref.shape[1] // E
    scale = 1.0 / math.sqrt(E)
    factor = scale * LOG2E

    @pl.when(step == 0)
    def _():
        if chained:
            for out, given in zip((dk_ref, dv_ref, dsk_ref, dsv_ref), acc_in):
                out[...] = given[...]
        else:
            for out in (dk_ref, dv_ref, dsk_ref, dsv_ref):
                out[...] = jnp.zeros_like(out)

    picks = [picks_ref[block, g] for g in range(slots - WIN)]
    live = [None] + [base_ref[0] + block - d >= 0 for d in range(1, WIN)] + [p >= 0 for p in picks]
    sink_at = [pl.multiple_of(jnp.maximum(p, 0) * BLK, BLK) for p in picks]

    def rows_of(d):
        return pl.ds(pl.multiple_of((block - d) * BLK, BLK), BLK)

    keys, vals = [], []
    for d in range(WIN):
        if d in crossing:
            at = first + LEAD - d
            keys.append(before_ref[0, at])
            vals.append(before_ref[1, at])
        else:
            keys.append(own_k[rows_of(d), :])
            vals.append(own_v[rows_of(d), :])
    for at in sink_at:
        keys.append(sink_k[pl.ds(at, BLK), :])
        vals.append(sink_v[pl.ds(at, BLK), :])
    kcat = jnp.concatenate(keys, axis=0)
    vcat = jnp.concatenate(vals, axis=0)
    kcat_t = kcat.T

    w1 = w_ref[0]
    w2 = jnp.concatenate([w1, w1], axis=1)
    slope = (w2 - 1.0) * LN2
    wide = 2 * BLK
    key_id = lax.broadcasted_iota(jnp.int32, (BLK, wide), 0)
    row_id = lax.broadcasted_iota(jnp.int32, (BLK, wide), 1) & (BLK - 1)
    causal = key_id <= row_id
    low = jnp.float32(-1e9)
    loss = jnp.zeros((1, wide), F32)

    def total(x):
        return jnp.sum(x, axis=0, keepdims=True)

    for pair in range(heads // 2):
        ha, hb = 2 * pair, 2 * pair + 1
        q2 = jnp.concatenate([q_ref[:, ha * E:(ha + 1) * E], q_ref[:, hb * E:(hb + 1) * E]], axis=0)
        g2 = jnp.concatenate([g_ref[:, ha * E:(ha + 1) * E], g_ref[:, hb * E:(hb + 1) * E]], axis=0)
        s_all = lax.dot_general(kcat, q2, NT, preferred_element_type=F32)
        pg_all = lax.dot_general(vcat, g2, NT, preferred_element_type=F32)
        held, stats = [], []
        for j in range(slots):
            s = s_all[j * BLK:(j + 1) * BLK]
            pg = pg_all[j * BLK:(j + 1) * BLK]
            t = jnp.concatenate([teacher_refs[j][0, 0, ha], teacher_refs[j][0, 0, hb]], axis=0)
            t = t.T.astype(F32)
            if j == 0:
                s = jnp.where(causal, s, low)
                t = jnp.where(causal, t, low)
            m = jnp.max(s, axis=0, keepdims=True)
            mt = jnp.max(t, axis=0, keepdims=True)
            x = (s - m) * factor
            y = (t - mt) * LOG2E
            es = jnp.exp2(x)
            et = jnp.exp2(y)
            gap = y - x
            u = pg + slope * gap
            stats.append((m, mt, total(es), total(et), total(et * gap), total(es * gap), total(es * u)))
            held.append((es, et, u))
        m = stats[0][0]
        mt = stats[0][1]
        for j in range(1, slots):
            m = jnp.maximum(m, jnp.where(live[j], stats[j][0], low))
            mt = jnp.maximum(mt, jnp.where(live[j], stats[j][1], low))
        a = [(st[0] - m) * factor for st in stats]
        b = [(st[1] - mt) * LOG2E for st in stats]
        fa = [jnp.exp2(v) for v in a]
        fb = [jnp.exp2(v) for v in b]
        for j in range(1, slots):
            fa[j] = jnp.where(live[j], fa[j], 0.0)
            fb[j] = jnp.where(live[j], fb[j], 0.0)
        z = functools.reduce(jnp.add, [f * st[2] for f, st in zip(fa, stats)])
        zt = functools.reduce(jnp.add, [f * st[3] for f, st in zip(fb, stats)])
        rz, rzt = 1.0 / z, 1.0 / zt
        both = jnp.log2(z) - jnp.log2(zt)
        off = [vb - va + both for va, vb in zip(a, b)]
        fwd = functools.reduce(jnp.add, [f * (st[4] + o * st[3]) for f, o, st in zip(fb, off, stats)])
        rev = functools.reduce(jnp.add, [f * (st[5] + o * st[2]) for f, o, st in zip(fa, off, stats)])
        mean_u = functools.reduce(
            jnp.add, [f * (st[6] + slope * o * st[2]) for f, o, st in zip(fa, off, stats)]
        )
        loss = loss + (w2 * LN2) * (rzt * fwd) + slope * (rz * rev)
        base = w2 - rz * mean_u
        cols = pl.ds(pair * wide, wide)
        for j in range(slots):
            es, et, u = held[j]
            p = es * (fa[j] * rz)
            ds = p * (u + (base + slope * off[j])) - et * (w2 * (fb[j] * rzt))
            ds_scr[j * BLK:(j + 1) * BLK, cols] = ds.astype(BF)
            pb_scr[j * BLK:(j + 1) * BLK, cols] = p.astype(BF)
        dq_t = jnp.dot(kcat_t, ds_scr[:, cols], preferred_element_type=F32) * scale
        dq2 = dq_t.T.astype(BF)
        dq_ref[:, ha * E:(ha + 1) * E] = dq2[:BLK]
        dq_ref[:, hb * E:(hb + 1) * E] = dq2[BLK:]
    loss_ref[0] = loss[:, :BLK] + loss[:, BLK:]

    q_all = jnp.concatenate([q_ref[:, h * E:(h + 1) * E] for h in range(heads)], axis=0)
    g_all = jnp.concatenate([g_ref[:, h * E:(h + 1) * E] for h in range(heads)], axis=0)
    dk = jnp.dot(ds_scr[...], q_all, preferred_element_type=F32) * scale
    dv = jnp.dot(pb_scr[...], g_all, preferred_element_type=F32)
    for d in range(WIN):
        part_k, part_v = dk[d * BLK:(d + 1) * BLK], dv[d * BLK:(d + 1) * BLK]
        if d in crossing:
            at = first + LEAD - d
            back_ref[0, at] = part_k
            back_ref[1, at] = part_v
        else:
            dk_ref[rows_of(d), :] += part_k
            dv_ref[rows_of(d), :] += part_v
    if crossing:
        untouched = [i for i in range(LEAD) if i not in [first + LEAD - d for d in crossing]]
        for i in untouched:
            back_ref[0, i] = jnp.zeros((BLK, E), F32)
            back_ref[1, i] = jnp.zeros((BLK, E), F32)
    for g, at in enumerate(sink_at):
        j = WIN + g
        dsk_ref[pl.ds(at, BLK), :] += dk[j * BLK:(j + 1) * BLK]
        dsv_ref[pl.ds(at, BLK), :] += dv[j * BLK:(j + 1) * BLK]


def run_blocks(first, count, base, picks, queries, out_grad, window, incoming, glob, own, sinks, weights,
               before, acc):
    crossing = [d for d in range(WIN) if d > first]
    assert not crossing or count == 1
    tokens, columns = queries.shape
    heads = window.shape[2]
    slots = WIN + picks.shape[1]
    tile = (1, 1, heads, BLK, BLK)
    whole = lambda i, *_: (0, 0)
    args = [queries, out_grad]
    specs = [pl.BlockSpec((BLK, columns), lambda i, *_: (first + i, 0))] * 2
    for d in range(WIN):
        if d in crossing:
            args.append(incoming[d])
            specs.append(pl.BlockSpec(tile, lambda i, *_: (0, 0, 0, 0, 0)))
        else:
            args.append(window)
            specs.append(pl.BlockSpec(tile, lambda i, *_, d=d: (first + i - d, d, 0, 0, 0)))
    for g in range(slots - WIN):
        args.append(glob)
        specs.append(pl.BlockSpec(tile, lambda i, *_, g=g: (first + i, g, 0, 0, 0)))
    for x in (*own, *sinks):
        args.append(x)
        specs.append(pl.BlockSpec(x.shape, whole))
    args.append(weights)
    specs.append(pl.BlockSpec((1, 1, BLK), lambda i, *_: (first + i, 0, 0)))
    if crossing:
        args.append(before)
        specs.append(pl.BlockSpec(before.shape, lambda i, *_: (0, 0, 0, 0)))
    chained = acc is not None
    acc_shapes = [(tokens, E)] * 2 + [(NGLOB * BLK, E)] * 2
    if chained:
        args.extend(acc)
        specs.extend(pl.BlockSpec(s, whole) for s in acc_shapes)
    outs = [
        jax.ShapeDtypeStruct((count * BLK, columns), BF),
        jax.ShapeDtypeStruct((count, 1, BLK), F32),
    ] + [jax.ShapeDtypeStruct(s, F32) for s in acc_shapes]
    out_specs = [
        pl.BlockSpec((BLK, columns), lambda i, *_: (i, 0)),
        pl.BlockSpec((1, 1, BLK), lambda i, *_: (i, 0, 0)),
    ] + [pl.BlockSpec(s, whole) for s in acc_shapes]
    if crossing:
        back = (2, LEAD, BLK, E)
        outs.append(jax.ShapeDtypeStruct(back, F32))
        out_specs.append(pl.BlockSpec(back, lambda i, *_: (0, 0, 0, 0)))
    elements = count * slots * heads * BLK * BLK
    return pl.pallas_call(
        functools.partial(block_kernel, first, crossing, slots, chained),
        out_shape=outs,
        grid_spec=pltpu.PrefetchScalarGridSpec(
            num_scalar_prefetch=2,
            grid=(count,),
            in_specs=specs,
            out_specs=out_specs,
            scratch_shapes=[pltpu.VMEM((slots * BLK, heads * BLK), BF)] * 2,
        ),
        compiler_params=pltpu.CompilerParams(vmem_limit_bytes=48 * 1024 * 1024),
        cost_estimate=pl.CostEstimate(
            flops=elements * E * 10, bytes_accessed=elements * 3, transcendentals=2 * elements
        ),
        name=f"blocks_from_{first}",
    )(base, picks, *args)


def local(queries, key_rows, values, out_grad, teacher_window, teacher_global, global_picks, mix_weight):
    tokens, columns = queries.shape
    blocks = tokens // BLK
    assert key_rows.shape[1] == E and blocks >= NGLOB
    where = lax.axis_index("seq")
    count = lax.axis_size("seq")
    base = (where * blocks).astype(jnp.int32).reshape(1)
    weights = mix_weight.reshape(blocks, 1, BLK)

    tail = slice(tokens - LEAD * BLK, tokens)
    first_rows = slice(0, NGLOB * BLK)
    pair = jnp.stack([key_rows, values])
    got = shift(pair, "seq", 1)
    before = got[:, tail].reshape(2, LEAD, BLK, E)
    sinks = jnp.where(where == 0, pair[:, first_rows], got[:, first_rows])
    span, known = 1, pair[:, first_rows]
    while span < count:
        for times in range(1, FAN):
            if span == 1 and times == 1:
                continue
            route = [(i, i + times * span) for i in range(span) if i + times * span < count]
            if route:
                more = lax.ppermute(known, "seq", route)
                sinks = jnp.where((where >= times * span) & (where < (times + 1) * span), more, sinks)
        span *= FAN
        known = sinks

    incoming = {}
    for block in range(LEAD - 1, -1, -1):
        offsets = list(range(block + 1, WIN))
        out = jnp.concatenate(
            [teacher_window[blocks + block - d:blocks + block - d + 1, d:d + 1] for d in offsets], axis=0
        )
        came = shift(out, "seq", 1)
        incoming[block] = {d: came[i:i + 1] for i, d in enumerate(offsets)}

    own = (key_rows, values)
    sink_arrays = (sinks[0], sinks[1])
    run = lambda first, n, acc: run_blocks(
        first, n, base, global_picks, queries, out_grad, teacher_window, incoming.get(first),
        teacher_global, own, sink_arrays, weights, before, acc,
    )
    dq, loss = {}, {}
    dq[LEAD], loss[LEAD], *acc = run(LEAD, blocks - LEAD, None)
    back = 0.0
    for block in range(LEAD - 1, -1, -1):
        dq[block], loss[block], *rest = run(block, 1, acc)
        acc, part = rest[:4], rest[4]
        back = back + part
    order = sorted(dq)
    query_grad = jnp.concatenate([dq[i] for i in order], axis=0)
    row_terms = jnp.concatenate([loss[i] for i in order], axis=0).reshape(tokens)

    dk, dv, dsk, dsv = acc
    sums = [dsk, dsv]
    steps = []
    reach = 1
    while reach < count:
        steps.append([(i, i - reach) for i in range(reach, count, 2 * reach)])
        reach *= 2
    returned = None
    for number, route in enumerate(steps):
        low = [x.astype(BF) for x in sums]
        if number == 1:
            row_terms, low[1] = lax.optimization_barrier((row_terms, low[1]))
        came = [lax.ppermute(x, "seq", route) for x in low]
        if number == 0:
            returned = shift(back.astype(BF), "seq", -1).astype(F32)
        sums = [x + y.astype(F32) for x, y in zip(sums, came)]
    row_loss = sum_over(sum_over(row_terms, "grp"), "head")
    grads = []
    for which, own_sum in enumerate((dk, dv)):
        whole = own_sum.at[tail].add(returned[which].reshape(LEAD * BLK, E))
        whole = whole.at[first_rows].add(jnp.where(where == 0, sums[which], 0.0))
        grads.append(whole.astype(BF))
    return (query_grad, grads[0], grads[1], row_loss)


def solution(mesh):
    heads = ("grp", "head")
    placed = (
        P("seq", heads),
        P("seq", heads),
        P("seq", heads),
        P("seq", heads),
        P("seq", None, heads, None, None),
        P("seq", None, heads, None, None),
        P("seq", None),
        P("seq"),
    )
    return jax.shard_map(
        local,
        mesh=mesh,
        in_specs=placed,
        out_specs=(P("seq", heads), P("seq", heads), P("seq", heads), P("seq")),
        check_vma=False,
    )
```

```python
import functools
import math

import jax
import jax.numpy as jnp
from jax import lax
from jax.experimental import pallas as pl
from jax.experimental.pallas import tpu as pltpu
from jax.sharding import PartitionSpec as P

E = 128
BLK = 128
WIN = 3
NGLOB = 4
LEAD = WIN - 1
FAN = 4
CHUNK = 32
LOG2E = math.log2(math.e)
LN2 = math.log(2.0)
NT = (((1,), (1,)), ((), ()))
BF = jnp.bfloat16
F32 = jnp.float32


def shift(block, axis, distance):
    count = lax.axis_size(axis)
    route = [(i, i + distance) for i in range(count) if 0 <= i + distance < count]
    return lax.ppermute(block, axis, route)


def sum_over(block, axis):
    count = lax.axis_size(axis)
    if count & (count - 1):
        return lax.psum(block, axis)
    step = 1
    while step < count:
        block = block + lax.ppermute(block, axis, [(i, i ^ step) for i in range(count)])
        step *= 2
    return block


def block_kernel(
    first, crossing, slots, chained,
    base_ref, picks_ref, q_ref, g_ref, *rest,
):
    teacher_refs = rest[:slots]
    rest = rest[slots:]
    own_k, own_v, sink_k, sink_v, w_ref = rest[:5]
    rest = rest[5:]
    if crossing:
        before_ref, rest = rest[0], rest[1:]
    if chained:
        acc_in, rest = rest[:4], rest[4:]
    dq_ref, loss_ref, dk_ref, dv_ref, dsk_ref, dsv_ref = rest[:6]
    rest = rest[6:]
    if crossing:
        back_ref, rest = rest[0], rest[1:]
    ds_scr, pb_scr, s_scr, t_scr, u_scr = rest
    step = pl.program_id(0)
    block = first + step
    heads = q_ref.shape[1] // E
    scale = 1.0 / math.sqrt(E)
    factor = scale * LOG2E

    @pl.when(step == 0)
    def _():
        if chained:
            for out, given in zip((dk_ref, dv_ref, dsk_ref, dsv_ref), acc_in):
                out[...] = given[...]
        else:
            for out in (dk_ref, dv_ref, dsk_ref, dsv_ref):
                out[...] = jnp.zeros_like(out)

    picks = [picks_ref[block, g] for g in range(slots - WIN)]
    live = [None] + [base_ref[0] + block - d >= 0 for d in range(1, WIN)] + [p >= 0 for p in picks]
    sink_at = [pl.multiple_of(jnp.maximum(p, 0) * BLK, BLK) for p in picks]

    def rows_of(d):
        return pl.ds(pl.multiple_of((block - d) * BLK, BLK), BLK)

    keys, vals = [], []
    for d in range(WIN):
        if d in crossing:
            at = first + LEAD - d
            keys.append(before_ref[0, at])
            vals.append(before_ref[1, at])
        else:
            keys.append(own_k[rows_of(d), :])
            vals.append(own_v[rows_of(d), :])
    for at in sink_at:
        keys.append(sink_k[pl.ds(at, BLK), :])
        vals.append(sink_v[pl.ds(at, BLK), :])
    kcat = jnp.concatenate(keys, axis=0)
    vcat = jnp.concatenate(vals, axis=0)
    kcat_t = kcat.T

    w1 = w_ref[0]
    w2 = jnp.concatenate([w1, w1], axis=1)
    slope = (w2 - 1.0) * LN2
    wide = 2 * BLK
    key_id = lax.broadcasted_iota(jnp.int32, (BLK, wide), 0)
    row_id = lax.broadcasted_iota(jnp.int32, (BLK, wide), 1) & (BLK - 1)
    causal = key_id <= row_id
    low = jnp.float32(-1e9)
    loss = jnp.zeros((1, wide), F32)

    def rows_pair(ref, pair):
        ha, hb = 2 * pair, 2 * pair + 1
        return jnp.concatenate([ref[:, ha * E:(ha + 1) * E], ref[:, hb * E:(hb + 1) * E]], axis=0)

    def products(pair):
        at = pair % 2
        s_scr[at] = lax.dot_general(kcat, rows_pair(q_ref, pair), NT, preferred_element_type=F32)
        u_scr[at] = lax.dot_general(vcat, rows_pair(g_ref, pair), NT, preferred_element_type=F32)

    def fold(x, op):
        return functools.reduce(op, [x[i:i + 8] for i in range(0, CHUNK, 8)])

    def up(x):
        return jnp.sum(x, axis=0, keepdims=True)

    products(0)
    dk = dv = 0.0
    for pair in range(heads // 2):
        at = pair % 2
        if pair + 1 < heads // 2:
            products(pair + 1)
        ha, hb = 2 * pair, 2 * pair + 1
        stats = []
        for j in range(slots):
            tile = slice(j * BLK, (j + 1) * BLK)
            t = jnp.concatenate([teacher_refs[j][0, 0, ha], teacher_refs[j][0, 0, hb]], axis=0)
            t = t.T.astype(F32)
            if j == 0:
                t = jnp.where(causal, t, low)
                s_scr[at, tile] = jnp.where(causal, s_scr[at, tile], low)
            t_scr[at, tile] = t
            chunks = [slice(k, k + CHUNK) for k in range(j * BLK, (j + 1) * BLK, CHUNK)]
            m = functools.reduce(jnp.maximum, [fold(s_scr[at, c], jnp.maximum) for c in chunks])
            mt = functools.reduce(jnp.maximum, [fold(t_scr[at, c], jnp.maximum) for c in chunks])
            m = jnp.max(m, axis=0, keepdims=True)
            mt = jnp.max(mt, axis=0, keepdims=True)
            sums = None
            for c in chunks:
                x = (s_scr[at, c] - m) * factor
                y = (t_scr[at, c] - mt) * LOG2E
                es = jnp.exp2(x)
                et = jnp.exp2(y)
                gap = y - x
                u = u_scr[at, c] + slope * gap
                part = [fold(v, jnp.add) for v in (es, et, et * gap, es * gap, es * u)]
                sums = part if sums is None else [v + w for v, w in zip(sums, part)]
                s_scr[at, c] = es
                t_scr[at, c] = et
                u_scr[at, c] = u
            stats.append((m, mt, *[up(v) for v in sums]))
        m = stats[0][0]
        mt = stats[0][1]
        for j in range(1, slots):
            m = jnp.maximum(m, jnp.where(live[j], stats[j][0], low))
            mt = jnp.maximum(mt, jnp.where(live[j], stats[j][1], low))
        a = [(st[0] - m) * factor for st in stats]
        b = [(st[1] - mt) * LOG2E for st in stats]
        fa = [jnp.exp2(v) for v in a]
        fb = [jnp.exp2(v) for v in b]
        for j in range(1, slots):
            fa[j] = jnp.where(live[j], fa[j], 0.0)
            fb[j] = jnp.where(live[j], fb[j], 0.0)
        z = functools.reduce(jnp.add, [f * st[2] for f, st in zip(fa, stats)])
        zt = functools.reduce(jnp.add, [f * st[3] for f, st in zip(fb, stats)])
        rz, rzt = 1.0 / z, 1.0 / zt
        both = jnp.log2(z) - jnp.log2(zt)
        off = [vb - va + both for va, vb in zip(a, b)]
        fwd = functools.reduce(jnp.add, [f * (st[4] + o * st[3]) for f, o, st in zip(fb, off, stats)])
        rev = functools.reduce(jnp.add, [f * (st[5] + o * st[2]) for f, o, st in zip(fa, off, stats)])
        mean_u = functools.reduce(
            jnp.add, [f * (st[6] + slope * o * st[2]) for f, o, st in zip(fa, off, stats)]
        )
        loss = loss + (w2 * LN2) * (rzt * fwd) + slope * (rz * rev)
        base = w2 - rz * mean_u
        cols = slice(pair * wide, (pair + 1) * wide)
        for j in range(slots):
            to_p = fa[j] * rz
            to_t = w2 * (fb[j] * rzt)
            lift = base + slope * off[j]
            for k in range(j * BLK, (j + 1) * BLK, CHUNK):
                c = slice(k, k + CHUNK)
                p = s_scr[at, c] * to_p
                ds_scr[c, cols] = (p * (u_scr[at, c] + lift) - t_scr[at, c] * to_t).astype(BF)
                pb_scr[c, cols] = p.astype(BF)
        dq_t = jnp.dot(kcat_t, ds_scr[:, cols], preferred_element_type=F32) * scale
        dq2 = dq_t.T.astype(BF)
        dq_ref[:, ha * E:(ha + 1) * E] = dq2[:BLK]
        dq_ref[:, hb * E:(hb + 1) * E] = dq2[BLK:]
        if pair % 2 == 1 or pair + 1 == heads // 2:
            first_pair = pair - pair % 2
            cols = slice(first_pair * wide, (pair + 1) * wide)
            q_part = jnp.concatenate([rows_pair(q_ref, n) for n in range(first_pair, pair + 1)], axis=0)
            g_part = jnp.concatenate([rows_pair(g_ref, n) for n in range(first_pair, pair + 1)], axis=0)
            dk = dk + jnp.dot(ds_scr[:, cols], q_part, preferred_element_type=F32)
            dv = dv + jnp.dot(pb_scr[:, cols], g_part, preferred_element_type=F32)
    loss_ref[0] = loss[:, :BLK] + loss[:, BLK:]
    dk = dk * scale
    for d in range(WIN):
        part_k, part_v = dk[d * BLK:(d + 1) * BLK], dv[d * BLK:(d + 1) * BLK]
        if d in crossing:
            at = first + LEAD - d
            back_ref[0, at] = part_k
            back_ref[1, at] = part_v
        else:
            dk_ref[rows_of(d), :] += part_k
            dv_ref[rows_of(d), :] += part_v
    if crossing:
        untouched = [i for i in range(LEAD) if i not in [first + LEAD - d for d in crossing]]
        for i in untouched:
            back_ref[0, i] = jnp.zeros((BLK, E), F32)
            back_ref[1, i] = jnp.zeros((BLK, E), F32)
    for g, at in enumerate(sink_at):
        j = WIN + g
        dsk_ref[pl.ds(at, BLK), :] += dk[j * BLK:(j + 1) * BLK]
        dsv_ref[pl.ds(at, BLK), :] += dv[j * BLK:(j + 1) * BLK]


def run_blocks(first, count, base, picks, queries, out_grad, window, incoming, glob, own, sinks, weights,
               before, acc):
    crossing = [d for d in range(WIN) if d > first]
    assert not crossing or count == 1
    tokens, columns = queries.shape
    heads = window.shape[2]
    slots = WIN + picks.shape[1]
    tile = (1, 1, heads, BLK, BLK)
    whole = lambda i, *_: (0, 0)
    args = [queries, out_grad]
    specs = [pl.BlockSpec((BLK, columns), lambda i, *_: (first + i, 0))] * 2
    for d in range(WIN):
        if d in crossing:
            args.append(incoming[d])
            specs.append(pl.BlockSpec(tile, lambda i, *_: (0, 0, 0, 0, 0)))
        else:
            args.append(window)
            specs.append(pl.BlockSpec(tile, lambda i, *_, d=d: (first + i - d, d, 0, 0, 0)))
    for g in range(slots - WIN):
        args.append(glob)
        specs.append(pl.BlockSpec(tile, lambda i, *_, g=g: (first + i, g, 0, 0, 0)))
    for x in (*own, *sinks):
        args.append(x)
        specs.append(pl.BlockSpec(x.shape, whole))
    args.append(weights)
    specs.append(pl.BlockSpec((1, 1, BLK), lambda i, *_: (first + i, 0, 0)))
    if crossing:
        args.append(before)
        specs.append(pl.BlockSpec(before.shape, lambda i, *_: (0, 0, 0, 0)))
    chained = acc is not None
    acc_shapes = [(tokens, E)] * 2 + [(NGLOB * BLK, E)] * 2
    if chained:
        args.extend(acc)
        specs.extend(pl.BlockSpec(s, whole) for s in acc_shapes)
    outs = [
        jax.ShapeDtypeStruct((count * BLK, columns), BF),
        jax.ShapeDtypeStruct((count, 1, BLK), F32),
    ] + [jax.ShapeDtypeStruct(s, F32) for s in acc_shapes]
    out_specs = [
        pl.BlockSpec((BLK, columns), lambda i, *_: (i, 0)),
        pl.BlockSpec((1, 1, BLK), lambda i, *_: (i, 0, 0)),
    ] + [pl.BlockSpec(s, whole) for s in acc_shapes]
    if crossing:
        back = (2, LEAD, BLK, E)
        outs.append(jax.ShapeDtypeStruct(back, F32))
        out_specs.append(pl.BlockSpec(back, lambda i, *_: (0, 0, 0, 0)))
    elements = count * slots * heads * BLK * BLK
    return pl.pallas_call(
        functools.partial(block_kernel, first, crossing, slots, chained),
        out_shape=outs,
        grid_spec=pltpu.PrefetchScalarGridSpec(
            num_scalar_prefetch=2,
            grid=(count,),
            in_specs=specs,
            out_specs=out_specs,
            scratch_shapes=[pltpu.VMEM((slots * BLK, heads * BLK), BF)] * 2
            + [pltpu.VMEM((2, slots * BLK, 2 * BLK), F32)] * 3,
        ),
        compiler_params=pltpu.CompilerParams(vmem_limit_bytes=48 * 1024 * 1024),
        cost_estimate=pl.CostEstimate(
            flops=elements * E * 10, bytes_accessed=elements * 3, transcendentals=2 * elements
        ),
        name=f"blocks_from_{first}",
    )(base, picks, *args)


def local(queries, key_rows, values, out_grad, teacher_window, teacher_global, global_picks, mix_weight):
    tokens, columns = queries.shape
    blocks = tokens // BLK
    assert key_rows.shape[1] == E and blocks >= NGLOB
    where = lax.axis_index("seq")
    count = lax.axis_size("seq")
    base = (where * blocks).astype(jnp.int32).reshape(1)
    weights = mix_weight.reshape(blocks, 1, BLK)

    tail = slice(tokens - LEAD * BLK, tokens)
    first_rows = slice(0, NGLOB * BLK)
    pair = jnp.stack([key_rows, values])
    got = shift(pair, "seq", 1)
    before = got[:, tail].reshape(2, LEAD, BLK, E)
    sinks = jnp.where(where == 0, pair[:, first_rows], got[:, first_rows])
    span, known = 1, pair[:, first_rows]
    while span < count:
        for times in range(1, FAN):
            if span == 1 and times == 1:
                continue
            route = [(i, i + times * span) for i in range(span) if i + times * span < count]
            if route:
                more = lax.ppermute(known, "seq", route)
                sinks = jnp.where((where >= times * span) & (where < (times + 1) * span), more, sinks)
        span *= FAN
        known = sinks

    incoming = {}
    for block in range(LEAD - 1, -1, -1):
        offsets = list(range(block + 1, WIN))
        out = jnp.concatenate(
            [teacher_window[blocks + block - d:blocks + block - d + 1, d:d + 1] for d in offsets], axis=0
        )
        came = shift(out, "seq", 1)
        incoming[block] = {d: came[i:i + 1] for i, d in enumerate(offsets)}

    own = (key_rows, values)
    sink_arrays = (sinks[0], sinks[1])
    run = lambda first, n, acc: run_blocks(
        first, n, base, global_picks, queries, out_grad, teacher_window, incoming.get(first),
        teacher_global, own, sink_arrays, weights, before, acc,
    )
    dq, loss = {}, {}
    dq[LEAD], loss[LEAD], *acc = run(LEAD, blocks - LEAD, None)
    back = 0.0
    for block in range(LEAD - 1, -1, -1):
        dq[block], loss[block], *rest = run(block, 1, acc)
        acc, part = rest[:4], rest[4]
        back = back + part
    order = sorted(dq)
    query_grad = jnp.concatenate([dq[i] for i in order], axis=0)
    row_terms = jnp.concatenate([loss[i] for i in order], axis=0).reshape(tokens)

    dk, dv, dsk, dsv = acc
    sums = [dsk, dsv]
    steps = []
    reach = 1
    while reach < count:
        steps.append([(i, i - reach) for i in range(reach, count, 2 * reach)])
        reach *= 2
    returned = None
    for number, route in enumerate(steps):
        low = [x.astype(BF) for x in sums]
        if number == 1:
            row_terms, low[1] = lax.optimization_barrier((row_terms, low[1]))
        came = [lax.ppermute(x, "seq", route) for x in low]
        if number == 0:
            returned = shift(back.astype(BF), "seq", -1).astype(F32)
        sums = [x + y.astype(F32) for x, y in zip(sums, came)]
    row_loss = sum_over(sum_over(row_terms, "grp"), "head")
    grads = []
    for which, own_sum in enumerate((dk, dv)):
        whole = own_sum.at[tail].add(returned[which].reshape(LEAD * BLK, E))
        whole = whole.at[first_rows].add(jnp.where(where == 0, sums[which], 0.0))
        grads.append(whole.astype(BF))
    return (query_grad, grads[0], grads[1], row_loss)


def solution(mesh):
    heads = ("grp", "head")
    placed = (
        P("seq", heads),
        P("seq", heads),
        P("seq", heads),
        P("seq", heads),
        P("seq", None, heads, None, None),
        P("seq", None, heads, None, None),
        P("seq", None),
        P("seq"),
    )
    return jax.shard_map(
        local,
        mesh=mesh,
        in_specs=placed,
        out_specs=(P("seq", heads), P("seq", heads), P("seq", heads), P("seq")),
        check_vma=False,
    )
```

```python
import functools
import math

import jax
import jax.numpy as jnp
from jax import lax
from jax.experimental import pallas as pl
from jax.experimental.pallas import tpu as pltpu
from jax.sharding import PartitionSpec as P

E = 128
BLK = 128
WIN = 3
NGLOB = 4
LEAD = WIN - 1
FAN = 4
CHUNK = 32
LOG2E = math.log2(math.e)
LN2 = math.log(2.0)
NT = (((1,), (1,)), ((), ()))
BF = jnp.bfloat16
F32 = jnp.float32


def shift(block, axis, distance):
    count = lax.axis_size(axis)
    route = [(i, i + distance) for i in range(count) if 0 <= i + distance < count]
    return lax.ppermute(block, axis, route)


def sum_over(block, axis):
    count = lax.axis_size(axis)
    if count & (count - 1):
        return lax.psum(block, axis)
    step = 1
    while step < count:
        block = block + lax.ppermute(block, axis, [(i, i ^ step) for i in range(count)])
        step *= 2
    return block


def block_kernel(
    first, crossing, slots, chained,
    base_ref, picks_ref, q_ref, g_ref, *rest,
):
    teacher_refs = rest[:slots]
    rest = rest[slots:]
    own_k, own_v, sink_k, sink_v, w_ref = rest[:5]
    rest = rest[5:]
    if crossing:
        before_ref, rest = rest[0], rest[1:]
    if chained:
        acc_in, rest = rest[:4], rest[4:]
    dq_ref, loss_ref, dk_ref, dv_ref, dsk_ref, dsv_ref = rest[:6]
    rest = rest[6:]
    if crossing:
        back_ref, rest = rest[0], rest[1:]
    ds_scr, pb_scr, s_scr, t_scr, u_scr = rest
    step = pl.program_id(0)
    block = first + step
    heads = q_ref.shape[1] // E
    scale = 1.0 / math.sqrt(E)
    factor = scale * LOG2E

    @pl.when(step == 0)
    def _():
        if chained:
            for out, given in zip((dk_ref, dv_ref, dsk_ref, dsv_ref), acc_in):
                out[...] = given[...]
        else:
            for out in (dk_ref, dv_ref, dsk_ref, dsv_ref):
                out[...] = jnp.zeros_like(out)

    picks = [picks_ref[block, g] for g in range(slots - WIN)]
    live = [None] + [base_ref[0] + block - d >= 0 for d in range(1, WIN)] + [p >= 0 for p in picks]
    sink_at = [pl.multiple_of(jnp.maximum(p, 0) * BLK, BLK) for p in picks]

    def rows_of(d):
        return pl.ds(pl.multiple_of((block - d) * BLK, BLK), BLK)

    keys, vals = [], []
    for d in range(WIN):
        if d in crossing:
            at = first + LEAD - d
            keys.append(before_ref[0, at])
            vals.append(before_ref[1, at])
        else:
            keys.append(own_k[rows_of(d), :])
            vals.append(own_v[rows_of(d), :])
    for at in sink_at:
        keys.append(sink_k[pl.ds(at, BLK), :])
        vals.append(sink_v[pl.ds(at, BLK), :])
    kcat = jnp.concatenate(keys, axis=0)
    vcat = jnp.concatenate(vals, axis=0)
    kcat_t = kcat.T

    w1 = w_ref[0]
    w2 = jnp.concatenate([w1, w1], axis=1)
    slope = (w2 - 1.0) * LN2
    wide = 2 * BLK
    key_id = lax.broadcasted_iota(jnp.int32, (BLK, wide), 0)
    row_id = lax.broadcasted_iota(jnp.int32, (BLK, wide), 1) & (BLK - 1)
    causal = key_id <= row_id
    square = (BLK, BLK)
    unit = (lax.broadcasted_iota(jnp.int32, square, 0) == lax.broadcasted_iota(jnp.int32, square, 1)).astype(F32).astype(BF)
    low = jnp.float32(-1e9)
    loss = jnp.zeros((1, wide), F32)

    def rows_pair(ref, pair):
        ha, hb = 2 * pair, 2 * pair + 1
        return jnp.concatenate([ref[:, ha * E:(ha + 1) * E], ref[:, hb * E:(hb + 1) * E]], axis=0)

    def products(pair):
        at = pair % 2
        s_scr[at] = lax.dot_general(kcat, rows_pair(q_ref, pair), NT, preferred_element_type=F32)
        u_scr[at] = lax.dot_general(vcat, rows_pair(g_ref, pair), NT, preferred_element_type=F32)

    def fold(x, op):
        return functools.reduce(op, [x[i:i + 8] for i in range(0, CHUNK, 8)])

    def up(x):
        return jnp.sum(x, axis=0, keepdims=True)

    products(0)
    dk = dv = 0.0
    for pair in range(heads // 2):
        at = pair % 2
        if pair + 1 < heads // 2:
            products(pair + 1)
        ha, hb = 2 * pair, 2 * pair + 1
        stats = []
        for j in range(slots):
            tile = slice(j * BLK, (j + 1) * BLK)
            t = jnp.concatenate([teacher_refs[j][0, 0, ha], teacher_refs[j][0, 0, hb]], axis=0)
            t = lax.dot_general(unit, t, NT, preferred_element_type=F32)
            if j == 0:
                t = jnp.where(causal, t, low)
                s_scr[at, tile] = jnp.where(causal, s_scr[at, tile], low)
            t_scr[at, tile] = t
            chunks = [slice(k, k + CHUNK) for k in range(j * BLK, (j + 1) * BLK, CHUNK)]
            m = functools.reduce(jnp.maximum, [fold(s_scr[at, c], jnp.maximum) for c in chunks])
            mt = functools.reduce(jnp.maximum, [fold(t_scr[at, c], jnp.maximum) for c in chunks])
            m = jnp.max(m, axis=0, keepdims=True)
            mt = jnp.max(mt, axis=0, keepdims=True)
            sums = None
            for c in chunks:
                x = (s_scr[at, c] - m) * factor
                y = (t_scr[at, c] - mt) * LOG2E
                es = jnp.exp2(x)
                et = jnp.exp2(y)
                gap = y - x
                u = u_scr[at, c] + slope * gap
                part = [fold(v, jnp.add) for v in (es, et, et * gap, es * gap, es * u)]
                sums = part if sums is None else [v + w for v, w in zip(sums, part)]
                s_scr[at, c] = es
                t_scr[at, c] = et
                u_scr[at, c] = u
            stats.append((m, mt, *[up(v) for v in sums]))
        m = stats[0][0]
        mt = stats[0][1]
        for j in range(1, slots):
            m = jnp.maximum(m, jnp.where(live[j], stats[j][0], low))
            mt = jnp.maximum(mt, jnp.where(live[j], stats[j][1], low))
        a = [(st[0] - m) * factor for st in stats]
        b = [(st[1] - mt) * LOG2E for st in stats]
        fa = [jnp.exp2(v) for v in a]
        fb = [jnp.exp2(v) for v in b]
        for j in range(1, slots):
            fa[j] = jnp.where(live[j], fa[j], 0.0)
            fb[j] = jnp.where(live[j], fb[j], 0.0)
        z = functools.reduce(jnp.add, [f * st[2] for f, st in zip(fa, stats)])
        zt = functools.reduce(jnp.add, [f * st[3] for f, st in zip(fb, stats)])
        rz, rzt = 1.0 / z, 1.0 / zt
        both = jnp.log2(z) - jnp.log2(zt)
        off = [vb - va + both for va, vb in zip(a, b)]
        fwd = functools.reduce(jnp.add, [f * (st[4] + o * st[3]) for f, o, st in zip(fb, off, stats)])
        rev = functools.reduce(jnp.add, [f * (st[5] + o * st[2]) for f, o, st in zip(fa, off, stats)])
        mean_u = functools.reduce(
            jnp.add, [f * (st[6] + slope * o * st[2]) for f, o, st in zip(fa, off, stats)]
        )
        loss = loss + (w2 * LN2) * (rzt * fwd) + slope * (rz * rev)
        base = w2 - rz * mean_u
        cols = slice(pair * wide, (pair + 1) * wide)
        for j in range(slots):
            to_p = fa[j] * rz
            to_t = w2 * (fb[j] * rzt)
            lift = base + slope * off[j]
            for k in range(j * BLK, (j + 1) * BLK, CHUNK):
                c = slice(k, k + CHUNK)
                p = s_scr[at, c] * to_p
                ds_scr[c, cols] = (p * (u_scr[at, c] + lift) - t_scr[at, c] * to_t).astype(BF)
                pb_scr[c, cols] = p.astype(BF)
        dq_t = jnp.dot(kcat_t, ds_scr[:, cols], preferred_element_type=F32) * scale
        dq2 = dq_t.T.astype(BF)
        dq_ref[:, ha * E:(ha + 1) * E] = dq2[:BLK]
        dq_ref[:, hb * E:(hb + 1) * E] = dq2[BLK:]
        if pair % 2 == 1 or pair + 1 == heads // 2:
            first_pair = pair - pair % 2
            cols = slice(first_pair * wide, (pair + 1) * wide)
            q_part = jnp.concatenate([rows_pair(q_ref, n) for n in range(first_pair, pair + 1)], axis=0)
            g_part = jnp.concatenate([rows_pair(g_ref, n) for n in range(first_pair, pair + 1)], axis=0)
            dk = dk + jnp.dot(ds_scr[:, cols], q_part, preferred_element_type=F32)
            dv = dv + jnp.dot(pb_scr[:, cols], g_part, preferred_element_type=F32)
    loss_ref[0] = loss[:, :BLK] + loss[:, BLK:]
    dk = dk * scale
    for d in range(WIN):
        part_k, part_v = dk[d * BLK:(d + 1) * BLK], dv[d * BLK:(d + 1) * BLK]
        if d in crossing:
            at = first + LEAD - d
            back_ref[0, at] = part_k
            back_ref[1, at] = part_v
        else:
            dk_ref[rows_of(d), :] += part_k
            dv_ref[rows_of(d), :] += part_v
    if crossing:
        untouched = [i for i in range(LEAD) if i not in [first + LEAD - d for d in crossing]]
        for i in untouched:
            back_ref[0, i] = jnp.zeros((BLK, E), F32)
            back_ref[1, i] = jnp.zeros((BLK, E), F32)
    for g, at in enumerate(sink_at):
        j = WIN + g
        dsk_ref[pl.ds(at, BLK), :] += dk[j * BLK:(j + 1) * BLK]
        dsv_ref[pl.ds(at, BLK), :] += dv[j * BLK:(j + 1) * BLK]


def pack_kernel(*refs):
    out = refs[-1]
    for i, ref in enumerate(refs[:-1]):
        out[i] = ref[...]


def pack(arrays):
    shape = arrays[0].shape
    return pl.pallas_call(
        pack_kernel,
        out_shape=jax.ShapeDtypeStruct((len(arrays), *shape), arrays[0].dtype),
        compiler_params=pltpu.CompilerParams(vmem_limit_bytes=16 * 1024 * 1024),
        name="pack",
    )(*arrays)


def finish_kernel(root_ref, dk_ref, dv_ref, dsk_ref, dsv_ref, back_ref, *rest):
    came, (kg_ref, vg_ref) = rest[:-2], rest[-2:]
    root = root_ref[0] == 0
    tokens = dk_ref.shape[0]
    for which, (own, sink, out) in enumerate(((dk_ref, dsk_ref, kg_ref), (dv_ref, dsv_ref, vg_ref))):
        for block in range(tokens // BLK):
            rows = slice(block * BLK, (block + 1) * BLK)
            value = own[rows]
            late = block - (tokens // BLK - LEAD)
            if late >= 0:
                value = value + back_ref[which, late].astype(F32)
            if block < NGLOB:
                extra = sink[rows]
                for arrived in came[which::2]:
                    extra = extra + arrived[rows].astype(F32)
                value = value + jnp.where(root, extra, 0.0)
            out[rows] = value.astype(BF)


def finish(root, dk, dv, dsk, dsv, back, came):
    vmem = pl.BlockSpec(memory_space=pltpu.VMEM)
    return pl.pallas_call(
        finish_kernel,
        out_shape=[jax.ShapeDtypeStruct(dk.shape, BF)] * 2,
        in_specs=[pl.BlockSpec(memory_space=pltpu.SMEM)] + [vmem] * (5 + len(came)),
        out_specs=[vmem] * 2,
        compiler_params=pltpu.CompilerParams(vmem_limit_bytes=16 * 1024 * 1024),
        name="finish",
    )(root, dk, dv, dsk, dsv, back, *came)


def run_blocks(first, count, base, picks, queries, out_grad, window, incoming, glob, own, sinks, weights,
               before, acc):
    crossing = [d for d in range(WIN) if d > first]
    assert not crossing or count == 1
    tokens, columns = queries.shape
    heads = window.shape[2]
    slots = WIN + picks.shape[1]
    tile = (1, 1, heads, BLK, BLK)
    whole = lambda i, *_: (0, 0)
    args = [queries, out_grad]
    specs = [pl.BlockSpec((BLK, columns), lambda i, *_: (first + i, 0))] * 2
    for d in range(WIN):
        if d in crossing:
            args.append(incoming[d])
            specs.append(pl.BlockSpec(tile, lambda i, *_: (0, 0, 0, 0, 0)))
        else:
            args.append(window)
            specs.append(pl.BlockSpec(tile, lambda i, *_, d=d: (first + i - d, d, 0, 0, 0)))
    for g in range(slots - WIN):
        args.append(glob)
        specs.append(pl.BlockSpec(tile, lambda i, *_, g=g: (first + i, g, 0, 0, 0)))
    for x in (*own, *sinks):
        args.append(x)
        specs.append(pl.BlockSpec(x.shape, whole))
    args.append(weights)
    specs.append(pl.BlockSpec((1, 1, BLK), lambda i, *_: (first + i, 0, 0)))
    if crossing:
        args.append(before)
        specs.append(pl.BlockSpec(before.shape, lambda i, *_: (0, 0, 0, 0)))
    chained = acc is not None
    acc_shapes = [(tokens, E)] * 2 + [(NGLOB * BLK, E)] * 2
    if chained:
        args.extend(acc)
        specs.extend(pl.BlockSpec(s, whole) for s in acc_shapes)
    outs = [
        jax.ShapeDtypeStruct((count * BLK, columns), BF),
        jax.ShapeDtypeStruct((count, 1, BLK), F32),
    ] + [jax.ShapeDtypeStruct(s, F32) for s in acc_shapes]
    out_specs = [
        pl.BlockSpec((BLK, columns), lambda i, *_: (i, 0)),
        pl.BlockSpec((1, 1, BLK), lambda i, *_: (i, 0, 0)),
    ] + [pl.BlockSpec(s, whole) for s in acc_shapes]
    if crossing:
        back = (2, LEAD, BLK, E)
        outs.append(jax.ShapeDtypeStruct(back, F32))
        out_specs.append(pl.BlockSpec(back, lambda i, *_: (0, 0, 0, 0)))
    elements = count * slots * heads * BLK * BLK
    return pl.pallas_call(
        functools.partial(block_kernel, first, crossing, slots, chained),
        out_shape=outs,
        grid_spec=pltpu.PrefetchScalarGridSpec(
            num_scalar_prefetch=2,
            grid=(count,),
            in_specs=specs,
            out_specs=out_specs,
            scratch_shapes=[pltpu.VMEM((slots * BLK, heads * BLK), BF)] * 2
            + [pltpu.VMEM((2, slots * BLK, 2 * BLK), F32)] * 3,
        ),
        compiler_params=pltpu.CompilerParams(vmem_limit_bytes=48 * 1024 * 1024),
        cost_estimate=pl.CostEstimate(
            flops=elements * E * 10, bytes_accessed=elements * 3, transcendentals=2 * elements
        ),
        name=f"blocks_from_{first}",
    )(base, picks, *args)


def local(queries, key_rows, values, out_grad, teacher_window, teacher_global, global_picks, mix_weight):
    tokens, columns = queries.shape
    blocks = tokens // BLK
    assert key_rows.shape[1] == E and blocks >= NGLOB
    where = lax.axis_index("seq")
    count = lax.axis_size("seq")
    base = (where * blocks).astype(jnp.int32).reshape(1)
    weights = mix_weight.reshape(blocks, 1, BLK)

    tail = slice(tokens - LEAD * BLK, tokens)
    first_rows = slice(0, NGLOB * BLK)
    pair = pack([key_rows, values])
    got = shift(pair, "seq", 1)
    before = got[:, tail].reshape(2, LEAD, BLK, E)
    sinks = jnp.where(where == 0, pair[:, first_rows], got[:, first_rows])
    span, known = 1, pair[:, first_rows]
    while span < count:
        for times in range(1, FAN):
            if span == 1 and times == 1:
                continue
            route = [(i, i + times * span) for i in range(span) if i + times * span < count]
            if route:
                more = lax.ppermute(known, "seq", route)
                sinks = jnp.where((where >= times * span) & (where < (times + 1) * span), more, sinks)
        span *= FAN
        known = sinks

    incoming = {}
    for block in range(LEAD - 1, -1, -1):
        offsets = list(range(block + 1, WIN))
        out = jnp.concatenate(
            [teacher_window[blocks + block - d:blocks + block - d + 1, d:d + 1] for d in offsets], axis=0
        )
        came = shift(out, "seq", 1)
        incoming[block] = {d: came[i:i + 1] for i, d in enumerate(offsets)}

    own = (key_rows, values)
    sink_arrays = (sinks[0], sinks[1])
    run = lambda first, n, acc: run_blocks(
        first, n, base, global_picks, queries, out_grad, teacher_window, incoming.get(first),
        teacher_global, own, sink_arrays, weights, before, acc,
    )
    dq, loss = {}, {}
    dq[LEAD], loss[LEAD], *acc = run(LEAD, blocks - LEAD, None)
    back = 0.0
    for block in range(LEAD - 1, -1, -1):
        dq[block], loss[block], *rest = run(block, 1, acc)
        acc, part = rest[:4], rest[4]
        back = back + part
    order = sorted(dq)
    query_grad = jnp.concatenate([dq[i] for i in order], axis=0)
    row_terms = jnp.concatenate([loss[i] for i in order], axis=0).reshape(tokens)

    dk, dv, dsk, dsv = acc
    sums = [dsk, dsv]
    steps = []
    reach = 1
    while reach < count:
        steps.append([(i, i - reach) for i in range(reach, count, 2 * reach)])
        reach *= 2
    returned = None
    arrived = []
    for number, route in enumerate(steps):
        low = [x.astype(BF) for x in sums]
        came = [lax.ppermute(x, "seq", route) for x in low]
        if number == 0:
            returned = shift(back.astype(BF), "seq", -1)
        sums = [x + y.astype(F32) for x, y in zip(sums, came)]
        arrived += came
    row_terms, returned = lax.optimization_barrier((row_terms, returned))
    row_loss = sum_over(sum_over(row_terms, "grp"), "head")
    root = where.astype(jnp.int32).reshape(1)
    grads = finish(root, dk, dv, dsk, dsv, returned, arrived)
    return (query_grad, grads[0], grads[1], row_loss)


def solution(mesh):
    heads = ("grp", "head")
    placed = (
        P("seq", heads),
        P("seq", heads),
        P("seq", heads),
        P("seq", heads),
        P("seq", None, heads, None, None),
        P("seq", None, heads, None, None),
        P("seq", None),
        P("seq"),
    )
    return jax.shard_map(
        local,
        mesh=mesh,
        in_specs=placed,
        out_specs=(P("seq", heads), P("seq", heads), P("seq", heads), P("seq")),
        check_vma=False,
    )
```

```python
import functools
import math

import jax
import jax.numpy as jnp
from jax import lax
from jax.experimental import pallas as pl
from jax.experimental.pallas import tpu as pltpu
from jax.sharding import PartitionSpec as P

E = 128
BLK = 128
WIN = 3
NGLOB = 4
LEAD = WIN - 1
FAN = 4
CHUNK = 32
LOG2E = math.log2(math.e)
LN2 = math.log(2.0)
NT = (((1,), (1,)), ((), ()))
BF = jnp.bfloat16
F32 = jnp.float32


def shift(block, axis, distance):
    count = lax.axis_size(axis)
    route = [(i, i + distance) for i in range(count) if 0 <= i + distance < count]
    return lax.ppermute(block, axis, route)


def sum_over(block, axis):
    count = lax.axis_size(axis)
    if count & (count - 1):
        return lax.psum(block, axis)
    step = 1
    while step < count:
        block = block + lax.ppermute(block, axis, [(i, i ^ step) for i in range(count)])
        step *= 2
    return block


def block_kernel(
    first, crossing, slots, chained,
    base_ref, picks_ref, q_ref, g_ref, *rest,
):
    teacher_refs = rest[:slots]
    rest = rest[slots:]
    own_k, own_v, sink_k, sink_v, w_ref = rest[:5]
    rest = rest[5:]
    if crossing:
        before_ref, rest = rest[0], rest[1:]
    if chained:
        acc_in, rest = rest[:4], rest[4:]
    dq_ref, loss_ref, dk_ref, dv_ref, dsk_ref, dsv_ref = rest[:6]
    rest = rest[6:]
    if crossing:
        back_ref, rest = rest[0], rest[1:]
    ds_scr, pb_scr, s_scr, t_scr, u_scr = rest
    step = pl.program_id(0)
    block = first + step
    heads = q_ref.shape[1] // E
    scale = 1.0 / math.sqrt(E)
    factor = scale * LOG2E

    @pl.when(step == 0)
    def _():
        if chained:
            for out, given in zip((dk_ref, dv_ref, dsk_ref, dsv_ref), acc_in):
                out[...] = given[...]
        else:
            for out in (dk_ref, dv_ref, dsk_ref, dsv_ref):
                out[...] = jnp.zeros_like(out)

    picks = [picks_ref[block, g] for g in range(slots - WIN)]
    live = [None] + [base_ref[0] + block - d >= 0 for d in range(1, WIN)] + [p >= 0 for p in picks]
    sink_at = [pl.multiple_of(jnp.maximum(p, 0) * BLK, BLK) for p in picks]

    def rows_of(d):
        return pl.ds(pl.multiple_of((block - d) * BLK, BLK), BLK)

    keys, vals = [], []
    for d in range(WIN):
        if d in crossing:
            at = first + LEAD - d
            keys.append(before_ref[0, at])
            vals.append(before_ref[1, at])
        else:
            keys.append(own_k[rows_of(d), :])
            vals.append(own_v[rows_of(d), :])
    for at in sink_at:
        keys.append(sink_k[pl.ds(at, BLK), :])
        vals.append(sink_v[pl.ds(at, BLK), :])
    kcat = jnp.concatenate(keys, axis=0)
    vcat = jnp.concatenate(vals, axis=0)
    kcat_t = kcat.T

    w1 = w_ref[0]
    w2 = jnp.concatenate([w1, w1], axis=1)
    slope = (w2 - 1.0) * LN2
    wide = 2 * BLK
    key_id = lax.broadcasted_iota(jnp.int32, (BLK, wide), 0)
    row_id = lax.broadcasted_iota(jnp.int32, (BLK, wide), 1) & (BLK - 1)
    causal = key_id <= row_id
    low = jnp.float32(-1e9)
    loss = jnp.zeros((1, wide), F32)

    def rows_pair(ref, pair):
        ha, hb = 2 * pair, 2 * pair + 1
        return jnp.concatenate([ref[:, ha * E:(ha + 1) * E], ref[:, hb * E:(hb + 1) * E]], axis=0)

    def products(pair):
        at = pair % 2
        s_scr[at] = lax.dot_general(kcat, rows_pair(q_ref, pair), NT, preferred_element_type=F32)
        u_scr[at] = lax.dot_general(vcat, rows_pair(g_ref, pair), NT, preferred_element_type=F32)

    def fold(x, op):
        return functools.reduce(op, [x[i:i + 8] for i in range(0, CHUNK, 8)])

    def up(x):
        return jnp.sum(x, axis=0, keepdims=True)

    products(0)
    dk = dv = 0.0
    for pair in range(heads // 2):
        at = pair % 2
        if pair + 1 < heads // 2:
            products(pair + 1)
        ha, hb = 2 * pair, 2 * pair + 1
        stats = []
        for j in range(slots):
            tile = slice(j * BLK, (j + 1) * BLK)
            t = jnp.concatenate([teacher_refs[j][0, 0, ha], teacher_refs[j][0, 0, hb]], axis=0)
            t = t.T.astype(F32)
            if j == 0:
                t = jnp.where(causal, t, low)
                s_scr[at, tile] = jnp.where(causal, s_scr[at, tile], low)
            t_scr[at, tile] = t
            chunks = [slice(k, k + CHUNK) for k in range(j * BLK, (j + 1) * BLK, CHUNK)]
            m = functools.reduce(jnp.maximum, [fold(s_scr[at, c], jnp.maximum) for c in chunks])
            mt = functools.reduce(jnp.maximum, [fold(t_scr[at, c], jnp.maximum) for c in chunks])
            m = jnp.max(m, axis=0, keepdims=True)
            mt = jnp.max(mt, axis=0, keepdims=True)
            sums = None
            for c in chunks:
                x = (s_scr[at, c] - m) * factor
                y = (t_scr[at, c] - mt) * LOG2E
                es = jnp.exp2(x)
                et = jnp.exp2(y)
                gap = y - x
                u = u_scr[at, c] + slope * gap
                part = [fold(v, jnp.add) for v in (es, et, et * gap, es * gap, es * u)]
                sums = part if sums is None else [v + w for v, w in zip(sums, part)]
                s_scr[at, c] = es
                t_scr[at, c] = et
                u_scr[at, c] = u
            stats.append((m, mt, *[up(v) for v in sums]))
        m = stats[0][0]
        mt = stats[0][1]
        for j in range(1, slots):
            m = jnp.maximum(m, jnp.where(live[j], stats[j][0], low))
            mt = jnp.maximum(mt, jnp.where(live[j], stats[j][1], low))
        a = [(st[0] - m) * factor for st in stats]
        b = [(st[1] - mt) * LOG2E for st in stats]
        fa = [jnp.exp2(v) for v in a]
        fb = [jnp.exp2(v) for v in b]
        for j in range(1, slots):
            fa[j] = jnp.where(live[j], fa[j], 0.0)
            fb[j] = jnp.where(live[j], fb[j], 0.0)
        z = functools.reduce(jnp.add, [f * st[2] for f, st in zip(fa, stats)])
        zt = functools.reduce(jnp.add, [f * st[3] for f, st in zip(fb, stats)])
        rz, rzt = 1.0 / z, 1.0 / zt
        both = jnp.log2(z) - jnp.log2(zt)
        off = [vb - va + both for va, vb in zip(a, b)]
        fwd = functools.reduce(jnp.add, [f * (st[4] + o * st[3]) for f, o, st in zip(fb, off, stats)])
        rev = functools.reduce(jnp.add, [f * (st[5] + o * st[2]) for f, o, st in zip(fa, off, stats)])
        mean_u = functools.reduce(
            jnp.add, [f * (st[6] + slope * o * st[2]) for f, o, st in zip(fa, off, stats)]
        )
        loss = loss + (w2 * LN2) * (rzt * fwd) + slope * (rz * rev)
        base = w2 - rz * mean_u
        cols = slice(pair * wide, (pair + 1) * wide)
        for j in range(slots):
            to_p = fa[j] * rz
            to_t = w2 * (fb[j] * rzt)
            lift = base + slope * off[j]
            for k in range(j * BLK, (j + 1) * BLK, CHUNK):
                c = slice(k, k + CHUNK)
                p = s_scr[at, c] * to_p
                ds_scr[c, cols] = (p * (u_scr[at, c] + lift) - t_scr[at, c] * to_t).astype(BF)
                pb_scr[c, cols] = p.astype(BF)
        dq_t = jnp.dot(kcat_t, ds_scr[:, cols], preferred_element_type=F32) * scale
        dq2 = dq_t.T.astype(BF)
        dq_ref[:, ha * E:(ha + 1) * E] = dq2[:BLK]
        dq_ref[:, hb * E:(hb + 1) * E] = dq2[BLK:]
        if pair % 2 == 1 or pair + 1 == heads // 2:
            first_pair = pair - pair % 2
            cols = slice(first_pair * wide, (pair + 1) * wide)
            q_part = jnp.concatenate([rows_pair(q_ref, n) for n in range(first_pair, pair + 1)], axis=0)
            g_part = jnp.concatenate([rows_pair(g_ref, n) for n in range(first_pair, pair + 1)], axis=0)
            dk = dk + jnp.dot(ds_scr[:, cols], q_part, preferred_element_type=F32)
            dv = dv + jnp.dot(pb_scr[:, cols], g_part, preferred_element_type=F32)
    loss_ref[0] = loss[:, :BLK] + loss[:, BLK:]
    dk = dk * scale
    for d in range(WIN):
        part_k, part_v = dk[d * BLK:(d + 1) * BLK], dv[d * BLK:(d + 1) * BLK]
        if d in crossing:
            at = first + LEAD - d
            back_ref[0, at] = part_k
            back_ref[1, at] = part_v
        else:
            dk_ref[rows_of(d), :] += part_k
            dv_ref[rows_of(d), :] += part_v
    if crossing:
        untouched = [i for i in range(LEAD) if i not in [first + LEAD - d for d in crossing]]
        for i in untouched:
            back_ref[0, i] = jnp.zeros((BLK, E), F32)
            back_ref[1, i] = jnp.zeros((BLK, E), F32)
    for g, at in enumerate(sink_at):
        j = WIN + g
        dsk_ref[pl.ds(at, BLK), :] += dk[j * BLK:(j + 1) * BLK]
        dsv_ref[pl.ds(at, BLK), :] += dv[j * BLK:(j + 1) * BLK]


def pack_kernel(*refs):
    out = refs[-1]
    for i, ref in enumerate(refs[:-1]):
        out[i] = ref[...]


def pack(arrays):
    shape = arrays[0].shape
    return pl.pallas_call(
        pack_kernel,
        out_shape=jax.ShapeDtypeStruct((len(arrays), *shape), arrays[0].dtype),
        compiler_params=pltpu.CompilerParams(vmem_limit_bytes=16 * 1024 * 1024),
        name="pack",
    )(*arrays)


def finish_kernel(root_ref, dk_ref, dv_ref, dsk_ref, dsv_ref, back_ref, *rest):
    came, (kg_ref, vg_ref) = rest[:-2], rest[-2:]
    root = root_ref[0] == 0
    tokens = dk_ref.shape[0]
    for which, (own, sink, out) in enumerate(((dk_ref, dsk_ref, kg_ref), (dv_ref, dsv_ref, vg_ref))):
        for block in range(tokens // BLK):
            rows = slice(block * BLK, (block + 1) * BLK)
            value = own[rows]
            late = block - (tokens // BLK - LEAD)
            if late >= 0:
                value = value + back_ref[which, late].astype(F32)
            if block < NGLOB:
                extra = sink[rows]
                for arrived in came[which::2]:
                    extra = extra + arrived[rows].astype(F32)
                value = value + jnp.where(root, extra, 0.0)
            out[rows] = value.astype(BF)


def finish(root, dk, dv, dsk, dsv, back, came):
    vmem = pl.BlockSpec(memory_space=pltpu.VMEM)
    return pl.pallas_call(
        finish_kernel,
        out_shape=[jax.ShapeDtypeStruct(dk.shape, BF)] * 2,
        in_specs=[pl.BlockSpec(memory_space=pltpu.SMEM)] + [vmem] * (5 + len(came)),
        out_specs=[vmem] * 2,
        compiler_params=pltpu.CompilerParams(vmem_limit_bytes=16 * 1024 * 1024),
        name="finish",
    )(root, dk, dv, dsk, dsv, back, *came)


def run_blocks(first, count, base, picks, queries, out_grad, window, incoming, glob, own, sinks, weights,
               before, acc):
    crossing = [d for d in range(WIN) if d > first]
    assert not crossing or count == 1
    tokens, columns = queries.shape
    heads = window.shape[2]
    slots = WIN + picks.shape[1]
    tile = (1, 1, heads, BLK, BLK)
    whole = lambda i, *_: (0, 0)
    args = [queries, out_grad]
    specs = [pl.BlockSpec((BLK, columns), lambda i, *_: (first + i, 0))] * 2
    for d in range(WIN):
        if d in crossing:
            args.append(incoming)
            specs.append(pl.BlockSpec(tile, lambda i, *_, d=d: (crossing.index(d), 0, 0, 0, 0)))
        else:
            args.append(window)
            specs.append(pl.BlockSpec(tile, lambda i, *_, d=d: (first + i - d, d, 0, 0, 0)))
    for g in range(slots - WIN):
        args.append(glob)
        specs.append(pl.BlockSpec(tile, lambda i, *_, g=g: (first + i, g, 0, 0, 0)))
    for x in (*own, *sinks):
        args.append(x)
        specs.append(pl.BlockSpec(x.shape, whole))
    args.append(weights)
    specs.append(pl.BlockSpec((1, 1, BLK), lambda i, *_: (first + i, 0, 0)))
    if crossing:
        args.append(before)
        specs.append(pl.BlockSpec(before.shape, lambda i, *_: (0, 0, 0, 0)))
    chained = acc is not None
    acc_shapes = [(tokens, E)] * 2 + [(NGLOB * BLK, E)] * 2
    if chained:
        args.extend(acc)
        specs.extend(pl.BlockSpec(s, whole) for s in acc_shapes)
    outs = [
        jax.ShapeDtypeStruct((count * BLK, columns), BF),
        jax.ShapeDtypeStruct((count, 1, BLK), F32),
    ] + [jax.ShapeDtypeStruct(s, F32) for s in acc_shapes]
    out_specs = [
        pl.BlockSpec((BLK, columns), lambda i, *_: (i, 0)),
        pl.BlockSpec((1, 1, BLK), lambda i, *_: (i, 0, 0)),
    ] + [pl.BlockSpec(s, whole) for s in acc_shapes]
    if crossing:
        back = (2, LEAD, BLK, E)
        outs.append(jax.ShapeDtypeStruct(back, F32))
        out_specs.append(pl.BlockSpec(back, lambda i, *_: (0, 0, 0, 0)))
    elements = count * slots * heads * BLK * BLK
    return pl.pallas_call(
        functools.partial(block_kernel, first, crossing, slots, chained),
        out_shape=outs,
        grid_spec=pltpu.PrefetchScalarGridSpec(
            num_scalar_prefetch=2,
            grid=(count,),
            in_specs=specs,
            out_specs=out_specs,
            scratch_shapes=[pltpu.VMEM((slots * BLK, heads * BLK), BF)] * 2
            + [pltpu.VMEM((2, slots * BLK, 2 * BLK), F32)] * 3,
        ),
        compiler_params=pltpu.CompilerParams(vmem_limit_bytes=48 * 1024 * 1024),
        cost_estimate=pl.CostEstimate(
            flops=elements * E * 10, bytes_accessed=elements * 3, transcendentals=2 * elements
        ),
        name=f"blocks_from_{first}",
    )(base, picks, *args)


def local(queries, key_rows, values, out_grad, teacher_window, teacher_global, global_picks, mix_weight):
    tokens, columns = queries.shape
    blocks = tokens // BLK
    assert key_rows.shape[1] == E and blocks >= NGLOB
    where = lax.axis_index("seq")
    count = lax.axis_size("seq")
    base = (where * blocks).astype(jnp.int32).reshape(1)
    weights = mix_weight.reshape(blocks, 1, BLK)

    tail = slice(tokens - LEAD * BLK, tokens)
    first_rows = slice(0, NGLOB * BLK)
    pair = pack([key_rows, values])
    half = 1
    while 2 * half < count:
        half *= 2
    sinks = pair[:, first_rows]
    known, later = [0], None
    while half > 1:
        came = lax.ppermute(sinks, "seq", [(i, i + half) for i in known if i + half < count])
        sinks = jnp.where(where % (2 * half) == half, came, sinks)
        known = sorted(known + [i + half for i in known if i + half < count])
        half //= 2
    got = shift(pair, "seq", 1)
    before = got[:, tail].reshape(2, LEAD, BLK, E)
    forward = [(i, i + 1) for i in known if i > 0 and i + 1 < count]
    if forward:
        came = lax.ppermute(sinks, "seq", forward)
        later = sinks
        sinks = jnp.where(where % 2 == 1, came, sinks)
    sinks = jnp.where(where == 1, got[:, first_rows], sinks)

    incoming = {}
    for block in range(LEAD - 1, -1, -1):
        out = jnp.concatenate(
            [teacher_window[blocks + block - d:blocks + block - d + 1, d:d + 1] for d in range(block + 1, WIN)],
            axis=0,
        )
        if block == 0 and later is not None:
            out, _ = lax.optimization_barrier((out, later))
        incoming[block] = shift(out, "seq", 1)

    own = (key_rows, values)
    sink_arrays = (sinks[0], sinks[1])
    run = lambda first, n, acc: run_blocks(
        first, n, base, global_picks, queries, out_grad, teacher_window, incoming.get(first),
        teacher_global, own, sink_arrays, weights, before, acc,
    )
    dq, loss = {}, {}
    dq[LEAD], loss[LEAD], *acc = run(LEAD, blocks - LEAD, None)
    back = 0.0
    for block in range(LEAD - 1, -1, -1):
        dq[block], loss[block], *rest = run(block, 1, acc)
        acc, part = rest[:4], rest[4]
        back = back + part
    order = sorted(dq)
    query_grad = jnp.concatenate([dq[i] for i in order], axis=0)
    row_terms = jnp.concatenate([loss[i] for i in order], axis=0).reshape(tokens)

    dk, dv, dsk, dsv = acc
    sums = [dsk, dsv]
    steps = []
    reach = 1
    while reach < count:
        steps.append([(i, i - reach) for i in range(reach, count, 2 * reach)])
        reach *= 2
    returned = None
    arrived = []
    for number, route in enumerate(steps):
        low = [x.astype(BF) for x in sums]
        came = [lax.ppermute(x, "seq", route) for x in low]
        if number == 0:
            returned = shift(back.astype(BF), "seq", -1)
        sums = [x + y.astype(F32) for x, y in zip(sums, came)]
        arrived += came
    row_terms, returned = lax.optimization_barrier((row_terms, returned))
    row_loss = sum_over(sum_over(row_terms, "grp"), "head")
    root = where.astype(jnp.int32).reshape(1)
    grads = finish(root, dk, dv, dsk, dsv, returned, arrived)
    return (query_grad, grads[0], grads[1], row_loss)


def solution(mesh):
    heads = ("grp", "head")
    placed = (
        P("seq", heads),
        P("seq", heads),
        P("seq", heads),
        P("seq", heads),
        P("seq", None, heads, None, None),
        P("seq", None, heads, None, None),
        P("seq", None),
        P("seq"),
    )
    return jax.shard_map(
        local,
        mesh=mesh,
        in_specs=placed,
        out_specs=(P("seq", heads), P("seq", heads), P("seq", heads), P("seq")),
        check_vma=False,
    )
```

```python
import functools
import math

import jax
import jax.numpy as jnp
from jax import lax
from jax.experimental import pallas as pl
from jax.experimental.pallas import tpu as pltpu
from jax.sharding import PartitionSpec as P

E = 128
BLK = 128
WIN = 3
NGLOB = 4
LEAD = WIN - 1
FAN = 4
CHUNK = 32
LOG2E = math.log2(math.e)
LN2 = math.log(2.0)
NT = (((1,), (1,)), ((), ()))
BF = jnp.bfloat16
F32 = jnp.float32


def shift(block, axis, distance):
    count = lax.axis_size(axis)
    route = [(i, i + distance) for i in range(count) if 0 <= i + distance < count]
    return lax.ppermute(block, axis, route)


def sum_over(block, axis):
    count = lax.axis_size(axis)
    if count & (count - 1):
        return lax.psum(block, axis)
    step = 1
    while step < count:
        block = block + lax.ppermute(block, axis, [(i, i ^ step) for i in range(count)])
        step *= 2
    return block


def block_kernel(
    first, crossing, slots, chained,
    base_ref, picks_ref, q_ref, g_ref, *rest,
):
    teacher_refs = rest[:slots]
    rest = rest[slots:]
    own_k, own_v, sink_k, sink_v, w_ref = rest[:5]
    rest = rest[5:]
    if crossing:
        before_ref, rest = rest[0], rest[1:]
    if chained:
        acc_in, rest = rest[:4], rest[4:]
    dq_ref, loss_ref, dk_ref, dv_ref, dsk_ref, dsv_ref = rest[:6]
    rest = rest[6:]
    if crossing:
        back_ref, rest = rest[0], rest[1:]
    ds_scr, pb_scr, s_scr, t_scr, u_scr = rest
    step = pl.program_id(0)
    block = first + step
    heads = q_ref.shape[1] // E
    scale = 1.0 / math.sqrt(E)
    factor = scale * LOG2E

    @pl.when(step == 0)
    def _():
        if chained:
            for out, given in zip((dk_ref, dv_ref, dsk_ref, dsv_ref), acc_in):
                out[...] = given[...]
        else:
            for out in (dk_ref, dv_ref, dsk_ref, dsv_ref):
                out[...] = jnp.zeros_like(out)

    picks = [picks_ref[block, g] for g in range(slots - WIN)]
    live = [None] + [base_ref[0] + block - d >= 0 for d in range(1, WIN)] + [p >= 0 for p in picks]
    sink_at = [pl.multiple_of(jnp.maximum(p, 0) * BLK, BLK) for p in picks]

    def rows_of(d):
        return pl.ds(pl.multiple_of((block - d) * BLK, BLK), BLK)

    keys, vals = [], []
    for d in range(WIN):
        if d in crossing:
            at = first + LEAD - d
            keys.append(before_ref[0, at])
            vals.append(before_ref[1, at])
        else:
            keys.append(own_k[rows_of(d), :])
            vals.append(own_v[rows_of(d), :])
    for at in sink_at:
        keys.append(sink_k[pl.ds(at, BLK), :])
        vals.append(sink_v[pl.ds(at, BLK), :])
    kcat = jnp.concatenate(keys, axis=0)
    vcat = jnp.concatenate(vals, axis=0)
    kcat_t = kcat.T

    w1 = w_ref[0]
    w2 = jnp.concatenate([w1, w1], axis=1)
    slope = (w2 - 1.0) * LN2
    wide = 2 * BLK
    key_id = lax.broadcasted_iota(jnp.int32, (BLK, wide), 0)
    row_id = lax.broadcasted_iota(jnp.int32, (BLK, wide), 1) & (BLK - 1)
    causal = key_id <= row_id
    low = jnp.float32(-1e9)
    loss = jnp.zeros((1, wide), F32)

    def rows_pair(ref, pair):
        ha, hb = 2 * pair, 2 * pair + 1
        return jnp.concatenate([ref[:, ha * E:(ha + 1) * E], ref[:, hb * E:(hb + 1) * E]], axis=0)

    def products(pair):
        at = pair % 2
        s_scr[at] = lax.dot_general(kcat, rows_pair(q_ref, pair), NT, preferred_element_type=F32)
        u_scr[at] = lax.dot_general(vcat, rows_pair(g_ref, pair), NT, preferred_element_type=F32)

    def fold(x, op):
        return functools.reduce(op, [x[i:i + 8] for i in range(0, CHUNK, 8)])

    def up(x):
        return jnp.sum(x, axis=0, keepdims=True)

    products(0)
    dk = dv = 0.0
    for pair in range(heads // 2):
        at = pair % 2
        if pair + 1 < heads // 2:
            products(pair + 1)
        ha, hb = 2 * pair, 2 * pair + 1
        stats = []
        for j in range(slots):
            tile = slice(j * BLK, (j + 1) * BLK)
            t = jnp.concatenate([teacher_refs[j][0, 0, ha], teacher_refs[j][0, 0, hb]], axis=0)
            t = t.T.astype(F32)
            if j == 0:
                t = jnp.where(causal, t, low)
                s_scr[at, tile] = jnp.where(causal, s_scr[at, tile], low)
            t_scr[at, tile] = t
            chunks = [slice(k, k + CHUNK) for k in range(j * BLK, (j + 1) * BLK, CHUNK)]
            m = functools.reduce(jnp.maximum, [fold(s_scr[at, c], jnp.maximum) for c in chunks])
            mt = functools.reduce(jnp.maximum, [fold(t_scr[at, c], jnp.maximum) for c in chunks])
            m = jnp.max(m, axis=0, keepdims=True)
            mt = jnp.max(mt, axis=0, keepdims=True)
            sums = None
            for c in chunks:
                x = (s_scr[at, c] - m) * factor
                y = (t_scr[at, c] - mt) * LOG2E
                es = jnp.exp2(x)
                et = jnp.exp2(y)
                gap = y - x
                u = u_scr[at, c] + slope * gap
                part = [fold(v, jnp.add) for v in (es, et, et * gap, es * gap, es * u)]
                sums = part if sums is None else [v + w for v, w in zip(sums, part)]
                s_scr[at, c] = es
                t_scr[at, c] = et
                u_scr[at, c] = u
            stats.append((m, mt, *[up(v) for v in sums]))
        m = stats[0][0]
        mt = stats[0][1]
        for j in range(1, slots):
            m = jnp.maximum(m, jnp.where(live[j], stats[j][0], low))
            mt = jnp.maximum(mt, jnp.where(live[j], stats[j][1], low))
        a = [(st[0] - m) * factor for st in stats]
        b = [(st[1] - mt) * LOG2E for st in stats]
        fa = [jnp.exp2(v) for v in a]
        fb = [jnp.exp2(v) for v in b]
        for j in range(1, slots):
            fa[j] = jnp.where(live[j], fa[j], 0.0)
            fb[j] = jnp.where(live[j], fb[j], 0.0)
        z = functools.reduce(jnp.add, [f * st[2] for f, st in zip(fa, stats)])
        zt = functools.reduce(jnp.add, [f * st[3] for f, st in zip(fb, stats)])
        rz, rzt = 1.0 / z, 1.0 / zt
        both = jnp.log2(z) - jnp.log2(zt)
        off = [vb - va + both for va, vb in zip(a, b)]
        fwd = functools.reduce(jnp.add, [f * (st[4] + o * st[3]) for f, o, st in zip(fb, off, stats)])
        rev = functools.reduce(jnp.add, [f * (st[5] + o * st[2]) for f, o, st in zip(fa, off, stats)])
        mean_u = functools.reduce(
            jnp.add, [f * (st[6] + slope * o * st[2]) for f, o, st in zip(fa, off, stats)]
        )
        loss = loss + (w2 * LN2) * (rzt * fwd) + slope * (rz * rev)
        base = w2 - rz * mean_u
        cols = slice(pair * wide, (pair + 1) * wide)
        for j in range(slots):
            to_p = fa[j] * rz
            to_t = w2 * (fb[j] * rzt)
            lift = base + slope * off[j]
            for k in range(j * BLK, (j + 1) * BLK, CHUNK):
                c = slice(k, k + CHUNK)
                p = s_scr[at, c] * to_p
                ds_scr[c, cols] = (p * (u_scr[at, c] + lift) - t_scr[at, c] * to_t).astype(BF)
                pb_scr[c, cols] = p.astype(BF)
        dq_t = jnp.dot(kcat_t, ds_scr[:, cols], preferred_element_type=F32) * scale
        dq2 = dq_t.T.astype(BF)
        dq_ref[:, ha * E:(ha + 1) * E] = dq2[:BLK]
        dq_ref[:, hb * E:(hb + 1) * E] = dq2[BLK:]
        if pair % 2 == 1 or pair + 1 == heads // 2:
            first_pair = pair - pair % 2
            cols = slice(first_pair * wide, (pair + 1) * wide)
            q_part = jnp.concatenate([rows_pair(q_ref, n) for n in range(first_pair, pair + 1)], axis=0)
            g_part = jnp.concatenate([rows_pair(g_ref, n) for n in range(first_pair, pair + 1)], axis=0)
            dk = dk + jnp.dot(ds_scr[:, cols], q_part, preferred_element_type=F32)
            dv = dv + jnp.dot(pb_scr[:, cols], g_part, preferred_element_type=F32)
    loss_ref[0] = loss[:, :BLK] + loss[:, BLK:]
    dk = dk * scale
    for d in range(WIN):
        part_k, part_v = dk[d * BLK:(d + 1) * BLK], dv[d * BLK:(d + 1) * BLK]
        if d in crossing:
            at = first + LEAD - d
            back_ref[0, at] = part_k
            back_ref[1, at] = part_v
        else:
            dk_ref[rows_of(d), :] += part_k
            dv_ref[rows_of(d), :] += part_v
    if crossing:
        untouched = [i for i in range(LEAD) if i not in [first + LEAD - d for d in crossing]]
        for i in untouched:
            back_ref[0, i] = jnp.zeros((BLK, E), F32)
            back_ref[1, i] = jnp.zeros((BLK, E), F32)
    for g, at in enumerate(sink_at):
        j = WIN + g
        dsk_ref[pl.ds(at, BLK), :] += dk[j * BLK:(j + 1) * BLK]
        dsv_ref[pl.ds(at, BLK), :] += dv[j * BLK:(j + 1) * BLK]


def pack_kernel(key_ref, value_ref, tile_ref, pair_ref, all_ref):
    blocks = key_ref.shape[0] // BLK
    pair_ref[0] = key_ref[...]
    pair_ref[1] = value_ref[...]
    for i in range(blocks):
        rows = slice(i * BLK, (i + 1) * BLK)
        all_ref[i] = key_ref[rows]
        all_ref[blocks + i] = value_ref[rows]
    for h in range(tile_ref.shape[2]):
        all_ref[2 * blocks + h] = tile_ref[0, 0, h]


def pack(keys, vals, window):
    tokens = keys.shape[0]
    blocks, heads = tokens // BLK, window.shape[2]
    flat = pl.BlockSpec((tokens, E), lambda i: (0, 0))
    shapes = [(2, tokens, E), (2 * blocks + heads, BLK, BLK)]
    return pl.pallas_call(
        pack_kernel,
        out_shape=[jax.ShapeDtypeStruct(x, BF) for x in shapes],
        grid=(1,),
        in_specs=[flat, flat, pl.BlockSpec((1, 1, heads, BLK, BLK), lambda i: (blocks - 1, WIN - 1, 0, 0, 0))],
        out_specs=[pl.BlockSpec(x, lambda i: (0, 0, 0)) for x in shapes],
        compiler_params=pltpu.CompilerParams(vmem_limit_bytes=16 * 1024 * 1024),
        name="pack",
    )(keys, vals, window)


def finish_kernel(root_ref, dk_ref, dv_ref, dsk_ref, dsv_ref, back_ref, *rest):
    came, (kg_ref, vg_ref) = rest[:-2], rest[-2:]
    root = root_ref[0] == 0
    tokens = dk_ref.shape[0]
    for which, (own, sink, out) in enumerate(((dk_ref, dsk_ref, kg_ref), (dv_ref, dsv_ref, vg_ref))):
        for block in range(tokens // BLK):
            rows = slice(block * BLK, (block + 1) * BLK)
            value = own[rows]
            late = block - (tokens // BLK - LEAD)
            if late >= 0:
                value = value + back_ref[which, late].astype(F32)
            if block < NGLOB:
                extra = sink[rows]
                for arrived in came[which::2]:
                    extra = extra + arrived[rows].astype(F32)
                value = value + jnp.where(root, extra, 0.0)
            out[rows] = value.astype(BF)


def finish(root, dk, dv, dsk, dsv, back, came):
    vmem = pl.BlockSpec(memory_space=pltpu.VMEM)
    return pl.pallas_call(
        finish_kernel,
        out_shape=[jax.ShapeDtypeStruct(dk.shape, BF)] * 2,
        in_specs=[pl.BlockSpec(memory_space=pltpu.SMEM)] + [vmem] * (5 + len(came)),
        out_specs=[vmem] * 2,
        compiler_params=pltpu.CompilerParams(vmem_limit_bytes=16 * 1024 * 1024),
        name="finish",
    )(root, dk, dv, dsk, dsv, back, *came)


def run_blocks(first, count, base, picks, queries, out_grad, window, incoming, glob, own, sinks, weights,
               before, acc):
    crossing = [d for d in range(WIN) if d > first]
    assert not crossing or count == 1
    tokens, columns = queries.shape
    heads = window.shape[2]
    slots = WIN + picks.shape[1]
    tile = (1, 1, heads, BLK, BLK)
    whole = lambda i, *_: (0, 0)
    args = [queries, out_grad]
    specs = [pl.BlockSpec((BLK, columns), lambda i, *_: (first + i, 0))] * 2
    for d in range(WIN):
        if d in crossing:
            arrived, skip = incoming
            args.append(arrived)
            specs.append(pl.BlockSpec(tile, lambda i, *_, d=d: (skip + crossing.index(d), 0, 0, 0, 0)))
        else:
            args.append(window)
            specs.append(pl.BlockSpec(tile, lambda i, *_, d=d: (first + i - d, d, 0, 0, 0)))
    for g in range(slots - WIN):
        args.append(glob)
        specs.append(pl.BlockSpec(tile, lambda i, *_, g=g: (first + i, g, 0, 0, 0)))
    for x in (*own, *sinks):
        args.append(x)
        specs.append(pl.BlockSpec(x.shape, whole))
    args.append(weights)
    specs.append(pl.BlockSpec((1, 1, BLK), lambda i, *_: (first + i, 0, 0)))
    if crossing:
        args.append(before)
        specs.append(pl.BlockSpec(before.shape, lambda i, *_: (0, 0, 0, 0)))
    chained = acc is not None
    acc_shapes = [(tokens, E)] * 2 + [(NGLOB * BLK, E)] * 2
    if chained:
        args.extend(acc)
        specs.extend(pl.BlockSpec(s, whole) for s in acc_shapes)
    outs = [
        jax.ShapeDtypeStruct((count * BLK, columns), BF),
        jax.ShapeDtypeStruct((count, 1, BLK), F32),
    ] + [jax.ShapeDtypeStruct(s, F32) for s in acc_shapes]
    out_specs = [
        pl.BlockSpec((BLK, columns), lambda i, *_: (i, 0)),
        pl.BlockSpec((1, 1, BLK), lambda i, *_: (i, 0, 0)),
    ] + [pl.BlockSpec(s, whole) for s in acc_shapes]
    if crossing:
        back = (2, LEAD, BLK, E)
        outs.append(jax.ShapeDtypeStruct(back, F32))
        out_specs.append(pl.BlockSpec(back, lambda i, *_: (0, 0, 0, 0)))
    elements = count * slots * heads * BLK * BLK
    return pl.pallas_call(
        functools.partial(block_kernel, first, crossing, slots, chained),
        out_shape=outs,
        grid_spec=pltpu.PrefetchScalarGridSpec(
            num_scalar_prefetch=2,
            grid=(count,),
            in_specs=specs,
            out_specs=out_specs,
            scratch_shapes=[pltpu.VMEM((slots * BLK, heads * BLK), BF)] * 2
            + [pltpu.VMEM((2, slots * BLK, 2 * BLK), F32)] * 3,
        ),
        compiler_params=pltpu.CompilerParams(vmem_limit_bytes=48 * 1024 * 1024),
        cost_estimate=pl.CostEstimate(
            flops=elements * E * 10, bytes_accessed=elements * 3, transcendentals=2 * elements
        ),
        name=f"blocks_from_{first}",
    )(base, picks, *args)


def local(queries, key_rows, values, out_grad, teacher_window, teacher_global, global_picks, mix_weight):
    tokens, columns = queries.shape
    blocks = tokens // BLK
    assert key_rows.shape[1] == E and blocks >= NGLOB
    where = lax.axis_index("seq")
    count = lax.axis_size("seq")
    base = (where * blocks).astype(jnp.int32).reshape(1)
    weights = mix_weight.reshape(blocks, 1, BLK)

    tail = slice(tokens - LEAD * BLK, tokens)
    first_rows = slice(0, NGLOB * BLK)
    pair, packed = pack(key_rows, values, teacher_window)
    heads = teacher_window.shape[2]
    half = 1
    while 2 * half < count:
        half *= 2
    sinks = pair[:, first_rows]
    known, later = [0], None
    while half > 1:
        came = lax.ppermute(sinks, "seq", [(i, i + half) for i in known if i + half < count])
        sinks = jnp.where(where % (2 * half) == half, came, sinks)
        known = sorted(known + [i + half for i in known if i + half < count])
        half //= 2
    got = shift(packed, "seq", 1)
    got_pair = got[:2 * blocks].reshape(2, tokens, E)
    before = got_pair[:, tail].reshape(2, LEAD, BLK, E)
    if 2 * blocks % heads == 0:
        arrived = (got.reshape(-1, 1, heads, BLK, BLK), 2 * blocks // heads)
    else:
        arrived = (got[2 * blocks:].reshape(1, 1, heads, BLK, BLK), 0)
    incoming = {LEAD - 1: arrived}
    forward = [(i, i + 1) for i in known if i > 0 and i + 1 < count]
    if forward:
        came = lax.ppermute(sinks, "seq", forward)
        later = sinks
        sinks = jnp.where(where % 2 == 1, came, sinks)
    sinks = jnp.where(where == 1, got_pair[:, first_rows], sinks)

    for block in range(LEAD - 2, -1, -1):
        out = jnp.concatenate(
            [teacher_window[blocks + block - d:blocks + block - d + 1, d:d + 1] for d in range(block + 1, WIN)],
            axis=0,
        )
        if block == 0 and later is not None:
            out, _ = lax.optimization_barrier((out, later))
        incoming[block] = (shift(out, "seq", 1), 0)

    own = (key_rows, values)
    sink_arrays = (sinks[0], sinks[1])
    run = lambda first, n, acc: run_blocks(
        first, n, base, global_picks, queries, out_grad, teacher_window, incoming.get(first),
        teacher_global, own, sink_arrays, weights, before, acc,
    )
    dq, loss = {}, {}
    dq[LEAD], loss[LEAD], *acc = run(LEAD, blocks - LEAD, None)
    back = 0.0
    for block in range(LEAD - 1, -1, -1):
        dq[block], loss[block], *rest = run(block, 1, acc)
        acc, part = rest[:4], rest[4]
        back = back + part
    order = sorted(dq)
    query_grad = jnp.concatenate([dq[i] for i in order], axis=0)
    row_terms = jnp.concatenate([loss[i] for i in order], axis=0).reshape(tokens)

    dk, dv, dsk, dsv = acc
    sums = [dsk, dsv]
    steps = []
    reach = 1
    while reach < count:
        steps.append([(i, i - reach) for i in range(reach, count, 2 * reach)])
        reach *= 2
    returned = None
    arrived = []
    for number, route in enumerate(steps):
        low = [x.astype(BF) for x in sums]
        came = [lax.ppermute(x, "seq", route) for x in low]
        if number == 0:
            row_terms = sum_over(row_terms, "grp")
            leaving, row_terms = lax.optimization_barrier((back.astype(BF), row_terms))
            returned = shift(leaving, "seq", -1)
        sums = [x + y.astype(F32) for x, y in zip(sums, came)]
        arrived += came
    row_terms, returned = lax.optimization_barrier((row_terms, returned))
    row_loss = sum_over(row_terms, "head")
    root = where.astype(jnp.int32).reshape(1)
    grads = finish(root, dk, dv, dsk, dsv, returned, arrived)
    return (query_grad, grads[0], grads[1], row_loss)


def solution(mesh):
    heads = ("grp", "head")
    placed = (
        P("seq", heads),
        P("seq", heads),
        P("seq", heads),
        P("seq", heads),
        P("seq", None, heads, None, None),
        P("seq", None, heads, None, None),
        P("seq", None),
        P("seq"),
    )
    return jax.shard_map(
        local,
        mesh=mesh,
        in_specs=placed,
        out_specs=(P("seq", heads), P("seq", heads), P("seq", heads), P("seq")),
        check_vma=False,
    )
```

```python
import functools
import math

import jax
import jax.numpy as jnp
from jax import lax
from jax.experimental import pallas as pl
from jax.experimental.pallas import tpu as pltpu
from jax.sharding import PartitionSpec as P

E = 128
BLK = 128
WIN = 3
NGLOB = 4
LEAD = WIN - 1
FAN = 4
CHUNK = 32
LOG2E = math.log2(math.e)
LN2 = math.log(2.0)
NT = (((1,), (1,)), ((), ()))
BF = jnp.bfloat16
F32 = jnp.float32


def shift(block, axis, distance):
    count = lax.axis_size(axis)
    route = [(i, i + distance) for i in range(count) if 0 <= i + distance < count]
    return lax.ppermute(block, axis, route)


def sum_over(block, axis):
    count = lax.axis_size(axis)
    if count & (count - 1):
        return lax.psum(block, axis)
    step = 1
    while step < count:
        block = block + lax.ppermute(block, axis, [(i, i ^ step) for i in range(count)])
        step *= 2
    return block


def block_kernel(
    first, crossing, slots, chained,
    base_ref, picks_ref, q_ref, g_ref, *rest,
):
    teacher_refs = rest[:slots]
    rest = rest[slots:]
    own_k, own_v, sink_k, sink_v, w_ref = rest[:5]
    rest = rest[5:]
    if crossing:
        before_ref, rest = rest[0], rest[1:]
    if chained:
        acc_in, rest = rest[:4], rest[4:]
    dq_ref, loss_ref, dk_ref, dv_ref, dsk_ref, dsv_ref = rest[:6]
    rest = rest[6:]
    if crossing:
        back_ref, rest = rest[0], rest[1:]
    ds_scr, pb_scr, s_scr, t_scr, u_scr = rest
    step = pl.program_id(0)
    block = first + step
    heads = q_ref.shape[1] // E
    scale = 1.0 / math.sqrt(E)
    factor = scale * LOG2E

    @pl.when(step == 0)
    def _():
        if chained:
            for out, given in zip((dk_ref, dv_ref, dsk_ref, dsv_ref), acc_in):
                out[...] = given[...]
        else:
            for out in (dk_ref, dv_ref, dsk_ref, dsv_ref):
                out[...] = jnp.zeros_like(out)

    picks = [picks_ref[block, g] for g in range(slots - WIN)]
    live = [None] + [base_ref[0] + block - d >= 0 for d in range(1, WIN)] + [p >= 0 for p in picks]
    sink_at = [pl.multiple_of(jnp.maximum(p, 0) * BLK, BLK) for p in picks]

    def rows_of(d):
        return pl.ds(pl.multiple_of((block - d) * BLK, BLK), BLK)

    keys, vals = [], []
    for d in range(WIN):
        if d in crossing:
            at = first + LEAD - d
            keys.append(before_ref[0, at])
            vals.append(before_ref[1, at])
        else:
            keys.append(own_k[rows_of(d), :])
            vals.append(own_v[rows_of(d), :])
    for at in sink_at:
        keys.append(sink_k[pl.ds(at, BLK), :])
        vals.append(sink_v[pl.ds(at, BLK), :])
    kcat = jnp.concatenate(keys, axis=0)
    vcat = jnp.concatenate(vals, axis=0)
    kcat_t = kcat.T

    w1 = w_ref[0]
    w2 = jnp.concatenate([w1, w1], axis=1)
    slope = (w2 - 1.0) * LN2
    wide = 2 * BLK
    key_id = lax.broadcasted_iota(jnp.int32, (BLK, wide), 0)
    row_id = lax.broadcasted_iota(jnp.int32, (BLK, wide), 1) & (BLK - 1)
    causal = key_id <= row_id
    low = jnp.float32(-1e9)
    loss = jnp.zeros((1, wide), F32)

    def rows_pair(ref, pair):
        ha, hb = 2 * pair, 2 * pair + 1
        return jnp.concatenate([ref[:, ha * E:(ha + 1) * E], ref[:, hb * E:(hb + 1) * E]], axis=0)

    def products(pair):
        at = pair % 2
        s_scr[at] = lax.dot_general(kcat, rows_pair(q_ref, pair), NT, preferred_element_type=F32)
        u_scr[at] = lax.dot_general(vcat, rows_pair(g_ref, pair), NT, preferred_element_type=F32)

    def fold(x, op):
        return functools.reduce(op, [x[i:i + 8] for i in range(0, CHUNK, 8)])

    def up(x):
        return jnp.sum(x, axis=0, keepdims=True)

    products(0)
    dk = dv = 0.0
    for pair in range(heads // 2):
        at = pair % 2
        if pair + 1 < heads // 2:
            products(pair + 1)
        ha, hb = 2 * pair, 2 * pair + 1
        stats = []
        for j in range(slots):
            tile = slice(j * BLK, (j + 1) * BLK)
            t = jnp.concatenate([teacher_refs[j][0, 0, ha], teacher_refs[j][0, 0, hb]], axis=0)
            t = t.T.astype(F32)
            if j == 0:
                t = jnp.where(causal, t, low)
                s_scr[at, tile] = jnp.where(causal, s_scr[at, tile], low)
            t_scr[at, tile] = t
            chunks = [slice(k, k + CHUNK) for k in range(j * BLK, (j + 1) * BLK, CHUNK)]
            m = functools.reduce(jnp.maximum, [fold(s_scr[at, c], jnp.maximum) for c in chunks])
            mt = functools.reduce(jnp.maximum, [fold(t_scr[at, c], jnp.maximum) for c in chunks])
            m = jnp.max(m, axis=0, keepdims=True)
            mt = jnp.max(mt, axis=0, keepdims=True)
            sums = None
            for c in chunks:
                x = (s_scr[at, c] - m) * factor
                y = (t_scr[at, c] - mt) * LOG2E
                es = jnp.exp2(x)
                et = jnp.exp2(y)
                gap = y - x
                u = u_scr[at, c] + slope * gap
                part = [fold(v, jnp.add) for v in (es, et, et * gap, es * gap, es * u)]
                sums = part if sums is None else [v + w for v, w in zip(sums, part)]
                s_scr[at, c] = es
                t_scr[at, c] = et
                u_scr[at, c] = u
            stats.append((m, mt, *[up(v) for v in sums]))
        m = stats[0][0]
        mt = stats[0][1]
        for j in range(1, slots):
            m = jnp.maximum(m, jnp.where(live[j], stats[j][0], low))
            mt = jnp.maximum(mt, jnp.where(live[j], stats[j][1], low))
        a = [(st[0] - m) * factor for st in stats]
        b = [(st[1] - mt) * LOG2E for st in stats]
        fa = [jnp.exp2(v) for v in a]
        fb = [jnp.exp2(v) for v in b]
        for j in range(1, slots):
            fa[j] = jnp.where(live[j], fa[j], 0.0)
            fb[j] = jnp.where(live[j], fb[j], 0.0)
        z = functools.reduce(jnp.add, [f * st[2] for f, st in zip(fa, stats)])
        zt = functools.reduce(jnp.add, [f * st[3] for f, st in zip(fb, stats)])
        rz, rzt = 1.0 / z, 1.0 / zt
        both = jnp.log2(z) - jnp.log2(zt)
        off = [vb - va + both for va, vb in zip(a, b)]
        fwd = functools.reduce(jnp.add, [f * (st[4] + o * st[3]) for f, o, st in zip(fb, off, stats)])
        rev = functools.reduce(jnp.add, [f * (st[5] + o * st[2]) for f, o, st in zip(fa, off, stats)])
        mean_u = functools.reduce(
            jnp.add, [f * (st[6] + slope * o * st[2]) for f, o, st in zip(fa, off, stats)]
        )
        loss = loss + (w2 * LN2) * (rzt * fwd) + slope * (rz * rev)
        base = w2 - rz * mean_u
        cols = slice(pair * wide, (pair + 1) * wide)
        for j in range(slots):
            to_p = fa[j] * rz
            to_t = w2 * (fb[j] * rzt)
            lift = base + slope * off[j]
            for k in range(j * BLK, (j + 1) * BLK, CHUNK):
                c = slice(k, k + CHUNK)
                p = s_scr[at, c] * to_p
                ds_scr[c, cols] = (p * (u_scr[at, c] + lift) - t_scr[at, c] * to_t).astype(BF)
                pb_scr[c, cols] = p.astype(BF)
        dq_t = jnp.dot(kcat_t, ds_scr[:, cols], preferred_element_type=F32) * scale
        dq2 = dq_t.T.astype(BF)
        dq_ref[:, ha * E:(ha + 1) * E] = dq2[:BLK]
        dq_ref[:, hb * E:(hb + 1) * E] = dq2[BLK:]
        if pair % 2 == 1 or pair + 1 == heads // 2:
            first_pair = pair - pair % 2
            cols = slice(first_pair * wide, (pair + 1) * wide)
            q_part = jnp.concatenate([rows_pair(q_ref, n) for n in range(first_pair, pair + 1)], axis=0)
            g_part = jnp.concatenate([rows_pair(g_ref, n) for n in range(first_pair, pair + 1)], axis=0)
            dk = dk + jnp.dot(ds_scr[:, cols], q_part, preferred_element_type=F32)
            dv = dv + jnp.dot(pb_scr[:, cols], g_part, preferred_element_type=F32)
    loss_ref[0] = loss[:, :BLK] + loss[:, BLK:]
    dk = dk * scale
    for d in range(WIN):
        part_k, part_v = dk[d * BLK:(d + 1) * BLK], dv[d * BLK:(d + 1) * BLK]
        if d in crossing:
            at = first + LEAD - d
            back_ref[0, at] = part_k
            back_ref[1, at] = part_v
        else:
            dk_ref[rows_of(d), :] += part_k
            dv_ref[rows_of(d), :] += part_v
    if crossing:
        untouched = [i for i in range(LEAD) if i not in [first + LEAD - d for d in crossing]]
        for i in untouched:
            back_ref[0, i] = jnp.zeros((BLK, E), F32)
            back_ref[1, i] = jnp.zeros((BLK, E), F32)
    for g, at in enumerate(sink_at):
        j = WIN + g
        dsk_ref[pl.ds(at, BLK), :] += dk[j * BLK:(j + 1) * BLK]
        dsv_ref[pl.ds(at, BLK), :] += dv[j * BLK:(j + 1) * BLK]


def run_blocks(first, count, base, picks, queries, out_grad, window, incoming, glob, own, sinks, weights,
               before, acc):
    crossing = [d for d in range(WIN) if d > first]
    assert not crossing or count == 1
    tokens, columns = queries.shape
    heads = window.shape[2]
    slots = WIN + picks.shape[1]
    tile = (1, 1, heads, BLK, BLK)
    whole = lambda i, *_: (0, 0)
    args = [queries, out_grad]
    specs = [pl.BlockSpec((BLK, columns), lambda i, *_: (first + i, 0))] * 2
    for d in range(WIN):
        if d in crossing:
            args.append(incoming)
            specs.append(pl.BlockSpec(tile, lambda i, *_, d=d: (crossing.index(d), 0, 0, 0, 0)))
        else:
            args.append(window)
            specs.append(pl.BlockSpec(tile, lambda i, *_, d=d: (first + i - d, d, 0, 0, 0)))
    for g in range(slots - WIN):
        args.append(glob)
        specs.append(pl.BlockSpec(tile, lambda i, *_, g=g: (first + i, g, 0, 0, 0)))
    for x in (*own, *sinks):
        args.append(x)
        specs.append(pl.BlockSpec(x.shape, whole))
    args.append(weights)
    specs.append(pl.BlockSpec((1, 1, BLK), lambda i, *_: (first + i, 0, 0)))
    if crossing:
        args.append(before)
        specs.append(pl.BlockSpec(before.shape, lambda i, *_: (0, 0, 0, 0)))
    chained = acc is not None
    acc_shapes = [(tokens, E)] * 2 + [(NGLOB * BLK, E)] * 2
    if chained:
        args.extend(acc)
        specs.extend(pl.BlockSpec(s, whole) for s in acc_shapes)
    outs = [
        jax.ShapeDtypeStruct((count * BLK, columns), BF),
        jax.ShapeDtypeStruct((count, 1, BLK), F32),
    ] + [jax.ShapeDtypeStruct(s, F32) for s in acc_shapes]
    out_specs = [
        pl.BlockSpec((BLK, columns), lambda i, *_: (i, 0)),
        pl.BlockSpec((1, 1, BLK), lambda i, *_: (i, 0, 0)),
    ] + [pl.BlockSpec(s, whole) for s in acc_shapes]
    if crossing:
        back = (2, LEAD, BLK, E)
        outs.append(jax.ShapeDtypeStruct(back, F32))
        out_specs.append(pl.BlockSpec(back, lambda i, *_: (0, 0, 0, 0)))
    elements = count * slots * heads * BLK * BLK
    return pl.pallas_call(
        functools.partial(block_kernel, first, crossing, slots, chained),
        out_shape=outs,
        grid_spec=pltpu.PrefetchScalarGridSpec(
            num_scalar_prefetch=2,
            grid=(count,),
            in_specs=specs,
            out_specs=out_specs,
            scratch_shapes=[pltpu.VMEM((slots * BLK, heads * BLK), BF)] * 2
            + [pltpu.VMEM((2, slots * BLK, 2 * BLK), F32)] * 3,
        ),
        compiler_params=pltpu.CompilerParams(vmem_limit_bytes=48 * 1024 * 1024),
        cost_estimate=pl.CostEstimate(
            flops=elements * E * 10, bytes_accessed=elements * 3, transcendentals=2 * elements
        ),
        name=f"blocks_from_{first}",
    )(base, picks, *args)


def local(queries, key_rows, values, out_grad, teacher_window, teacher_global, global_picks, mix_weight):
    tokens, columns = queries.shape
    blocks = tokens // BLK
    assert key_rows.shape[1] == E and blocks >= NGLOB
    where = lax.axis_index("seq")
    count = lax.axis_size("seq")
    base = (where * blocks).astype(jnp.int32).reshape(1)
    weights = mix_weight.reshape(blocks, 1, BLK)

    tail = slice(tokens - LEAD * BLK, tokens)
    first_rows = slice(0, NGLOB * BLK)
    pair = jnp.stack([key_rows, values])
    known = pair[:, first_rows]
    far = {}
    for times in range(min(FAN, count) - 1, 1, -1):
        far[times] = lax.ppermute(known, "seq", [(0, times)])
    tiles = [
        jnp.concatenate(
            [teacher_window[blocks + block - d:blocks + block - d + 1, d:d + 1] for d in range(block + 1, WIN)],
            axis=0,
        )
        for block in range(LEAD)
    ]
    pair, *tiles = lax.optimization_barrier((pair, *tiles))
    got = shift(pair, "seq", 1)
    before = got[:, tail].reshape(2, LEAD, BLK, E)
    sinks = jnp.where(where == 0, known, got[:, first_rows])
    for times, more in far.items():
        sinks = jnp.where(where == times, more, sinks)
    span = FAN
    while span < count:
        more = sinks
        for times in range(FAN - 1, 0, -1):
            route = [(i, i + times * span) for i in range(span) if i + times * span < count]
            if route:
                came = lax.ppermute(sinks, "seq", route)
                more = jnp.where((where >= times * span) & (where < (times + 1) * span), came, more)
        sinks = more
        span *= FAN

    incoming = {block: shift(tiles[block], "seq", 1) for block in range(LEAD - 1, -1, -1)}
    own = (key_rows, values)
    sink_arrays = (sinks[0], sinks[1])
    run = lambda first, n, acc: run_blocks(
        first, n, base, global_picks, queries, out_grad, teacher_window, incoming.get(first),
        teacher_global, own, sink_arrays, weights, before, acc,
    )
    dq, loss = {}, {}
    dq[LEAD], loss[LEAD], *acc = run(LEAD, blocks - LEAD, None)
    back = 0.0
    for block in range(LEAD - 1, -1, -1):
        dq[block], loss[block], *rest = run(block, 1, acc)
        acc, part = rest[:4], rest[4]
        back = back + part
    order = sorted(dq)
    query_grad = jnp.concatenate([dq[i] for i in order], axis=0)
    row_terms = jnp.concatenate([loss[i] for i in order], axis=0).reshape(tokens)

    dk, dv, dsk, dsv = acc
    sums = [dsk, dsv]
    steps = []
    reach = 1
    while reach < count:
        steps.append([(i, i - reach) for i in range(reach, count, 2 * reach)])
        reach *= 2
    returned = None
    for number, route in enumerate(steps):
        low = [x.astype(BF) for x in sums]
        if number == 1:
            row_terms, low[1] = lax.optimization_barrier((row_terms, low[1]))
        came = [lax.ppermute(x, "seq", route) for x in low]
        if number == 0:
            returned = shift(back.astype(BF), "seq", -1).astype(F32)
        sums = [x + y.astype(F32) for x, y in zip(sums, came)]
    row_loss = sum_over(sum_over(row_terms, "grp"), "head")
    grads = []
    for which, own_sum in enumerate((dk, dv)):
        whole = own_sum.at[tail].add(returned[which].reshape(LEAD * BLK, E))
        whole = whole.at[first_rows].add(jnp.where(where == 0, sums[which], 0.0))
        grads.append(whole.astype(BF))
    return (query_grad, grads[0], grads[1], row_loss)


def solution(mesh):
    heads = ("grp", "head")
    placed = (
        P("seq", heads),
        P("seq", heads),
        P("seq", heads),
        P("seq", heads),
        P("seq", None, heads, None, None),
        P("seq", None, heads, None, None),
        P("seq", None),
        P("seq"),
    )
    return jax.shard_map(
        local,
        mesh=mesh,
        in_specs=placed,
        out_specs=(P("seq", heads), P("seq", heads), P("seq", heads), P("seq")),
        check_vma=False,
    )
```

```python
import functools
import math

import jax
import jax.numpy as jnp
from jax import lax
from jax.experimental import pallas as pl
from jax.experimental.pallas import tpu as pltpu
from jax.sharding import PartitionSpec as P

E = 128
BLK = 128
WIN = 3
NGLOB = 4
LEAD = WIN - 1
FAN = 4
CHUNK = 32
LOG2E = math.log2(math.e)
LN2 = math.log(2.0)
NT = (((1,), (1,)), ((), ()))
BF = jnp.bfloat16
F32 = jnp.float32


def shift(block, axis, distance):
    count = lax.axis_size(axis)
    route = [(i, i + distance) for i in range(count) if 0 <= i + distance < count]
    return lax.ppermute(block, axis, route)


def sum_over(block, axis):
    count = lax.axis_size(axis)
    if count & (count - 1):
        return lax.psum(block, axis)
    step = 1
    while step < count:
        block = block + lax.ppermute(block, axis, [(i, i ^ step) for i in range(count)])
        step *= 2
    return block


def block_kernel(
    first, crossing, slots, chained,
    base_ref, picks_ref, q_ref, g_ref, *rest,
):
    teacher_refs = rest[:slots]
    rest = rest[slots:]
    own_k, own_v, sink_k, sink_v, w_ref = rest[:5]
    rest = rest[5:]
    if crossing:
        before_ref, rest = rest[0], rest[1:]
    if chained:
        acc_in, rest = rest[:4], rest[4:]
    dq_ref, loss_ref, dk_ref, dv_ref, dsk_ref, dsv_ref = rest[:6]
    rest = rest[6:]
    if crossing:
        back_ref, rest = rest[0], rest[1:]
    ds_scr, pb_scr, s_scr, t_scr, u_scr = rest
    step = pl.program_id(0)
    block = first + step
    heads = q_ref.shape[1] // E
    scale = 1.0 / math.sqrt(E)
    factor = scale * LOG2E

    @pl.when(step == 0)
    def _():
        if chained:
            for out, given in zip((dk_ref, dv_ref, dsk_ref, dsv_ref), acc_in):
                out[...] = given[...]
        else:
            for out in (dk_ref, dv_ref, dsk_ref, dsv_ref):
                out[...] = jnp.zeros_like(out)

    picks = [picks_ref[block, g] for g in range(slots - WIN)]
    live = [None] + [base_ref[0] + block - d >= 0 for d in range(1, WIN)] + [p >= 0 for p in picks]
    sink_at = [pl.multiple_of(jnp.maximum(p, 0) * BLK, BLK) for p in picks]

    def rows_of(d):
        return pl.ds(pl.multiple_of((block - d) * BLK, BLK), BLK)

    keys, vals = [], []
    for d in range(WIN):
        if d in crossing:
            at = first + LEAD - d
            keys.append(before_ref[0, at])
            vals.append(before_ref[1, at])
        else:
            keys.append(own_k[rows_of(d), :])
            vals.append(own_v[rows_of(d), :])
    for at in sink_at:
        keys.append(sink_k[pl.ds(at, BLK), :])
        vals.append(sink_v[pl.ds(at, BLK), :])
    kcat = jnp.concatenate(keys, axis=0)
    vcat = jnp.concatenate(vals, axis=0)
    kcat_t = kcat.T

    w1 = w_ref[0]
    w2 = jnp.concatenate([w1, w1], axis=1)
    slope = (w2 - 1.0) * LN2
    wide = 2 * BLK
    key_id = lax.broadcasted_iota(jnp.int32, (BLK, wide), 0)
    row_id = lax.broadcasted_iota(jnp.int32, (BLK, wide), 1) & (BLK - 1)
    causal = key_id <= row_id
    low = jnp.float32(-1e9)
    loss = jnp.zeros((1, wide), F32)

    def rows_pair(ref, pair):
        ha, hb = 2 * pair, 2 * pair + 1
        return jnp.concatenate([ref[:, ha * E:(ha + 1) * E], ref[:, hb * E:(hb + 1) * E]], axis=0)

    def products(pair):
        at = pair % 2
        s_scr[at] = lax.dot_general(kcat, rows_pair(q_ref, pair), NT, preferred_element_type=F32)
        u_scr[at] = lax.dot_general(vcat, rows_pair(g_ref, pair), NT, preferred_element_type=F32)

    def fold(x, op):
        return functools.reduce(op, [x[i:i + 8] for i in range(0, CHUNK, 8)])

    def up(x):
        return jnp.sum(x, axis=0, keepdims=True)

    products(0)
    dk = dv = 0.0
    for pair in range(heads // 2):
        at = pair % 2
        if pair + 1 < heads // 2:
            products(pair + 1)
        ha, hb = 2 * pair, 2 * pair + 1
        stats = []
        for j in range(slots):
            tile = slice(j * BLK, (j + 1) * BLK)
            t = jnp.concatenate([teacher_refs[j][0, 0, ha], teacher_refs[j][0, 0, hb]], axis=0)
            t = t.T
            mt = jnp.max(t, axis=0, keepdims=True).astype(F32)
            t = t.astype(F32)
            if j == 0:
                t = jnp.where(causal, t, low)
                s_scr[at, tile] = jnp.where(causal, s_scr[at, tile], low)
            t_scr[at, tile] = t
            chunks = [slice(k, k + CHUNK) for k in range(j * BLK, (j + 1) * BLK, CHUNK)]
            m = functools.reduce(jnp.maximum, [fold(s_scr[at, c], jnp.maximum) for c in chunks])
            m = jnp.max(m, axis=0, keepdims=True)
            if j == 0:
                mt = functools.reduce(jnp.maximum, [fold(t_scr[at, c], jnp.maximum) for c in chunks])
                mt = jnp.max(mt, axis=0, keepdims=True)
            sums = None
            for c in chunks:
                x = (s_scr[at, c] - m) * factor
                y = (t_scr[at, c] - mt) * LOG2E
                es = jnp.exp2(x)
                et = jnp.exp2(y)
                gap = y - x
                u = u_scr[at, c] + slope * gap
                part = [fold(v, jnp.add) for v in (es, et, et * gap, es * gap, es * u)]
                sums = part if sums is None else [v + w for v, w in zip(sums, part)]
                s_scr[at, c] = es
                t_scr[at, c] = et
                u_scr[at, c] = u
            stats.append((m, mt, *[up(v) for v in sums]))
        m = stats[0][0]
        mt = stats[0][1]
        for j in range(1, slots):
            m = jnp.maximum(m, jnp.where(live[j], stats[j][0], low))
            mt = jnp.maximum(mt, jnp.where(live[j], stats[j][1], low))
        a = [(st[0] - m) * factor for st in stats]
        b = [(st[1] - mt) * LOG2E for st in stats]
        fa = [jnp.exp2(v) for v in a]
        fb = [jnp.exp2(v) for v in b]
        for j in range(1, slots):
            fa[j] = jnp.where(live[j], fa[j], 0.0)
            fb[j] = jnp.where(live[j], fb[j], 0.0)
        z = functools.reduce(jnp.add, [f * st[2] for f, st in zip(fa, stats)])
        zt = functools.reduce(jnp.add, [f * st[3] for f, st in zip(fb, stats)])
        rz, rzt = 1.0 / z, 1.0 / zt
        both = jnp.log2(z) - jnp.log2(zt)
        off = [vb - va + both for va, vb in zip(a, b)]
        fwd = functools.reduce(jnp.add, [f * (st[4] + o * st[3]) for f, o, st in zip(fb, off, stats)])
        rev = functools.reduce(jnp.add, [f * (st[5] + o * st[2]) for f, o, st in zip(fa, off, stats)])
        mean_u = functools.reduce(
            jnp.add, [f * (st[6] + slope * o * st[2]) for f, o, st in zip(fa, off, stats)]
        )
        loss = loss + (w2 * LN2) * (rzt * fwd) + slope * (rz * rev)
        base = w2 - rz * mean_u
        cols = slice(pair * wide, (pair + 1) * wide)
        for j in range(slots):
            to_p = fa[j] * rz
            to_t = w2 * (fb[j] * rzt)
            lift = base + slope * off[j]
            for k in range(j * BLK, (j + 1) * BLK, CHUNK):
                c = slice(k, k + CHUNK)
                p = s_scr[at, c] * to_p
                ds_scr[c, cols] = (p * (u_scr[at, c] + lift) - t_scr[at, c] * to_t).astype(BF)
                pb_scr[c, cols] = p.astype(BF)
        dq_t = jnp.dot(kcat_t, ds_scr[:, cols], preferred_element_type=F32) * scale
        dq2 = dq_t.T.astype(BF)
        dq_ref[:, ha * E:(ha + 1) * E] = dq2[:BLK]
        dq_ref[:, hb * E:(hb + 1) * E] = dq2[BLK:]
        if pair % 2 == 1 or pair + 1 == heads // 2:
            first_pair = pair - pair % 2
            cols = slice(first_pair * wide, (pair + 1) * wide)
            q_part = jnp.concatenate([rows_pair(q_ref, n) for n in range(first_pair, pair + 1)], axis=0)
            g_part = jnp.concatenate([rows_pair(g_ref, n) for n in range(first_pair, pair + 1)], axis=0)
            dk = dk + jnp.dot(ds_scr[:, cols], q_part, preferred_element_type=F32)
            dv = dv + jnp.dot(pb_scr[:, cols], g_part, preferred_element_type=F32)
    loss_ref[0] = loss[:, :BLK] + loss[:, BLK:]
    dk = dk * scale
    for d in range(WIN):
        part_k, part_v = dk[d * BLK:(d + 1) * BLK], dv[d * BLK:(d + 1) * BLK]
        if d in crossing:
            at = first + LEAD - d
            back_ref[0, at] = part_k
            back_ref[1, at] = part_v
        else:
            dk_ref[rows_of(d), :] += part_k
            dv_ref[rows_of(d), :] += part_v
    if crossing:
        untouched = [i for i in range(LEAD) if i not in [first + LEAD - d for d in crossing]]
        for i in untouched:
            back_ref[0, i] = jnp.zeros((BLK, E), F32)
            back_ref[1, i] = jnp.zeros((BLK, E), F32)
    for g, at in enumerate(sink_at):
        j = WIN + g
        dsk_ref[pl.ds(at, BLK), :] += dk[j * BLK:(j + 1) * BLK]
        dsv_ref[pl.ds(at, BLK), :] += dv[j * BLK:(j + 1) * BLK]


def run_blocks(first, count, base, picks, queries, out_grad, window, incoming, glob, own, sinks, weights,
               before, acc):
    crossing = [d for d in range(WIN) if d > first]
    assert not crossing or count == 1
    tokens, columns = queries.shape
    heads = window.shape[2]
    slots = WIN + picks.shape[1]
    tile = (1, 1, heads, BLK, BLK)
    whole = lambda i, *_: (0, 0)
    args = [queries, out_grad]
    specs = [pl.BlockSpec((BLK, columns), lambda i, *_: (first + i, 0))] * 2
    for d in range(WIN):
        if d in crossing:
            args.append(incoming[d])
            specs.append(pl.BlockSpec(tile, lambda i, *_: (0, 0, 0, 0, 0)))
        else:
            args.append(window)
            specs.append(pl.BlockSpec(tile, lambda i, *_, d=d: (first + i - d, d, 0, 0, 0)))
    for g in range(slots - WIN):
        args.append(glob)
        specs.append(pl.BlockSpec(tile, lambda i, *_, g=g: (first + i, g, 0, 0, 0)))
    for x in (*own, *sinks):
        args.append(x)
        specs.append(pl.BlockSpec(x.shape, whole))
    args.append(weights)
    specs.append(pl.BlockSpec((1, 1, BLK), lambda i, *_: (first + i, 0, 0)))
    if crossing:
        args.append(before)
        specs.append(pl.BlockSpec(before.shape, lambda i, *_: (0, 0, 0, 0)))
    chained = acc is not None
    acc_shapes = [(tokens, E)] * 2 + [(NGLOB * BLK, E)] * 2
    if chained:
        args.extend(acc)
        specs.extend(pl.BlockSpec(s, whole) for s in acc_shapes)
    outs = [
        jax.ShapeDtypeStruct((count * BLK, columns), BF),
        jax.ShapeDtypeStruct((count, 1, BLK), F32),
    ] + [jax.ShapeDtypeStruct(s, F32) for s in acc_shapes]
    out_specs = [
        pl.BlockSpec((BLK, columns), lambda i, *_: (i, 0)),
        pl.BlockSpec((1, 1, BLK), lambda i, *_: (i, 0, 0)),
    ] + [pl.BlockSpec(s, whole) for s in acc_shapes]
    if crossing:
        back = (2, LEAD, BLK, E)
        outs.append(jax.ShapeDtypeStruct(back, F32))
        out_specs.append(pl.BlockSpec(back, lambda i, *_: (0, 0, 0, 0)))
    elements = count * slots * heads * BLK * BLK
    return pl.pallas_call(
        functools.partial(block_kernel, first, crossing, slots, chained),
        out_shape=outs,
        grid_spec=pltpu.PrefetchScalarGridSpec(
            num_scalar_prefetch=2,
            grid=(count,),
            in_specs=specs,
            out_specs=out_specs,
            scratch_shapes=[pltpu.VMEM((slots * BLK, heads * BLK), BF)] * 2
            + [pltpu.VMEM((2, slots * BLK, 2 * BLK), F32)] * 3,
        ),
        compiler_params=pltpu.CompilerParams(vmem_limit_bytes=(28 if crossing else 48) * 1024 * 1024),
        cost_estimate=pl.CostEstimate(
            flops=elements * E * 10, bytes_accessed=elements * 3, transcendentals=2 * elements
        ),
        name=f"blocks_from_{first}",
    )(base, picks, *args)


def local(queries, key_rows, values, out_grad, teacher_window, teacher_global, global_picks, mix_weight):
    tokens, columns = queries.shape
    blocks = tokens // BLK
    assert key_rows.shape[1] == E and blocks >= NGLOB
    where = lax.axis_index("seq")
    count = lax.axis_size("seq")
    base = (where * blocks).astype(jnp.int32).reshape(1)
    weights = mix_weight.reshape(blocks, 1, BLK)

    tail = slice(tokens - LEAD * BLK, tokens)
    first_rows = slice(0, NGLOB * BLK)
    pair = jnp.stack([key_rows, values])
    got = shift(pair, "seq", 1)
    before = got[:, tail].reshape(2, LEAD, BLK, E)
    sinks = jnp.where(where == 0, pair[:, first_rows], got[:, first_rows])
    span, known = 1, pair[:, first_rows]
    while span < count:
        for times in range(1, FAN):
            if span == 1 and times == 1:
                continue
            route = [(i, i + times * span) for i in range(span) if i + times * span < count]
            if route:
                more = lax.ppermute(known, "seq", route)
                sinks = jnp.where((where >= times * span) & (where < (times + 1) * span), more, sinks)
        span *= FAN
        known = sinks

    incoming = {}
    for block in range(LEAD - 1, -1, -1):
        offsets = list(range(block + 1, WIN))
        out = jnp.concatenate(
            [teacher_window[blocks + block - d:blocks + block - d + 1, d:d + 1] for d in offsets], axis=0
        )
        came = shift(out, "seq", 1)
        incoming[block] = {d: came[i:i + 1] for i, d in enumerate(offsets)}

    own = (key_rows, values)
    sink_arrays = (sinks[0], sinks[1])
    run = lambda first, n, acc: run_blocks(
        first, n, base, global_picks, queries, out_grad, teacher_window, incoming.get(first),
        teacher_global, own, sink_arrays, weights, before, acc,
    )
    dq, loss = {}, {}
    dq[LEAD], loss[LEAD], *acc = run(LEAD, blocks - LEAD, None)
    back = 0.0
    for block in range(LEAD - 1, -1, -1):
        dq[block], loss[block], *rest = run(block, 1, acc)
        acc, part = rest[:4], rest[4]
        back = back + part
    order = sorted(dq)
    query_grad = jnp.concatenate([dq[i] for i in order], axis=0)
    row_terms = jnp.concatenate([loss[i] for i in order], axis=0).reshape(tokens)

    dk, dv, dsk, dsv = acc
    sums = [dsk, dsv]
    steps = []
    reach = 1
    while reach < count:
        steps.append([(i, i - reach) for i in range(reach, count, 2 * reach)])
        reach *= 2
    returned = None
    for number, route in enumerate(steps):
        low = [x.astype(BF) for x in sums]
        if number == 1:
            row_terms, low[1] = lax.optimization_barrier((row_terms, low[1]))
        came = [lax.ppermute(x, "seq", route) for x in low]
        if number == 0:
            returned = shift(back.astype(BF), "seq", -1).astype(F32)
        sums = [x + y.astype(F32) for x, y in zip(sums, came)]
    row_loss = sum_over(sum_over(row_terms, "grp"), "head")
    grads = []
    for which, own_sum in enumerate((dk, dv)):
        whole = own_sum.at[tail].add(returned[which].reshape(LEAD * BLK, E))
        whole = whole.at[first_rows].add(jnp.where(where == 0, sums[which], 0.0))
        grads.append(whole.astype(BF))
    return (query_grad, grads[0], grads[1], row_loss)


def solution(mesh):
    heads = ("grp", "head")
    placed = (
        P("seq", heads),
        P("seq", heads),
        P("seq", heads),
        P("seq", heads),
        P("seq", None, heads, None, None),
        P("seq", None, heads, None, None),
        P("seq", None),
        P("seq"),
    )
    return jax.shard_map(
        local,
        mesh=mesh,
        in_specs=placed,
        out_specs=(P("seq", heads), P("seq", heads), P("seq", heads), P("seq")),
        check_vma=False,
    )
```

```python
import functools
import math

import jax
import jax.numpy as jnp
from jax import lax
from jax.experimental import pallas as pl
from jax.experimental.pallas import tpu as pltpu
from jax.sharding import PartitionSpec as P

E = 128
BLK = 128
WIN = 3
NGLOB = 4
LEAD = WIN - 1
FAN = 4
CHUNK = 32
LOG2E = math.log2(math.e)
LN2 = math.log(2.0)
NT = (((1,), (1,)), ((), ()))
BF = jnp.bfloat16
F32 = jnp.float32


def shift(block, axis, distance):
    count = lax.axis_size(axis)
    route = [(i, i + distance) for i in range(count) if 0 <= i + distance < count]
    return lax.ppermute(block, axis, route)


def exchange_sum(block, axis, steps):
    for step in steps:
        block = block + lax.ppermute(block, axis, [(i, i ^ step) for i in range(lax.axis_size(axis))])
    return block


def distances(axis):
    count = lax.axis_size(axis)
    assert count & (count - 1) == 0
    return [1 << n for n in range(count.bit_length() - 1)]


def block_kernel(
    first, crossing, slots, chained,
    base_ref, picks_ref, q_ref, g_ref, *rest,
):
    teacher_refs = rest[:slots]
    rest = rest[slots:]
    own_k, own_v, sink_k, sink_v, w_ref = rest[:5]
    rest = rest[5:]
    if crossing:
        before_ref, rest = rest[0], rest[1:]
    if chained:
        acc_in, rest = rest[:4], rest[4:]
    dq_ref, loss_ref, dk_ref, dv_ref, dsk_ref, dsv_ref = rest[:6]
    rest = rest[6:]
    if crossing:
        back_ref, rest = rest[0], rest[1:]
    ds_scr, pb_scr, s_scr, t_scr, u_scr = rest
    step = pl.program_id(0)
    block = first + step
    heads = q_ref.shape[1] // E
    scale = 1.0 / math.sqrt(E)
    factor = scale * LOG2E

    @pl.when(step == 0)
    def _():
        if chained:
            for out, given in zip((dk_ref, dv_ref, dsk_ref, dsv_ref), acc_in):
                out[...] = given[...]
        else:
            for out in (dk_ref, dv_ref, dsk_ref, dsv_ref):
                out[...] = jnp.zeros_like(out)

    picks = [picks_ref[block, g] for g in range(slots - WIN)]
    live = [None] + [base_ref[0] + block - d >= 0 for d in range(1, WIN)] + [p >= 0 for p in picks]
    sink_at = [pl.multiple_of(jnp.maximum(p, 0) * BLK, BLK) for p in picks]

    def rows_of(d):
        return pl.ds(pl.multiple_of((block - d) * BLK, BLK), BLK)

    keys, vals = [], []
    for d in range(WIN):
        if d in crossing:
            at = first + LEAD - d
            keys.append(before_ref[0, at])
            vals.append(before_ref[1, at])
        else:
            keys.append(own_k[rows_of(d), :])
            vals.append(own_v[rows_of(d), :])
    for at in sink_at:
        keys.append(sink_k[pl.ds(at, BLK), :])
        vals.append(sink_v[pl.ds(at, BLK), :])
    kcat = jnp.concatenate(keys, axis=0)
    vcat = jnp.concatenate(vals, axis=0)
    kcat_t = kcat.T

    w1 = w_ref[0]
    w2 = jnp.concatenate([w1, w1], axis=1)
    slope = (w2 - 1.0) * LN2
    wide = 2 * BLK
    key_id = lax.broadcasted_iota(jnp.int32, (BLK, wide), 0)
    row_id = lax.broadcasted_iota(jnp.int32, (BLK, wide), 1) & (BLK - 1)
    causal = key_id <= row_id
    low = jnp.float32(-1e9)
    loss = jnp.zeros((1, wide), F32)

    def rows_pair(ref, pair):
        ha, hb = 2 * pair, 2 * pair + 1
        return jnp.concatenate([ref[:, ha * E:(ha + 1) * E], ref[:, hb * E:(hb + 1) * E]], axis=0)

    def products(pair):
        at = pair % 2
        s_scr[at] = lax.dot_general(kcat, rows_pair(q_ref, pair), NT, preferred_element_type=F32)
        u_scr[at] = lax.dot_general(vcat, rows_pair(g_ref, pair), NT, preferred_element_type=F32)

    def fold(x, op):
        return functools.reduce(op, [x[i:i + 8] for i in range(0, CHUNK, 8)])

    def up(x):
        return jnp.sum(x, axis=0, keepdims=True)

    products(0)
    dk = dv = 0.0
    for pair in range(heads // 2):
        at = pair % 2
        if pair + 1 < heads // 2:
            products(pair + 1)
        ha, hb = 2 * pair, 2 * pair + 1
        stats = []
        for j in range(slots):
            tile = slice(j * BLK, (j + 1) * BLK)
            t = jnp.concatenate([teacher_refs[j][0, 0, ha], teacher_refs[j][0, 0, hb]], axis=0)
            t = t.T
            mt = jnp.max(t, axis=0, keepdims=True).astype(F32)
            t = t.astype(F32)
            if j == 0:
                t = jnp.where(causal, t, low)
                s_scr[at, tile] = jnp.where(causal, s_scr[at, tile], low)
            t_scr[at, tile] = t
            chunks = [slice(k, k + CHUNK) for k in range(j * BLK, (j + 1) * BLK, CHUNK)]
            m = functools.reduce(jnp.maximum, [fold(s_scr[at, c], jnp.maximum) for c in chunks])
            m = jnp.max(m, axis=0, keepdims=True)
            if j == 0:
                mt = functools.reduce(jnp.maximum, [fold(t_scr[at, c], jnp.maximum) for c in chunks])
                mt = jnp.max(mt, axis=0, keepdims=True)
            sums = None
            for c in chunks:
                x = (s_scr[at, c] - m) * factor
                y = (t_scr[at, c] - mt) * LOG2E
                es = jnp.exp2(x)
                et = jnp.exp2(y)
                gap = y - x
                u = u_scr[at, c] + slope * gap
                part = [fold(v, jnp.add) for v in (es, et, et * gap, es * gap, es * u)]
                sums = part if sums is None else [v + w for v, w in zip(sums, part)]
                s_scr[at, c] = es
                t_scr[at, c] = et
                u_scr[at, c] = u
            stats.append((m, mt, *[up(v) for v in sums]))
        m = stats[0][0]
        mt = stats[0][1]
        for j in range(1, slots):
            m = jnp.maximum(m, jnp.where(live[j], stats[j][0], low))
            mt = jnp.maximum(mt, jnp.where(live[j], stats[j][1], low))
        a = [(st[0] - m) * factor for st in stats]
        b = [(st[1] - mt) * LOG2E for st in stats]
        fa = [jnp.exp2(v) for v in a]
        fb = [jnp.exp2(v) for v in b]
        for j in range(1, slots):
            fa[j] = jnp.where(live[j], fa[j], 0.0)
            fb[j] = jnp.where(live[j], fb[j], 0.0)
        z = functools.reduce(jnp.add, [f * st[2] for f, st in zip(fa, stats)])
        zt = functools.reduce(jnp.add, [f * st[3] for f, st in zip(fb, stats)])
        rz, rzt = 1.0 / z, 1.0 / zt
        both = jnp.log2(z) - jnp.log2(zt)
        off = [vb - va + both for va, vb in zip(a, b)]
        fwd = functools.reduce(jnp.add, [f * (st[4] + o * st[3]) for f, o, st in zip(fb, off, stats)])
        rev = functools.reduce(jnp.add, [f * (st[5] + o * st[2]) for f, o, st in zip(fa, off, stats)])
        mean_u = functools.reduce(
            jnp.add, [f * (st[6] + slope * o * st[2]) for f, o, st in zip(fa, off, stats)]
        )
        loss = loss + (w2 * LN2) * (rzt * fwd) + slope * (rz * rev)
        base = w2 - rz * mean_u
        cols = slice(pair * wide, (pair + 1) * wide)
        for j in range(slots):
            to_p = fa[j] * rz
            to_t = w2 * (fb[j] * rzt)
            lift = base + slope * off[j]
            for k in range(j * BLK, (j + 1) * BLK, CHUNK):
                c = slice(k, k + CHUNK)
                p = s_scr[at, c] * to_p
                ds_scr[c, cols] = (p * (u_scr[at, c] + lift) - t_scr[at, c] * to_t).astype(BF)
                pb_scr[c, cols] = p.astype(BF)
        dq_t = jnp.dot(kcat_t, ds_scr[:, cols], preferred_element_type=F32) * scale
        dq2 = dq_t.T.astype(BF)
        dq_ref[:, ha * E:(ha + 1) * E] = dq2[:BLK]
        dq_ref[:, hb * E:(hb + 1) * E] = dq2[BLK:]
        if pair % 2 == 1 or pair + 1 == heads // 2:
            first_pair = pair - pair % 2
            cols = slice(first_pair * wide, (pair + 1) * wide)
            q_part = jnp.concatenate([rows_pair(q_ref, n) for n in range(first_pair, pair + 1)], axis=0)
            g_part = jnp.concatenate([rows_pair(g_ref, n) for n in range(first_pair, pair + 1)], axis=0)
            dk = dk + jnp.dot(ds_scr[:, cols], q_part, preferred_element_type=F32)
            dv = dv + jnp.dot(pb_scr[:, cols], g_part, preferred_element_type=F32)
    loss_ref[0] = loss[:, :BLK] + loss[:, BLK:]
    dk = dk * scale
    for d in range(WIN):
        part_k, part_v = dk[d * BLK:(d + 1) * BLK], dv[d * BLK:(d + 1) * BLK]
        if d in crossing:
            at = first + LEAD - d
            back_ref[0, at] = part_k
            back_ref[1, at] = part_v
        else:
            dk_ref[rows_of(d), :] += part_k
            dv_ref[rows_of(d), :] += part_v
    if crossing:
        untouched = [i for i in range(LEAD) if i not in [first + LEAD - d for d in crossing]]
        for i in untouched:
            back_ref[0, i] = jnp.zeros((BLK, E), F32)
            back_ref[1, i] = jnp.zeros((BLK, E), F32)
    for g, at in enumerate(sink_at):
        j = WIN + g
        dsk_ref[pl.ds(at, BLK), :] += dk[j * BLK:(j + 1) * BLK]
        dsv_ref[pl.ds(at, BLK), :] += dv[j * BLK:(j + 1) * BLK]


def finish_kernel(root_ref, dk_ref, dv_ref, dsk_ref, dsv_ref, back_ref, *rest):
    came, (kg_ref, vg_ref) = rest[:-2], rest[-2:]
    root = root_ref[0] == 0
    tokens = dk_ref.shape[0]
    for which, (own, sink, out) in enumerate(((dk_ref, dsk_ref, kg_ref), (dv_ref, dsv_ref, vg_ref))):
        for block in range(tokens // BLK):
            rows = slice(block * BLK, (block + 1) * BLK)
            value = own[rows]
            late = block - (tokens // BLK - LEAD)
            if late >= 0:
                value = value + back_ref[which, late].astype(F32)
            if block < NGLOB:
                extra = sink[rows]
                for arrived in came[which::2]:
                    extra = extra + arrived[rows].astype(F32)
                value = value + jnp.where(root, extra, 0.0)
            out[rows] = value.astype(BF)


def finish(root, dk, dv, dsk, dsv, back, came):
    vmem = pl.BlockSpec(memory_space=pltpu.VMEM)
    return pl.pallas_call(
        finish_kernel,
        out_shape=[jax.ShapeDtypeStruct(dk.shape, BF)] * 2,
        in_specs=[pl.BlockSpec(memory_space=pltpu.SMEM)] + [vmem] * (5 + len(came)),
        out_specs=[vmem] * 2,
        compiler_params=pltpu.CompilerParams(vmem_limit_bytes=16 * 1024 * 1024),
        cost_estimate=pl.CostEstimate(flops=4 * dk.size, bytes_accessed=14 * dk.size, transcendentals=0),
        name="finish",
    )(root, dk, dv, dsk, dsv, back, *came)


def run_blocks(first, count, base, picks, queries, out_grad, window, incoming, glob, own, sinks, weights,
               before, acc):
    crossing = [d for d in range(WIN) if d > first]
    assert not crossing or count == 1
    tokens, columns = queries.shape
    heads = window.shape[2]
    slots = WIN + picks.shape[1]
    tile = (1, 1, heads, BLK, BLK)
    whole = lambda i, *_: (0, 0)
    args = [queries, out_grad]
    specs = [pl.BlockSpec((BLK, columns), lambda i, *_: (first + i, 0))] * 2
    for d in range(WIN):
        if d in crossing:
            args.append(incoming[d])
            specs.append(pl.BlockSpec(tile, lambda i, *_: (0, 0, 0, 0, 0)))
        else:
            args.append(window)
            specs.append(pl.BlockSpec(tile, lambda i, *_, d=d: (first + i - d, d, 0, 0, 0)))
    for g in range(slots - WIN):
        args.append(glob)
        specs.append(pl.BlockSpec(tile, lambda i, *_, g=g: (first + i, g, 0, 0, 0)))
    for x in (*own, *sinks):
        args.append(x)
        specs.append(pl.BlockSpec(x.shape, whole))
    args.append(weights)
    specs.append(pl.BlockSpec((1, 1, BLK), lambda i, *_: (first + i, 0, 0)))
    if crossing:
        args.append(before)
        specs.append(pl.BlockSpec(before.shape, lambda i, *_: (0, 0, 0, 0)))
    chained = acc is not None
    acc_shapes = [(tokens, E)] * 2 + [(NGLOB * BLK, E)] * 2
    if chained:
        args.extend(acc)
        specs.extend(pl.BlockSpec(s, whole) for s in acc_shapes)
    outs = [
        jax.ShapeDtypeStruct((count * BLK, columns), BF),
        jax.ShapeDtypeStruct((count, 1, BLK), F32),
    ] + [jax.ShapeDtypeStruct(s, F32) for s in acc_shapes]
    out_specs = [
        pl.BlockSpec((BLK, columns), lambda i, *_: (i, 0)),
        pl.BlockSpec((1, 1, BLK), lambda i, *_: (i, 0, 0)),
    ] + [pl.BlockSpec(s, whole) for s in acc_shapes]
    if crossing:
        back = (2, LEAD, BLK, E)
        outs.append(jax.ShapeDtypeStruct(back, F32))
        out_specs.append(pl.BlockSpec(back, lambda i, *_: (0, 0, 0, 0)))
    elements = count * slots * heads * BLK * BLK
    return pl.pallas_call(
        functools.partial(block_kernel, first, crossing, slots, chained),
        out_shape=outs,
        grid_spec=pltpu.PrefetchScalarGridSpec(
            num_scalar_prefetch=2,
            grid=(count,),
            in_specs=specs,
            out_specs=out_specs,
            scratch_shapes=[pltpu.VMEM((slots * BLK, heads * BLK), BF)] * 2
            + [pltpu.VMEM((2, slots * BLK, 2 * BLK), F32)] * 3,
        ),
        compiler_params=pltpu.CompilerParams(vmem_limit_bytes=(28 if crossing else 48) * 1024 * 1024),
        cost_estimate=pl.CostEstimate(
            flops=elements * E * 10, bytes_accessed=elements * 3, transcendentals=2 * elements
        ),
        name=f"blocks_from_{first}",
    )(base, picks, *args)


def local(queries, key_rows, values, out_grad, teacher_window, teacher_global, global_picks, mix_weight):
    tokens, columns = queries.shape
    blocks = tokens // BLK
    assert key_rows.shape[1] == E and blocks >= NGLOB
    where = lax.axis_index("seq")
    count = lax.axis_size("seq")
    base = (where * blocks).astype(jnp.int32).reshape(1)
    weights = mix_weight.reshape(blocks, 1, BLK)

    tail = slice(tokens - LEAD * BLK, tokens)
    first_rows = slice(0, NGLOB * BLK)
    pair = jnp.stack([key_rows, values])
    got = shift(pair, "seq", 1)
    before = got[:, tail].reshape(2, LEAD, BLK, E)
    sinks = jnp.where(where == 0, pair[:, first_rows], got[:, first_rows])
    span, known = 1, pair[:, first_rows]
    while span < count:
        for times in range(1, FAN):
            if span == 1 and times == 1:
                continue
            route = [(i, i + times * span) for i in range(span) if i + times * span < count]
            if route:
                more = lax.ppermute(known, "seq", route)
                sinks = jnp.where((where >= times * span) & (where < (times + 1) * span), more, sinks)
        span *= FAN
        known = sinks

    incoming = {}
    for block in range(LEAD - 1, -1, -1):
        offsets = list(range(block + 1, WIN))
        out = jnp.concatenate(
            [teacher_window[blocks + block - d:blocks + block - d + 1, d:d + 1] for d in offsets], axis=0
        )
        came = shift(out, "seq", 1)
        incoming[block] = {d: came[i:i + 1] for i, d in enumerate(offsets)}

    own = (key_rows, values)
    sink_arrays = (sinks[0], sinks[1])
    run = lambda first, n, acc: run_blocks(
        first, n, base, global_picks, queries, out_grad, teacher_window, incoming.get(first),
        teacher_global, own, sink_arrays, weights, before, acc,
    )
    dq, loss = {}, {}
    dq[LEAD], loss[LEAD], *acc = run(LEAD, blocks - LEAD, None)
    back = 0.0
    for block in range(LEAD - 1, -1, -1):
        dq[block], loss[block], *rest = run(block, 1, acc)
        acc, part = rest[:4], rest[4]
        back = back + part
    order = sorted(dq)
    query_grad = jnp.concatenate([dq[i] for i in order], axis=0)
    row_terms = jnp.concatenate([loss[i] for i in order], axis=0).reshape(tokens)

    dk, dv, dsk, dsv = acc
    sums = [dsk, dsv]
    steps = []
    reach = 1
    while reach < count:
        steps.append([(i, i - reach) for i in range(reach, count, 2 * reach)])
        reach *= 2
    returned = None
    early, late = distances("head")[:-1], distances("head")[-1:]
    row_terms = exchange_sum(exchange_sum(row_terms, "grp", distances("grp")), "head", early)
    arrived = []
    for number, route in enumerate(steps):
        low = [x.astype(BF) for x in sums]
        came = [lax.ppermute(x, "seq", route) for x in low]
        if number == 0:
            returned = shift(back.astype(BF), "seq", -1)
        sums = [x + y.astype(F32) for x, y in zip(sums, came)]
        arrived += came
    row_terms, returned = lax.optimization_barrier((row_terms, returned))
    row_loss = exchange_sum(row_terms, "head", late)
    root = where.astype(jnp.int32).reshape(1)
    grads = finish(root, dk, dv, dsk, dsv, returned, arrived)
    return (query_grad, grads[0], grads[1], row_loss)


def solution(mesh):
    heads = ("grp", "head")
    placed = (
        P("seq", heads),
        P("seq", heads),
        P("seq", heads),
        P("seq", heads),
        P("seq", None, heads, None, None),
        P("seq", None, heads, None, None),
        P("seq", None),
        P("seq"),
    )
    return jax.shard_map(
        local,
        mesh=mesh,
        in_specs=placed,
        out_specs=(P("seq", heads), P("seq", heads), P("seq", heads), P("seq")),
        check_vma=False,
    )
```

```python
import functools
import math

import jax
import jax.numpy as jnp
from jax import lax
from jax.experimental import pallas as pl
from jax.experimental.pallas import tpu as pltpu
from jax.sharding import PartitionSpec as P

E = 128
BLK = 128
WIN = 3
NGLOB = 4
LEAD = WIN - 1
FAN = 4
CHUNK = 32
LOG2E = math.log2(math.e)
LN2 = math.log(2.0)
NT = (((1,), (1,)), ((), ()))
BF = jnp.bfloat16
F32 = jnp.float32


def shift(block, axis, distance):
    count = lax.axis_size(axis)
    route = [(i, i + distance) for i in range(count) if 0 <= i + distance < count]
    return lax.ppermute(block, axis, route)


def exchange_sum(block, axis, steps):
    for step in steps:
        block = block + lax.ppermute(block, axis, [(i, i ^ step) for i in range(lax.axis_size(axis))])
    return block


def distances(axis):
    count = lax.axis_size(axis)
    assert count & (count - 1) == 0
    return [1 << n for n in range(count.bit_length() - 1)]


def block_kernel(
    first, crossing, slots, chained,
    base_ref, picks_ref, q_ref, g_ref, *rest,
):
    teacher_refs = rest[:slots]
    rest = rest[slots:]
    own_k, own_v, sink_k, sink_v, w_ref = rest[:5]
    rest = rest[5:]
    if crossing:
        before_ref, rest = rest[0], rest[1:]
    if chained:
        acc_in, rest = rest[:4], rest[4:]
    dq_ref, loss_ref, dk_ref, dv_ref, dsk_ref, dsv_ref = rest[:6]
    rest = rest[6:]
    if crossing:
        back_ref, rest = rest[0], rest[1:]
    ds_scr, pb_scr, s_scr, t_scr, u_scr = rest
    step = pl.program_id(0)
    block = first + step
    heads = q_ref.shape[1] // E
    scale = 1.0 / math.sqrt(E)
    factor = scale * LOG2E

    @pl.when(step == 0)
    def _():
        if chained:
            for out, given in zip((dk_ref, dv_ref, dsk_ref, dsv_ref), acc_in):
                out[...] = given[...]
        else:
            for out in (dk_ref, dv_ref, dsk_ref, dsv_ref):
                out[...] = jnp.zeros_like(out)

    picks = [picks_ref[block, g] for g in range(slots - WIN)]
    live = [None] + [base_ref[0] + block - d >= 0 for d in range(1, WIN)] + [p >= 0 for p in picks]
    sink_at = [pl.multiple_of(jnp.maximum(p, 0) * BLK, BLK) for p in picks]

    def rows_of(d):
        return pl.ds(pl.multiple_of((block - d) * BLK, BLK), BLK)

    keys, vals = [], []
    for d in range(WIN):
        if d in crossing:
            at = first + LEAD - d
            keys.append(before_ref[0, at])
            vals.append(before_ref[1, at])
        else:
            keys.append(own_k[rows_of(d), :])
            vals.append(own_v[rows_of(d), :])
    for at in sink_at:
        keys.append(sink_k[pl.ds(at, BLK), :])
        vals.append(sink_v[pl.ds(at, BLK), :])
    kcat = jnp.concatenate(keys, axis=0)
    vcat = jnp.concatenate(vals, axis=0)
    kcat_t = kcat.T

    w1 = w_ref[0]
    w2 = jnp.concatenate([w1, w1], axis=1)
    slope = (w2 - 1.0) * LN2
    wide = 2 * BLK
    key_id = lax.broadcasted_iota(jnp.int32, (BLK, wide), 0)
    row_id = lax.broadcasted_iota(jnp.int32, (BLK, wide), 1) & (BLK - 1)
    causal = key_id <= row_id
    low = jnp.float32(-1e9)
    loss = jnp.zeros((1, wide), F32)

    def rows_pair(ref, pair):
        ha, hb = 2 * pair, 2 * pair + 1
        return jnp.concatenate([ref[:, ha * E:(ha + 1) * E], ref[:, hb * E:(hb + 1) * E]], axis=0)

    def products(pair):
        at = pair % 2
        s_scr[at] = lax.dot_general(kcat, rows_pair(q_ref, pair), NT, preferred_element_type=F32)
        u_scr[at] = lax.dot_general(vcat, rows_pair(g_ref, pair), NT, preferred_element_type=F32)

    def fold(x, op):
        return functools.reduce(op, [x[i:i + 8] for i in range(0, CHUNK, 8)])

    def up(x):
        return jnp.sum(x, axis=0, keepdims=True)

    products(0)
    dk = dv = 0.0
    for pair in range(heads // 2):
        at = pair % 2
        if pair + 1 < heads // 2:
            products(pair + 1)
        ha, hb = 2 * pair, 2 * pair + 1
        stats = []
        for j in range(slots):
            tile = slice(j * BLK, (j + 1) * BLK)
            t = jnp.concatenate([teacher_refs[j][0, 0, ha], teacher_refs[j][0, 0, hb]], axis=0)
            t = t.T
            mt = jnp.max(t, axis=0, keepdims=True).astype(F32)
            t = t.astype(F32)
            if j == 0:
                t = jnp.where(causal, t, low)
                s_scr[at, tile] = jnp.where(causal, s_scr[at, tile], low)
            t_scr[at, tile] = t
            chunks = [slice(k, k + CHUNK) for k in range(j * BLK, (j + 1) * BLK, CHUNK)]
            m = functools.reduce(jnp.maximum, [fold(s_scr[at, c], jnp.maximum) for c in chunks])
            m = jnp.max(m, axis=0, keepdims=True)
            if j == 0:
                mt = functools.reduce(jnp.maximum, [fold(t_scr[at, c], jnp.maximum) for c in chunks])
                mt = jnp.max(mt, axis=0, keepdims=True)
            sums = None
            for c in chunks:
                x = (s_scr[at, c] - m) * factor
                y = (t_scr[at, c] - mt) * LOG2E
                es = jnp.exp2(x)
                et = jnp.exp2(y)
                gap = y - x
                u = u_scr[at, c] + slope * gap
                part = [fold(v, jnp.add) for v in (es, et, et * gap, es * gap, es * u)]
                sums = part if sums is None else [v + w for v, w in zip(sums, part)]
                s_scr[at, c] = es
                t_scr[at, c] = et
                u_scr[at, c] = u
            stats.append((m, mt, *[up(v) for v in sums]))
        m = stats[0][0]
        mt = stats[0][1]
        for j in range(1, slots):
            m = jnp.maximum(m, jnp.where(live[j], stats[j][0], low))
            mt = jnp.maximum(mt, jnp.where(live[j], stats[j][1], low))
        a = [(st[0] - m) * factor for st in stats]
        b = [(st[1] - mt) * LOG2E for st in stats]
        fa = [jnp.exp2(v) for v in a]
        fb = [jnp.exp2(v) for v in b]
        for j in range(1, slots):
            fa[j] = jnp.where(live[j], fa[j], 0.0)
            fb[j] = jnp.where(live[j], fb[j], 0.0)
        z = functools.reduce(jnp.add, [f * st[2] for f, st in zip(fa, stats)])
        zt = functools.reduce(jnp.add, [f * st[3] for f, st in zip(fb, stats)])
        rz, rzt = 1.0 / z, 1.0 / zt
        both = jnp.log2(z) - jnp.log2(zt)
        off = [vb - va + both for va, vb in zip(a, b)]
        fwd = functools.reduce(jnp.add, [f * (st[4] + o * st[3]) for f, o, st in zip(fb, off, stats)])
        rev = functools.reduce(jnp.add, [f * (st[5] + o * st[2]) for f, o, st in zip(fa, off, stats)])
        mean_u = functools.reduce(
            jnp.add, [f * (st[6] + slope * o * st[2]) for f, o, st in zip(fa, off, stats)]
        )
        loss = loss + (w2 * LN2) * (rzt * fwd) + slope * (rz * rev)
        base = w2 - rz * mean_u
        cols = slice(pair * wide, (pair + 1) * wide)
        for j in range(slots):
            to_p = fa[j] * rz
            to_t = w2 * (fb[j] * rzt)
            lift = base + slope * off[j]
            for k in range(j * BLK, (j + 1) * BLK, CHUNK):
                c = slice(k, k + CHUNK)
                p = s_scr[at, c] * to_p
                ds_scr[c, cols] = (p * (u_scr[at, c] + lift) - t_scr[at, c] * to_t).astype(BF)
                pb_scr[c, cols] = p.astype(BF)
        dq_t = jnp.dot(kcat_t, ds_scr[:, cols], preferred_element_type=F32) * scale
        dq2 = dq_t.T.astype(BF)
        dq_ref[:, ha * E:(ha + 1) * E] = dq2[:BLK]
        dq_ref[:, hb * E:(hb + 1) * E] = dq2[BLK:]
        if pair % 2 == 1 or pair + 1 == heads // 2:
            first_pair = pair - pair % 2
            cols = slice(first_pair * wide, (pair + 1) * wide)
            q_part = jnp.concatenate([rows_pair(q_ref, n) for n in range(first_pair, pair + 1)], axis=0)
            g_part = jnp.concatenate([rows_pair(g_ref, n) for n in range(first_pair, pair + 1)], axis=0)
            dk = dk + jnp.dot(ds_scr[:, cols], q_part, preferred_element_type=F32)
            dv = dv + jnp.dot(pb_scr[:, cols], g_part, preferred_element_type=F32)
    loss_ref[0] = loss[:, :BLK] + loss[:, BLK:]
    dk = dk * scale
    for d in range(WIN):
        part_k, part_v = dk[d * BLK:(d + 1) * BLK], dv[d * BLK:(d + 1) * BLK]
        if d in crossing:
            at = first + LEAD - d
            back_ref[0, at] = part_k
            back_ref[1, at] = part_v
        else:
            dk_ref[rows_of(d), :] += part_k
            dv_ref[rows_of(d), :] += part_v
    if crossing:
        untouched = [i for i in range(LEAD) if i not in [first + LEAD - d for d in crossing]]
        for i in untouched:
            back_ref[0, i] = jnp.zeros((BLK, E), F32)
            back_ref[1, i] = jnp.zeros((BLK, E), F32)
    for g, at in enumerate(sink_at):
        j = WIN + g
        dsk_ref[pl.ds(at, BLK), :] += dk[j * BLK:(j + 1) * BLK]
        dsv_ref[pl.ds(at, BLK), :] += dv[j * BLK:(j + 1) * BLK]


def finish_kernel(root_ref, dk_ref, dv_ref, dsk_ref, dsv_ref, back_ref, *rest):
    came, (kg_ref, vg_ref) = rest[:-2], rest[-2:]
    root = root_ref[0] == 0
    tokens = dk_ref.shape[0]
    for which, (own, sink, out) in enumerate(((dk_ref, dsk_ref, kg_ref), (dv_ref, dsv_ref, vg_ref))):
        for block in range(tokens // BLK):
            rows = slice(block * BLK, (block + 1) * BLK)
            value = own[rows]
            late = block - (tokens // BLK - LEAD)
            if late >= 0:
                value = value + back_ref[which, late].astype(F32)
            if block < NGLOB:
                extra = sink[rows]
                for arrived in came[which::2]:
                    extra = extra + arrived[rows].astype(F32)
                value = value + jnp.where(root, extra, 0.0)
            out[rows] = value.astype(BF)


def finish(root, dk, dv, dsk, dsv, back, came):
    vmem = pl.BlockSpec(memory_space=pltpu.VMEM)
    return pl.pallas_call(
        finish_kernel,
        out_shape=[jax.ShapeDtypeStruct(dk.shape, BF)] * 2,
        in_specs=[pl.BlockSpec(memory_space=pltpu.SMEM)] + [vmem] * (5 + len(came)),
        out_specs=[vmem] * 2,
        compiler_params=pltpu.CompilerParams(vmem_limit_bytes=16 * 1024 * 1024),
        cost_estimate=pl.CostEstimate(flops=4 * dk.size, bytes_accessed=14 * dk.size, transcendentals=0),
        name="finish",
    )(root, dk, dv, dsk, dsv, back, *came)


def run_blocks(first, count, base, picks, queries, out_grad, window, incoming, glob, own, sinks, weights,
               before, acc):
    crossing = [d for d in range(WIN) if d > first]
    assert not crossing or count == 1
    tokens, columns = queries.shape
    heads = window.shape[2]
    slots = WIN + picks.shape[1]
    tile = (1, 1, heads, BLK, BLK)
    whole = lambda i, *_: (0, 0)
    args = [queries, out_grad]
    specs = [pl.BlockSpec((BLK, columns), lambda i, *_: (first + i, 0))] * 2
    for d in range(WIN):
        if d in crossing:
            args.append(incoming[d])
            specs.append(pl.BlockSpec(tile, lambda i, *_: (0, 0, 0, 0, 0)))
        else:
            args.append(window)
            specs.append(pl.BlockSpec(tile, lambda i, *_, d=d: (first + i - d, d, 0, 0, 0)))
    for g in range(slots - WIN):
        args.append(glob)
        specs.append(pl.BlockSpec(tile, lambda i, *_, g=g: (first + i, g, 0, 0, 0)))
    for x in (*own, *sinks):
        args.append(x)
        specs.append(pl.BlockSpec(x.shape, whole))
    args.append(weights)
    specs.append(pl.BlockSpec((1, 1, BLK), lambda i, *_: (first + i, 0, 0)))
    if crossing:
        args.append(before)
        specs.append(pl.BlockSpec(before.shape, lambda i, *_: (0, 0, 0, 0)))
    chained = acc is not None
    acc_shapes = [(tokens, E)] * 2 + [(NGLOB * BLK, E)] * 2
    if chained:
        args.extend(acc)
        specs.extend(pl.BlockSpec(s, whole) for s in acc_shapes)
    outs = [
        jax.ShapeDtypeStruct((count * BLK, columns), BF),
        jax.ShapeDtypeStruct((count, 1, BLK), F32),
    ] + [jax.ShapeDtypeStruct(s, F32) for s in acc_shapes]
    out_specs = [
        pl.BlockSpec((BLK, columns), lambda i, *_: (i, 0)),
        pl.BlockSpec((1, 1, BLK), lambda i, *_: (i, 0, 0)),
    ] + [pl.BlockSpec(s, whole) for s in acc_shapes]
    if crossing:
        back = (2, LEAD, BLK, E)
        outs.append(jax.ShapeDtypeStruct(back, F32))
        out_specs.append(pl.BlockSpec(back, lambda i, *_: (0, 0, 0, 0)))
    elements = count * slots * heads * BLK * BLK
    return pl.pallas_call(
        functools.partial(block_kernel, first, crossing, slots, chained),
        out_shape=outs,
        grid_spec=pltpu.PrefetchScalarGridSpec(
            num_scalar_prefetch=2,
            grid=(count,),
            in_specs=specs,
            out_specs=out_specs,
            scratch_shapes=[pltpu.VMEM((slots * BLK, heads * BLK), BF)] * 2
            + [pltpu.VMEM((2, slots * BLK, 2 * BLK), F32)] * 3,
        ),
        compiler_params=pltpu.CompilerParams(vmem_limit_bytes=(28 if crossing else 46) * 1024 * 1024),
        cost_estimate=pl.CostEstimate(
            flops=elements * E * 10, bytes_accessed=elements * 3, transcendentals=2 * elements
        ),
        name=f"blocks_from_{first}",
    )(base, picks, *args)


def local(queries, key_rows, values, out_grad, teacher_window, teacher_global, global_picks, mix_weight):
    tokens, columns = queries.shape
    blocks = tokens // BLK
    assert key_rows.shape[1] == E and blocks >= NGLOB
    where = lax.axis_index("seq")
    count = lax.axis_size("seq")
    base = (where * blocks).astype(jnp.int32).reshape(1)
    weights = mix_weight.reshape(blocks, 1, BLK)

    tail = slice(tokens - LEAD * BLK, tokens)
    first_rows = slice(0, NGLOB * BLK)
    pair = jnp.stack([key_rows, values])
    got = shift(pair, "seq", 1)
    before = got[:, tail].reshape(2, LEAD, BLK, E)
    sinks = jnp.where(where == 0, pair[:, first_rows], got[:, first_rows])
    span, known = 1, pair[:, first_rows]
    while span < count:
        for times in range(1, FAN):
            if span == 1 and times == 1:
                continue
            route = [(i, i + times * span) for i in range(span) if i + times * span < count]
            if route:
                more = lax.ppermute(known, "seq", route)
                sinks = jnp.where((where >= times * span) & (where < (times + 1) * span), more, sinks)
        span *= FAN
        known = sinks

    incoming = {}
    for block in range(LEAD - 1, -1, -1):
        offsets = list(range(block + 1, WIN))
        out = jnp.concatenate(
            [teacher_window[blocks + block - d:blocks + block - d + 1, d:d + 1] for d in offsets], axis=0
        )
        came = shift(out, "seq", 1)
        incoming[block] = {d: came[i:i + 1] for i, d in enumerate(offsets)}

    own = (key_rows, values)
    sink_arrays = (sinks[0], sinks[1])
    run = lambda first, n, acc: run_blocks(
        first, n, base, global_picks, queries, out_grad, teacher_window, incoming.get(first),
        teacher_global, own, sink_arrays, weights, before, acc,
    )
    dq, loss = {}, {}
    dq[LEAD], loss[LEAD], *acc = run(LEAD, blocks - LEAD, None)
    back = 0.0
    for block in range(LEAD - 1, -1, -1):
        dq[block], loss[block], *rest = run(block, 1, acc)
        acc, part = rest[:4], rest[4]
        back = back + part
    order = sorted(dq)
    query_grad = jnp.concatenate([dq[i] for i in order], axis=0)
    row_terms = jnp.concatenate([loss[i] for i in order], axis=0).reshape(tokens)

    dk, dv, dsk, dsv = acc
    sums = [dsk, dsv]
    steps = []
    reach = 1
    while reach < count:
        steps.append([(i, i - reach) for i in range(reach, count, 2 * reach)])
        reach *= 2
    returned = None
    early, late = distances("head")[:-1], distances("head")[-1:]
    row_terms = exchange_sum(exchange_sum(row_terms, "grp", distances("grp")), "head", early)
    arrived = []
    for number, route in enumerate(steps):
        low = [x.astype(BF) for x in sums]
        if number == 1:
            row_terms, low[0] = lax.optimization_barrier((row_terms, low[0]))
        came = [lax.ppermute(x, "seq", route) for x in low]
        if number == 0:
            returned = shift(back.astype(BF), "seq", -1)
        sums = [x + y.astype(F32) for x, y in zip(sums, came)]
        arrived += came
    row_loss = exchange_sum(row_terms, "head", late)
    root = where.astype(jnp.int32).reshape(1)
    grads = finish(root, dk, dv, dsk, dsv, returned, arrived)
    return (query_grad, grads[0], grads[1], row_loss)


def solution(mesh):
    heads = ("grp", "head")
    placed = (
        P("seq", heads),
        P("seq", heads),
        P("seq", heads),
        P("seq", heads),
        P("seq", None, heads, None, None),
        P("seq", None, heads, None, None),
        P("seq", None),
        P("seq"),
    )
    return jax.shard_map(
        local,
        mesh=mesh,
        in_specs=placed,
        out_specs=(P("seq", heads), P("seq", heads), P("seq", heads), P("seq")),
        check_vma=False,
    )
```

```python
import functools
import math

import jax
import jax.numpy as jnp
from jax import lax
from jax.experimental import pallas as pl
from jax.experimental.pallas import tpu as pltpu
from jax.sharding import PartitionSpec as P

E = 128
BLK = 128
WIN = 3
NGLOB = 4
LEAD = WIN - 1
FAN = 4
CHUNK = 32
LOG2E = math.log2(math.e)
LN2 = math.log(2.0)
NT = (((1,), (1,)), ((), ()))
BF = jnp.bfloat16
F32 = jnp.float32


def shift(block, axis, distance):
    count = lax.axis_size(axis)
    route = [(i, i + distance) for i in range(count) if 0 <= i + distance < count]
    return lax.ppermute(block, axis, route)


def exchange_sum(block, axis, steps):
    for step in steps:
        block = block + lax.ppermute(block, axis, [(i, i ^ step) for i in range(lax.axis_size(axis))])
    return block


def distances(axis):
    count = lax.axis_size(axis)
    assert count & (count - 1) == 0
    return [1 << n for n in range(count.bit_length() - 1)]


def block_kernel(
    first, crossing, slots, chained,
    base_ref, picks_ref, q_ref, g_ref, *rest,
):
    teacher_refs = rest[:slots]
    rest = rest[slots:]
    own_k, own_v, sink_k, sink_v, w_ref = rest[:5]
    rest = rest[5:]
    if crossing:
        before_ref, rest = rest[0], rest[1:]
    if chained:
        acc_in, rest = rest[:4], rest[4:]
    dq_ref, loss_ref, dk_ref, dv_ref, dsk_ref, dsv_ref = rest[:6]
    rest = rest[6:]
    if crossing:
        back_ref, rest = rest[0], rest[1:]
    ds_scr, pb_scr, s_scr, t_scr, u_scr = rest
    step = pl.program_id(0)
    block = first + step
    heads = q_ref.shape[1] // E
    scale = 1.0 / math.sqrt(E)
    factor = scale * LOG2E

    @pl.when(step == 0)
    def _():
        if chained:
            for out, given in zip((dk_ref, dv_ref, dsk_ref, dsv_ref), acc_in):
                out[...] = given[...]
        else:
            for out in (dk_ref, dv_ref, dsk_ref, dsv_ref):
                out[...] = jnp.zeros_like(out)

    picks = [picks_ref[block, g] for g in range(slots - WIN)]
    live = [None] + [base_ref[0] + block - d >= 0 for d in range(1, WIN)] + [p >= 0 for p in picks]
    sink_at = [pl.multiple_of(jnp.maximum(p, 0) * BLK, BLK) for p in picks]

    def rows_of(d):
        return pl.ds(pl.multiple_of((block - d) * BLK, BLK), BLK)

    keys, vals = [], []
    for d in range(WIN):
        if d in crossing:
            at = first + LEAD - d
            keys.append(before_ref[0, at])
            vals.append(before_ref[1, at])
        else:
            keys.append(own_k[rows_of(d), :])
            vals.append(own_v[rows_of(d), :])
    for at in sink_at:
        keys.append(sink_k[pl.ds(at, BLK), :])
        vals.append(sink_v[pl.ds(at, BLK), :])
    kcat = jnp.concatenate(keys, axis=0)
    vcat = jnp.concatenate(vals, axis=0)
    kcat_t = kcat.T

    w1 = w_ref[0]
    w2 = jnp.concatenate([w1, w1], axis=1)
    slope = (w2 - 1.0) * LN2
    wide = 2 * BLK
    key_id = lax.broadcasted_iota(jnp.int32, (BLK, wide), 0)
    row_id = lax.broadcasted_iota(jnp.int32, (BLK, wide), 1) & (BLK - 1)
    causal = key_id <= row_id
    low = jnp.float32(-1e9)
    loss = jnp.zeros((1, wide), F32)

    def rows_pair(ref, pair):
        ha, hb = 2 * pair, 2 * pair + 1
        return jnp.concatenate([ref[:, ha * E:(ha + 1) * E], ref[:, hb * E:(hb + 1) * E]], axis=0)

    def products(pair):
        at = pair % 2
        s_scr[at] = lax.dot_general(kcat, rows_pair(q_ref, pair), NT, preferred_element_type=F32)
        u_scr[at] = lax.dot_general(vcat, rows_pair(g_ref, pair), NT, preferred_element_type=F32)

    def fold(x, op):
        return functools.reduce(op, [x[i:i + 8] for i in range(0, CHUNK, 8)])

    def up(x):
        return jnp.sum(x, axis=0, keepdims=True)

    products(0)
    dk = dv = 0.0
    for pair in range(heads // 2):
        at = pair % 2
        if pair + 1 < heads // 2:
            products(pair + 1)
        ha, hb = 2 * pair, 2 * pair + 1
        stats = []
        for j in range(slots):
            tile = slice(j * BLK, (j + 1) * BLK)
            t = jnp.concatenate([teacher_refs[j][0, 0, ha], teacher_refs[j][0, 0, hb]], axis=0)
            t = t.T
            mt = jnp.max(t, axis=0, keepdims=True).astype(F32)
            t = t.astype(F32)
            if j == 0:
                t = jnp.where(causal, t, low)
                s_scr[at, tile] = jnp.where(causal, s_scr[at, tile], low)
            t_scr[at, tile] = t
            chunks = [slice(k, k + CHUNK) for k in range(j * BLK, (j + 1) * BLK, CHUNK)]
            m = functools.reduce(jnp.maximum, [fold(s_scr[at, c], jnp.maximum) for c in chunks])
            m = jnp.max(m, axis=0, keepdims=True)
            if j == 0:
                mt = functools.reduce(jnp.maximum, [fold(t_scr[at, c], jnp.maximum) for c in chunks])
                mt = jnp.max(mt, axis=0, keepdims=True)
            sums = None
            for c in chunks:
                x = (s_scr[at, c] - m) * factor
                y = (t_scr[at, c] - mt) * LOG2E
                es = jnp.exp2(x)
                et = jnp.exp2(y)
                gap = y - x
                u = u_scr[at, c] + slope * gap
                part = [fold(v, jnp.add) for v in (es, et, et * gap, es * gap, es * u)]
                sums = part if sums is None else [v + w for v, w in zip(sums, part)]
                s_scr[at, c] = es
                t_scr[at, c] = et
                u_scr[at, c] = u
            stats.append((m, mt, *[up(v) for v in sums]))
        m = stats[0][0]
        mt = stats[0][1]
        for j in range(1, slots):
            m = jnp.maximum(m, jnp.where(live[j], stats[j][0], low))
            mt = jnp.maximum(mt, jnp.where(live[j], stats[j][1], low))
        a = [(st[0] - m) * factor for st in stats]
        b = [(st[1] - mt) * LOG2E for st in stats]
        fa = [jnp.exp2(v) for v in a]
        fb = [jnp.exp2(v) for v in b]
        for j in range(1, slots):
            fa[j] = jnp.where(live[j], fa[j], 0.0)
            fb[j] = jnp.where(live[j], fb[j], 0.0)
        z = functools.reduce(jnp.add, [f * st[2] for f, st in zip(fa, stats)])
        zt = functools.reduce(jnp.add, [f * st[3] for f, st in zip(fb, stats)])
        rz, rzt = 1.0 / z, 1.0 / zt
        both = jnp.log2(z) - jnp.log2(zt)
        off = [vb - va + both for va, vb in zip(a, b)]
        fwd = functools.reduce(jnp.add, [f * (st[4] + o * st[3]) for f, o, st in zip(fb, off, stats)])
        rev = functools.reduce(jnp.add, [f * (st[5] + o * st[2]) for f, o, st in zip(fa, off, stats)])
        mean_u = functools.reduce(
            jnp.add, [f * (st[6] + slope * o * st[2]) for f, o, st in zip(fa, off, stats)]
        )
        loss = loss + (w2 * LN2) * (rzt * fwd) + slope * (rz * rev)
        base = w2 - rz * mean_u
        cols = slice(pair * wide, (pair + 1) * wide)
        for j in range(slots):
            to_p = fa[j] * rz
            to_t = w2 * (fb[j] * rzt)
            lift = base + slope * off[j]
            for k in range(j * BLK, (j + 1) * BLK, CHUNK):
                c = slice(k, k + CHUNK)
                p = s_scr[at, c] * to_p
                ds_scr[c, cols] = (p * (u_scr[at, c] + lift) - t_scr[at, c] * to_t).astype(BF)
                pb_scr[c, cols] = p.astype(BF)
        dq_t = jnp.dot(kcat_t, ds_scr[:, cols], preferred_element_type=F32) * scale
        dq2 = dq_t.T.astype(BF)
        dq_ref[:, ha * E:(ha + 1) * E] = dq2[:BLK]
        dq_ref[:, hb * E:(hb + 1) * E] = dq2[BLK:]
        if pair % 2 == 1 or pair + 1 == heads // 2:
            first_pair = pair - pair % 2
            cols = slice(first_pair * wide, (pair + 1) * wide)
            q_part = jnp.concatenate([rows_pair(q_ref, n) for n in range(first_pair, pair + 1)], axis=0)
            g_part = jnp.concatenate([rows_pair(g_ref, n) for n in range(first_pair, pair + 1)], axis=0)
            dk = dk + jnp.dot(ds_scr[:, cols], q_part, preferred_element_type=F32)
            dv = dv + jnp.dot(pb_scr[:, cols], g_part, preferred_element_type=F32)
    loss_ref[0] = loss[:, :BLK] + loss[:, BLK:]
    dk = dk * scale
    for d in range(WIN):
        part_k, part_v = dk[d * BLK:(d + 1) * BLK], dv[d * BLK:(d + 1) * BLK]
        if d in crossing:
            at = first + LEAD - d
            back_ref[0, at] = part_k
            back_ref[1, at] = part_v
        else:
            dk_ref[rows_of(d), :] += part_k
            dv_ref[rows_of(d), :] += part_v
    if crossing:
        untouched = [i for i in range(LEAD) if i not in [first + LEAD - d for d in crossing]]
        for i in untouched:
            back_ref[0, i] = jnp.zeros((BLK, E), F32)
            back_ref[1, i] = jnp.zeros((BLK, E), F32)
    for g, at in enumerate(sink_at):
        j = WIN + g
        dsk_ref[pl.ds(at, BLK), :] += dk[j * BLK:(j + 1) * BLK]
        dsv_ref[pl.ds(at, BLK), :] += dv[j * BLK:(j + 1) * BLK]


def finish_kernel(root_ref, dk_ref, dv_ref, dsk_ref, dsv_ref, back_ref, *rest):
    came, (kg_ref, vg_ref) = rest[:-2], rest[-2:]
    root = root_ref[0] == 0
    tokens = dk_ref.shape[0]
    for which, (own, sink, out) in enumerate(((dk_ref, dsk_ref, kg_ref), (dv_ref, dsv_ref, vg_ref))):
        for block in range(tokens // BLK):
            rows = slice(block * BLK, (block + 1) * BLK)
            value = own[rows]
            late = block - (tokens // BLK - LEAD)
            if late >= 0:
                value = value + back_ref[which, late].astype(F32)
            if block < NGLOB:
                extra = sink[rows]
                for arrived in came[which::2]:
                    extra = extra + arrived[rows].astype(F32)
                value = value + jnp.where(root, extra, 0.0)
            out[rows] = value.astype(BF)


def finish(root, dk, dv, dsk, dsv, back, came):
    vmem = pl.BlockSpec(memory_space=pltpu.VMEM)
    return pl.pallas_call(
        finish_kernel,
        out_shape=[jax.ShapeDtypeStruct(dk.shape, BF)] * 2,
        in_specs=[pl.BlockSpec(memory_space=pltpu.SMEM)] + [vmem] * (5 + len(came)),
        out_specs=[vmem] * 2,
        compiler_params=pltpu.CompilerParams(vmem_limit_bytes=16 * 1024 * 1024),
        cost_estimate=pl.CostEstimate(flops=4 * dk.size, bytes_accessed=14 * dk.size, transcendentals=0),
        name="finish",
    )(root, dk, dv, dsk, dsv, back, *came)


def run_blocks(first, count, base, picks, queries, out_grad, window, incoming, glob, own, sinks, weights,
               before, acc):
    crossing = [d for d in range(WIN) if d > first]
    assert not crossing or count == 1
    tokens, columns = queries.shape
    heads = window.shape[2]
    slots = WIN + picks.shape[1]
    tile = (1, 1, heads, BLK, BLK)
    whole = lambda i, *_: (0, 0)
    args = [queries, out_grad]
    specs = [pl.BlockSpec((BLK, columns), lambda i, *_: (first + i, 0))] * 2
    for d in range(WIN):
        if d in crossing:
            args.append(incoming[d])
            specs.append(pl.BlockSpec(tile, lambda i, *_: (0, 0, 0, 0, 0)))
        else:
            args.append(window)
            specs.append(pl.BlockSpec(tile, lambda i, *_, d=d: (first + i - d, d, 0, 0, 0)))
    for g in range(slots - WIN):
        args.append(glob)
        specs.append(pl.BlockSpec(tile, lambda i, *_, g=g: (first + i, g, 0, 0, 0)))
    for x in (*own, *sinks):
        args.append(x)
        specs.append(pl.BlockSpec(x.shape, whole))
    args.append(weights)
    specs.append(pl.BlockSpec((1, 1, BLK), lambda i, *_: (first + i, 0, 0)))
    if crossing:
        args.append(before)
        specs.append(pl.BlockSpec(before.shape, lambda i, *_: (0, 0, 0, 0)))
    chained = acc is not None
    acc_shapes = [(tokens, E)] * 2 + [(NGLOB * BLK, E)] * 2
    if chained:
        args.extend(acc)
        specs.extend(pl.BlockSpec(s, whole) for s in acc_shapes)
    outs = [
        jax.ShapeDtypeStruct((count * BLK, columns), BF),
        jax.ShapeDtypeStruct((count, 1, BLK), F32),
    ] + [jax.ShapeDtypeStruct(s, F32) for s in acc_shapes]
    out_specs = [
        pl.BlockSpec((BLK, columns), lambda i, *_: (i, 0)),
        pl.BlockSpec((1, 1, BLK), lambda i, *_: (i, 0, 0)),
    ] + [pl.BlockSpec(s, whole) for s in acc_shapes]
    if crossing:
        back = (2, LEAD, BLK, E)
        outs.append(jax.ShapeDtypeStruct(back, F32))
        out_specs.append(pl.BlockSpec(back, lambda i, *_: (0, 0, 0, 0)))
    elements = count * slots * heads * BLK * BLK
    return pl.pallas_call(
        functools.partial(block_kernel, first, crossing, slots, chained),
        out_shape=outs,
        grid_spec=pltpu.PrefetchScalarGridSpec(
            num_scalar_prefetch=2,
            grid=(count,),
            in_specs=specs,
            out_specs=out_specs,
            scratch_shapes=[pltpu.VMEM((slots * BLK, heads * BLK), BF)] * 2
            + [pltpu.VMEM((2, slots * BLK, 2 * BLK), F32)] * 3,
        ),
        compiler_params=pltpu.CompilerParams(vmem_limit_bytes=(28 if crossing else 48) * 1024 * 1024),
        cost_estimate=pl.CostEstimate(
            flops=elements * E * 10, bytes_accessed=elements * 3, transcendentals=2 * elements
        ),
        name=f"blocks_from_{first}",
    )(base, picks, *args)


def local(queries, key_rows, values, out_grad, teacher_window, teacher_global, global_picks, mix_weight):
    tokens, columns = queries.shape
    blocks = tokens // BLK
    assert key_rows.shape[1] == E and blocks >= NGLOB
    where = lax.axis_index("seq")
    count = lax.axis_size("seq")
    base = (where * blocks).astype(jnp.int32).reshape(1)
    weights = mix_weight.reshape(blocks, 1, BLK)

    tail = slice(tokens - LEAD * BLK, tokens)
    first_rows = slice(0, NGLOB * BLK)
    pair = jnp.stack([key_rows, values])
    got = shift(pair, "seq", 1)
    before = got[:, tail].reshape(2, LEAD, BLK, E)
    sinks = jnp.where(where == 0, pair[:, first_rows], got[:, first_rows])
    span, known = 1, pair[:, first_rows]
    while span < count:
        for times in range(1, FAN):
            if span == 1 and times == 1:
                continue
            route = [(i, i + times * span) for i in range(span) if i + times * span < count]
            if route:
                more = lax.ppermute(known, "seq", route)
                sinks = jnp.where((where >= times * span) & (where < (times + 1) * span), more, sinks)
        span *= FAN
        known = sinks

    incoming = {}
    for block in range(LEAD - 1, -1, -1):
        offsets = list(range(block + 1, WIN))
        out = jnp.concatenate(
            [teacher_window[blocks + block - d:blocks + block - d + 1, d:d + 1] for d in offsets], axis=0
        )
        came = shift(out, "seq", 1)
        incoming[block] = {d: came[i:i + 1] for i, d in enumerate(offsets)}

    own = (key_rows, values)
    sink_arrays = (sinks[0], sinks[1])
    run = lambda first, n, acc: run_blocks(
        first, n, base, global_picks, queries, out_grad, teacher_window, incoming.get(first),
        teacher_global, own, sink_arrays, weights, before, acc,
    )
    dq, loss = {}, {}
    dq[LEAD], loss[LEAD], *acc = run(LEAD, blocks - LEAD, None)
    back = 0.0
    for block in range(LEAD - 1, -1, -1):
        dq[block], loss[block], *rest = run(block, 1, acc)
        acc, part = rest[:4], rest[4]
        back = back + part
    order = sorted(dq)
    query_grad = jnp.concatenate([dq[i] for i in order], axis=0)
    row_terms = jnp.concatenate([loss[i] for i in order], axis=0).reshape(tokens)

    dk, dv, dsk, dsv = acc
    sums = [dsk, dsv]
    steps = []
    reach = 1
    while reach < count:
        steps.append([(i, i - reach) for i in range(reach, count, 2 * reach)])
        reach *= 2
    returned = None
    early, late = distances("head")[:-1], distances("head")[-1:]
    row_terms = exchange_sum(exchange_sum(row_terms, "grp", distances("grp")), "head", early)
    arrived = []
    for number, route in enumerate(steps):
        low = [x.astype(BF) for x in sums]
        if number == 1:
            row_terms, low[0] = lax.optimization_barrier((row_terms, low[0]))
        came = [lax.ppermute(x, "seq", route) for x in low]
        if number == 0:
            returned = shift(back.astype(BF), "seq", -1)
        sums = [x + y.astype(F32) for x, y in zip(sums, came)]
        arrived += came
    row_loss = exchange_sum(row_terms, "head", late)
    root = where.astype(jnp.int32).reshape(1)
    grads = finish(root, dk, dv, dsk, dsv, returned, arrived)
    return (query_grad, grads[0], grads[1], row_loss)


def solution(mesh):
    heads = ("grp", "head")
    placed = (
        P("seq", heads),
        P("seq", heads),
        P("seq", heads),
        P("seq", heads),
        P("seq", None, heads, None, None),
        P("seq", None, heads, None, None),
        P("seq", None),
        P("seq"),
    )
    return jax.shard_map(
        local,
        mesh=mesh,
        in_specs=placed,
        out_specs=(P("seq", heads), P("seq", heads), P("seq", heads), P("seq")),
        check_vma=False,
    )
```

```python
import functools
import math

import jax
import jax.numpy as jnp
from jax import lax
from jax.experimental import pallas as pl
from jax.experimental.pallas import tpu as pltpu
from jax.sharding import PartitionSpec as P

E = 128
BLK = 128
WIN = 3
NGLOB = 4
LEAD = WIN - 1
FAN = 4
CHUNK = 32
LOG2E = math.log2(math.e)
LN2 = math.log(2.0)
NT = (((1,), (1,)), ((), ()))
BF = jnp.bfloat16
F32 = jnp.float32


def shift(block, axis, distance):
    count = lax.axis_size(axis)
    route = [(i, i + distance) for i in range(count) if 0 <= i + distance < count]
    return lax.ppermute(block, axis, route)


def exchange_sum(block, axis, steps):
    for step in steps:
        block = block + lax.ppermute(block, axis, [(i, i ^ step) for i in range(lax.axis_size(axis))])
    return block


def distances(axis):
    count = lax.axis_size(axis)
    assert count & (count - 1) == 0
    return [1 << n for n in range(count.bit_length() - 1)]


def block_kernel(
    first, crossing, slots, chained,
    base_ref, picks_ref, q_ref, g_ref, *rest,
):
    teacher_refs = rest[:slots]
    rest = rest[slots:]
    own_k, own_v, sink_k, sink_v, w_ref = rest[:5]
    rest = rest[5:]
    if crossing:
        before_ref, rest = rest[0], rest[1:]
    if chained:
        acc_in, rest = rest[:4], rest[4:]
    dq_ref, loss_ref, dk_ref, dv_ref, dsk_ref, dsv_ref = rest[:6]
    rest = rest[6:]
    if crossing:
        back_ref, rest = rest[0], rest[1:]
    ds_scr, pb_scr, s_scr, t_scr, u_scr = rest
    step = pl.program_id(0)
    block = first + step
    heads = q_ref.shape[1] // E
    scale = 1.0 / math.sqrt(E)
    factor = scale * LOG2E

    @pl.when(step == 0)
    def _():
        if chained:
            for out, given in zip((dk_ref, dv_ref, dsk_ref, dsv_ref), acc_in):
                out[...] = given[...]
        else:
            for out in (dk_ref, dv_ref, dsk_ref, dsv_ref):
                out[...] = jnp.zeros_like(out)

    picks = [picks_ref[block, g] for g in range(slots - WIN)]
    live = [None] + [base_ref[0] + block - d >= 0 for d in range(1, WIN)] + [p >= 0 for p in picks]
    sink_at = [pl.multiple_of(jnp.maximum(p, 0) * BLK, BLK) for p in picks]

    def rows_of(d):
        return pl.ds(pl.multiple_of((block - d) * BLK, BLK), BLK)

    keys, vals = [], []
    for d in range(WIN):
        if d in crossing:
            at = first + LEAD - d
            keys.append(before_ref[0, at])
            vals.append(before_ref[1, at])
        else:
            keys.append(own_k[rows_of(d), :])
            vals.append(own_v[rows_of(d), :])
    for at in sink_at:
        keys.append(sink_k[pl.ds(at, BLK), :])
        vals.append(sink_v[pl.ds(at, BLK), :])
    kcat = jnp.concatenate(keys, axis=0)
    vcat = jnp.concatenate(vals, axis=0)
    kcat_t = kcat.T

    w1 = w_ref[0]
    w2 = jnp.concatenate([w1, w1], axis=1)
    slope = (w2 - 1.0) * LN2
    wide = 2 * BLK
    key_id = lax.broadcasted_iota(jnp.int32, (BLK, wide), 0)
    row_id = lax.broadcasted_iota(jnp.int32, (BLK, wide), 1) & (BLK - 1)
    causal = key_id <= row_id
    low = jnp.float32(-1e9)
    loss = jnp.zeros((1, wide), F32)

    def rows_pair(ref, pair):
        ha, hb = 2 * pair, 2 * pair + 1
        return jnp.concatenate([ref[:, ha * E:(ha + 1) * E], ref[:, hb * E:(hb + 1) * E]], axis=0)

    def products(pair):
        at = pair % 2
        s_scr[at] = lax.dot_general(kcat, rows_pair(q_ref, pair), NT, preferred_element_type=F32)
        u_scr[at] = lax.dot_general(vcat, rows_pair(g_ref, pair), NT, preferred_element_type=F32)

    def fold(x, op):
        return functools.reduce(op, [x[i:i + 8] for i in range(0, CHUNK, 8)])

    def up(x):
        return jnp.sum(x, axis=0, keepdims=True)

    products(0)
    dk = dv = 0.0
    for pair in range(heads // 2):
        at = pair % 2
        if pair + 1 < heads // 2:
            products(pair + 1)
        ha, hb = 2 * pair, 2 * pair + 1
        stats = []
        for j in range(slots):
            tile = slice(j * BLK, (j + 1) * BLK)
            t = jnp.concatenate([teacher_refs[j][0, 0, ha], teacher_refs[j][0, 0, hb]], axis=0)
            t = t.T
            mt = jnp.max(t, axis=0, keepdims=True).astype(F32)
            t = t.astype(F32)
            if j == 0:
                t = jnp.where(causal, t, low)
                s_scr[at, tile] = jnp.where(causal, s_scr[at, tile], low)
            t_scr[at, tile] = t
            chunks = [slice(k, k + CHUNK) for k in range(j * BLK, (j + 1) * BLK, CHUNK)]
            m = functools.reduce(jnp.maximum, [fold(s_scr[at, c], jnp.maximum) for c in chunks])
            m = jnp.max(m, axis=0, keepdims=True)
            if j == 0:
                mt = functools.reduce(jnp.maximum, [fold(t_scr[at, c], jnp.maximum) for c in chunks])
                mt = jnp.max(mt, axis=0, keepdims=True)
            sums = None
            for c in chunks:
                x = (s_scr[at, c] - m) * factor
                y = (t_scr[at, c] - mt) * LOG2E
                es = jnp.exp2(x)
                et = jnp.exp2(y)
                gap = y - x
                u = u_scr[at, c] + slope * gap
                part = [fold(v, jnp.add) for v in (es, et, et * gap, es * gap, es * u)]
                sums = part if sums is None else [v + w for v, w in zip(sums, part)]
                s_scr[at, c] = es
                t_scr[at, c] = et
                u_scr[at, c] = u
            stats.append((m, mt, *[up(v) for v in sums]))
        m = stats[0][0]
        mt = stats[0][1]
        for j in range(1, slots):
            m = jnp.maximum(m, jnp.where(live[j], stats[j][0], low))
            mt = jnp.maximum(mt, jnp.where(live[j], stats[j][1], low))
        a = [(st[0] - m) * factor for st in stats]
        b = [(st[1] - mt) * LOG2E for st in stats]
        fa = [jnp.exp2(v) for v in a]
        fb = [jnp.exp2(v) for v in b]
        for j in range(1, slots):
            fa[j] = jnp.where(live[j], fa[j], 0.0)
            fb[j] = jnp.where(live[j], fb[j], 0.0)
        z = functools.reduce(jnp.add, [f * st[2] for f, st in zip(fa, stats)])
        zt = functools.reduce(jnp.add, [f * st[3] for f, st in zip(fb, stats)])
        rz, rzt = 1.0 / z, 1.0 / zt
        both = jnp.log2(z) - jnp.log2(zt)
        off = [vb - va + both for va, vb in zip(a, b)]
        fwd = functools.reduce(jnp.add, [f * (st[4] + o * st[3]) for f, o, st in zip(fb, off, stats)])
        rev = functools.reduce(jnp.add, [f * (st[5] + o * st[2]) for f, o, st in zip(fa, off, stats)])
        mean_u = functools.reduce(
            jnp.add, [f * (st[6] + slope * o * st[2]) for f, o, st in zip(fa, off, stats)]
        )
        loss = loss + (w2 * LN2) * (rzt * fwd) + slope * (rz * rev)
        base = w2 - rz * mean_u
        cols = slice(pair * wide, (pair + 1) * wide)
        for j in range(slots):
            to_p = fa[j] * rz
            to_t = w2 * (fb[j] * rzt)
            lift = base + slope * off[j]
            for k in range(j * BLK, (j + 1) * BLK, CHUNK):
                c = slice(k, k + CHUNK)
                p = s_scr[at, c] * to_p
                ds_scr[c, cols] = (p * (u_scr[at, c] + lift) - t_scr[at, c] * to_t).astype(BF)
                pb_scr[c, cols] = p.astype(BF)
        dq_t = jnp.dot(kcat_t, ds_scr[:, cols], preferred_element_type=F32) * scale
        dq2 = dq_t.T.astype(BF)
        dq_ref[:, ha * E:(ha + 1) * E] = dq2[:BLK]
        dq_ref[:, hb * E:(hb + 1) * E] = dq2[BLK:]
        if pair % 2 == 1 or pair + 1 == heads // 2:
            first_pair = pair - pair % 2
            cols = slice(first_pair * wide, (pair + 1) * wide)
            q_part = jnp.concatenate([rows_pair(q_ref, n) for n in range(first_pair, pair + 1)], axis=0)
            g_part = jnp.concatenate([rows_pair(g_ref, n) for n in range(first_pair, pair + 1)], axis=0)
            dk = dk + jnp.dot(ds_scr[:, cols], q_part, preferred_element_type=F32)
            dv = dv + jnp.dot(pb_scr[:, cols], g_part, preferred_element_type=F32)
    loss_ref[0] = loss[:, :BLK] + loss[:, BLK:]
    dk = dk * scale
    for d in range(WIN):
        part_k, part_v = dk[d * BLK:(d + 1) * BLK], dv[d * BLK:(d + 1) * BLK]
        if d in crossing:
            at = first + LEAD - d
            back_ref[0, at] = part_k
            back_ref[1, at] = part_v
        else:
            dk_ref[rows_of(d), :] += part_k
            dv_ref[rows_of(d), :] += part_v
    if crossing:
        untouched = [i for i in range(LEAD) if i not in [first + LEAD - d for d in crossing]]
        for i in untouched:
            back_ref[0, i] = jnp.zeros((BLK, E), F32)
            back_ref[1, i] = jnp.zeros((BLK, E), F32)
    for g, at in enumerate(sink_at):
        j = WIN + g
        dsk_ref[pl.ds(at, BLK), :] += dk[j * BLK:(j + 1) * BLK]
        dsv_ref[pl.ds(at, BLK), :] += dv[j * BLK:(j + 1) * BLK]


def finish_kernel(root_ref, dk_ref, dv_ref, dsk_ref, dsv_ref, back_ref, *rest):
    came, (kg_ref, vg_ref) = rest[:-2], rest[-2:]
    root = root_ref[0] == 0
    tokens = dk_ref.shape[0]
    for which, (own, sink, out) in enumerate(((dk_ref, dsk_ref, kg_ref), (dv_ref, dsv_ref, vg_ref))):
        for block in range(tokens // BLK):
            rows = slice(block * BLK, (block + 1) * BLK)
            value = own[rows]
            late = block - (tokens // BLK - LEAD)
            if late >= 0:
                value = value + back_ref[which, late].astype(F32)
            if block < NGLOB:
                extra = sink[rows]
                for arrived in came[which::2]:
                    extra = extra + arrived[rows].astype(F32)
                value = value + jnp.where(root, extra, 0.0)
            out[rows] = value.astype(BF)


def finish(root, dk, dv, dsk, dsv, back, came):
    vmem = pl.BlockSpec(memory_space=pltpu.VMEM)
    return pl.pallas_call(
        finish_kernel,
        out_shape=[jax.ShapeDtypeStruct(dk.shape, BF)] * 2,
        in_specs=[pl.BlockSpec(memory_space=pltpu.SMEM)] + [vmem] * (5 + len(came)),
        out_specs=[vmem] * 2,
        compiler_params=pltpu.CompilerParams(vmem_limit_bytes=16 * 1024 * 1024),
        cost_estimate=pl.CostEstimate(flops=4 * dk.size, bytes_accessed=14 * dk.size, transcendentals=0),
        name="finish",
    )(root, dk, dv, dsk, dsv, back, *came)


def run_blocks(first, count, base, picks, queries, out_grad, window, incoming, glob, own, sinks, weights,
               before, acc):
    crossing = [d for d in range(WIN) if d > first]
    assert not crossing or count == 1
    tokens, columns = queries.shape
    heads = window.shape[2]
    slots = WIN + picks.shape[1]
    tile = (1, 1, heads, BLK, BLK)
    whole = lambda i, *_: (0, 0)
    args = [queries, out_grad]
    specs = [pl.BlockSpec((BLK, columns), lambda i, *_: (first + i, 0))] * 2
    for d in range(WIN):
        if d in crossing:
            args.append(incoming[d])
            specs.append(pl.BlockSpec(tile, lambda i, *_: (0, 0, 0, 0, 0)))
        else:
            args.append(window)
            specs.append(pl.BlockSpec(tile, lambda i, *_, d=d: (first + i - d, d, 0, 0, 0)))
    for g in range(slots - WIN):
        args.append(glob)
        specs.append(pl.BlockSpec(tile, lambda i, *_, g=g: (first + i, g, 0, 0, 0)))
    for x in (*own, *sinks):
        args.append(x)
        specs.append(pl.BlockSpec(x.shape, whole))
    args.append(weights)
    specs.append(pl.BlockSpec((1, 1, BLK), lambda i, *_: (first + i, 0, 0)))
    if crossing:
        args.append(before)
        specs.append(pl.BlockSpec(before.shape, lambda i, *_: (0, 0, 0, 0)))
    chained = acc is not None
    acc_shapes = [(tokens, E)] * 2 + [(NGLOB * BLK, E)] * 2
    if chained:
        args.extend(acc)
        specs.extend(pl.BlockSpec(s, whole) for s in acc_shapes)
    outs = [
        jax.ShapeDtypeStruct((count * BLK, columns), BF),
        jax.ShapeDtypeStruct((count, 1, BLK), F32),
    ] + [jax.ShapeDtypeStruct(s, F32) for s in acc_shapes]
    out_specs = [
        pl.BlockSpec((BLK, columns), lambda i, *_: (i, 0)),
        pl.BlockSpec((1, 1, BLK), lambda i, *_: (i, 0, 0)),
    ] + [pl.BlockSpec(s, whole) for s in acc_shapes]
    if crossing:
        back = (2, LEAD, BLK, E)
        outs.append(jax.ShapeDtypeStruct(back, F32))
        out_specs.append(pl.BlockSpec(back, lambda i, *_: (0, 0, 0, 0)))
    elements = count * slots * heads * BLK * BLK
    return pl.pallas_call(
        functools.partial(block_kernel, first, crossing, slots, chained),
        out_shape=outs,
        grid_spec=pltpu.PrefetchScalarGridSpec(
            num_scalar_prefetch=2,
            grid=(count,),
            in_specs=specs,
            out_specs=out_specs,
            scratch_shapes=[pltpu.VMEM((slots * BLK, heads * BLK), BF)] * 2
            + [pltpu.VMEM((2, slots * BLK, 2 * BLK), F32)] * 3,
        ),
        compiler_params=pltpu.CompilerParams(vmem_limit_bytes=(28 if crossing else 48) * 1024 * 1024),
        cost_estimate=pl.CostEstimate(
            flops=elements * E * 10, bytes_accessed=elements * 3, transcendentals=2 * elements
        ),
        name=f"blocks_from_{first}",
    )(base, picks, *args)


def local(queries, key_rows, values, out_grad, teacher_window, teacher_global, global_picks, mix_weight):
    tokens, columns = queries.shape
    blocks = tokens // BLK
    assert key_rows.shape[1] == E and blocks >= NGLOB
    where = lax.axis_index("seq")
    count = lax.axis_size("seq")
    base = (where * blocks).astype(jnp.int32).reshape(1)
    weights = mix_weight.reshape(blocks, 1, BLK)

    tail = slice(tokens - LEAD * BLK, tokens)
    first_rows = slice(0, NGLOB * BLK)
    pair = jnp.stack([key_rows, values])
    got = shift(pair, "seq", 1)
    before = got[:, tail].reshape(2, LEAD, BLK, E)
    sinks = jnp.where(where == 0, pair[:, first_rows], got[:, first_rows])
    span, known = 1, pair[:, first_rows]
    while span < count:
        for times in range(1, FAN):
            if span == 1 and times == 1:
                continue
            route = [(i, i + times * span) for i in range(span) if i + times * span < count]
            if route:
                more = lax.ppermute(known, "seq", route)
                sinks = jnp.where((where >= times * span) & (where < (times + 1) * span), more, sinks)
        span *= FAN
        known = sinks

    incoming = {}
    for block in range(LEAD - 1, -1, -1):
        offsets = list(range(block + 1, WIN))
        out = jnp.concatenate(
            [teacher_window[blocks + block - d:blocks + block - d + 1, d:d + 1] for d in offsets], axis=0
        )
        came = shift(out, "seq", 1)
        incoming[block] = {d: came[i:i + 1] for i, d in enumerate(offsets)}

    own = (key_rows, values)
    sink_arrays = (sinks[0], sinks[1])
    run = lambda first, n, acc: run_blocks(
        first, n, base, global_picks, queries, out_grad, teacher_window, incoming.get(first),
        teacher_global, own, sink_arrays, weights, before, acc,
    )
    dq, loss = {}, {}
    dq[LEAD], loss[LEAD], *acc = run(LEAD, blocks - LEAD, None)
    back = 0.0
    for block in range(LEAD - 1, -1, -1):
        dq[block], loss[block], *rest = run(block, 1, acc)
        acc, part = rest[:4], rest[4]
        back = back + part
    order = sorted(dq)
    query_grad = jnp.concatenate([dq[i] for i in order], axis=0)
    row_terms = jnp.concatenate([loss[i] for i in order], axis=0).reshape(tokens)

    dk, dv, dsk, dsv = acc
    sums = [dsk, dsv]
    steps = []
    reach = 1
    while reach < count:
        steps.append([(i, i - reach) for i in range(reach, count, 2 * reach)])
        reach *= 2
    returned = None
    early, late = distances("head")[:-1], distances("head")[-1:]
    row_terms = exchange_sum(exchange_sum(row_terms, "grp", distances("grp")), "head", early)
    arrived = []
    for number, route in enumerate(steps):
        low = [x.astype(BF) for x in sums]
        if number == 1:
            row_terms, low[0] = lax.optimization_barrier((row_terms, low[0]))
        came = [lax.ppermute(x, "seq", route) for x in low]
        if number == min(1, len(steps) - 1):
            leaving, low[1] = lax.optimization_barrier((back.astype(BF), low[1]))
            returned = shift(leaving, "seq", -1)
        sums = [x + y.astype(F32) for x, y in zip(sums, came)]
        arrived += came
    row_loss = exchange_sum(row_terms, "head", late)
    root = where.astype(jnp.int32).reshape(1)
    grads = finish(root, dk, dv, dsk, dsv, returned, arrived)
    return (query_grad, grads[0], grads[1], row_loss)


def solution(mesh):
    heads = ("grp", "head")
    placed = (
        P("seq", heads),
        P("seq", heads),
        P("seq", heads),
        P("seq", heads),
        P("seq", None, heads, None, None),
        P("seq", None, heads, None, None),
        P("seq", None),
        P("seq"),
    )
    return jax.shard_map(
        local,
        mesh=mesh,
        in_specs=placed,
        out_specs=(P("seq", heads), P("seq", heads), P("seq", heads), P("seq")),
        check_vma=False,
    )
```
